32 devices in a mesh: ctx: 16 (over z, y, core), head: 2 (over x).
Axes of the slice: x: 2, y: 2, z: 4, core: 2. Of those that a mesh axis runs over, the one named last changes fastest.
Arguments:
- queries: bfloat16 [16384, 8, 128], P('ctx', 'head'), may hold values from -6 to 6
- keys: bfloat16 [16384, 128], P('ctx'), may hold values from -6 to 6
- values: bfloat16 [16384, 128], P('ctx'), may hold values from -6 to 6
- outputs: bfloat16 [16384, 8, 128], P('ctx', 'head'), may hold values from -6 to 6
- out_grad: bfloat16 [16384, 8, 128], P('ctx', 'head'), may hold values from -16 to 16
- log_norm: float32 [8, 16384], P('head', 'ctx'), may hold values from 6 to 8
- span_ids: int32 [32], replicated, may hold values from 0 to 31, as said below
Outputs:
- query_grad: bfloat16 [16384, 8, 128], P('ctx', 'head')
- key_grad: bfloat16 [16384, 128], P(('ctx', 'head'))
- value_grad: bfloat16 [16384, 128], P(('ctx', 'head'))
The draws below stay inside these ranges and needn't reach their ends.
Inputs may be any that keep to these rules, and one draw needn't show every extreme that they name: `span_ids`: a permutation of 0 to 31 in which blocks 2 k and 2 k + 1 hold two spans that sum to 31.
All inputs are finite; a program needn't handle non-finite values.
Results may differ from the reference program's by a relative error of at most 0.0065.
Values may be sent and summed in bfloat16 or wider, within the bound.
No kernel may reach another device: no remote copies, remote signals or barrier semaphores. Data moves between devices by JAX's collectives and lax.ppermute only.
A program may use at most 128 MiB of HBM per device.

```python
import jax
import jax.numpy as jnp
from jax import lax

HEAD_DIM = 128
HEADS = 8
TOK_DEV = 1024
STEPS = 3
TOKENS = 16384
SPANS = 32
SPAN = 512


def draw_span_ids(key, part):
    key = jax.random.fold_in(key, 7)
    half = SPANS // 2
    order = jax.random.permutation(jax.random.fold_in(key, 1), half).astype(jnp.int32)
    flips = jax.random.randint(jax.random.fold_in(key, 2), (half,), 0, 2).astype(jnp.int32)
    lower = order
    upper = (SPANS - 1 - order).astype(jnp.int32)
    first = jnp.where(flips == 1, upper, lower)
    second = jnp.where(flips == 1, lower, upper)
    return jnp.stack([first, second], axis=1).reshape(-1).astype(jnp.int32)


def block_scale(own_key, shape, pieces, low, largest):
    factor_of = 1.0
    for position, shards_of in pieces:
        heights = jax.random.uniform(jax.random.fold_in(jax.random.fold_in(own_key, 6), position), (shards_of,), jnp.float32, low / len(pieces), largest / len(pieces))
        factor_of = factor_of * jnp.repeat(jnp.exp(heights), shape[position] // shards_of).reshape((-1,) + (1,) * (len(shape) - 1 - position))
    return factor_of


def scatter_about(rng, dims, deviation, reach, cuts=(), kind=jnp.bfloat16):
    gain = block_scale(rng, dims, cuts, -0.22, 0.18) if cuts else 1.0
    array = jax.random.normal(rng, dims, jnp.float32) * deviation * gain
    return jnp.minimum(jnp.maximum(array, -reach), reach).astype(kind)


def setup_inputs(seed: int = 0) -> dict:
    streams_of = jax.random.split(jax.random.key(seed), 8)
    queries = scatter_about(streams_of[0], (TOKENS, HEADS, HEAD_DIM), 1.0, 6.0, ((0, 16), (1, 2)))
    keys = scatter_about(streams_of[1], (TOKENS, HEAD_DIM), 1.0, 6.0, ((0, 16),))
    values = scatter_about(streams_of[2], (TOKENS, HEAD_DIM), 1.0, 6.0, ((0, 16),))
    outputs = scatter_about(streams_of[3], (TOKENS, HEADS, HEAD_DIM), 1.0, 6.0, ((0, 16), (1, 2)))
    out_grad = scatter_about(streams_of[4], (TOKENS, HEADS, HEAD_DIM), 4.0, 16.0, ((0, 16), (1, 2)))
    log_norm = jnp.clip(6.0 + 2.0 * jax.random.uniform(streams_of[5], (HEADS, TOKENS), jnp.float32) ** block_scale(streams_of[5], (HEADS, TOKENS), ((0, 2), (1, 16)), -0.2, 0.2), 6.0, 8.0)
    span_ids = draw_span_ids(jax.random.fold_in(streams_of[7], 71), 0)
    return {"queries": queries, "keys": keys, "values": values, "outputs": outputs, "out_grad": out_grad, "log_norm": log_norm, "span_ids": span_ids}


def reference(queries, keys, values, outputs, out_grad, log_norm, span_ids):
    scale = HEAD_DIM ** -0.5
    holders = SPANS // 2
    offsets = jnp.arange(SPAN, dtype=jnp.int32)
    places = (span_ids[:, None] * SPAN + offsets[None, :]).reshape(-1).astype(jnp.int32)
    delta = jnp.sum(out_grad.astype(jnp.float32) * outputs.astype(jnp.float32), axis=2)

    def one_holder(carry, holder):
        key_acc, value_acc = carry
        start = (holder * TOK_DEV).astype(jnp.int32)
        query_rows = lax.dynamic_slice_in_dim(queries, start, TOK_DEV, 0).astype(jnp.float32)
        grad_rows = lax.dynamic_slice_in_dim(out_grad, start, TOK_DEV, 0).astype(jnp.float32)
        norm_rows = lax.dynamic_slice_in_dim(log_norm, start, TOK_DEV, 1)
        delta_rows = lax.dynamic_slice_in_dim(delta, start, TOK_DEV, 0)
        query_places = lax.dynamic_slice_in_dim(places, start, TOK_DEV, 0)
        query_total = jnp.zeros((TOK_DEV, HEADS, HEAD_DIM), jnp.float32)
        for step in range(STEPS):
            source = ((holder - step) % holders).astype(jnp.int32)
            key_start = (source * TOK_DEV).astype(jnp.int32)
            key_rows = lax.dynamic_slice_in_dim(keys, key_start, TOK_DEV, 0).astype(jnp.float32)
            value_rows = lax.dynamic_slice_in_dim(values, key_start, TOK_DEV, 0).astype(jnp.float32)
            key_places = lax.dynamic_slice_in_dim(places, key_start, TOK_DEV, 0)
            allowed = key_places[None, :] <= query_places[:, None]
            scores = jnp.einsum('qhd,kd->hqk', query_rows, key_rows) * scale
            prob = jnp.where(allowed[None], jnp.exp(scores - norm_rows[:, :, None]), 0.0)
            prob16 = lax.optimization_barrier(prob.astype(jnp.bfloat16)).astype(jnp.float32)
            value_part = jnp.einsum('hqk,qhd->kd', prob16, grad_rows)
            dprob = jnp.einsum('qhd,kd->hqk', grad_rows, value_rows)
            dscore = lax.optimization_barrier((prob * (dprob - delta_rows.T[:, :, None])).astype(jnp.bfloat16)).astype(jnp.float32)
            query_total = query_total + scale * jnp.einsum('hqk,kd->qhd', dscore, key_rows)
            key_part = scale * jnp.einsum('hqk,qhd->kd', dscore, query_rows)
            old_key = lax.dynamic_slice_in_dim(key_acc, key_start, TOK_DEV, 0)
            key_acc = lax.dynamic_update_slice_in_dim(key_acc, old_key + key_part, key_start, 0)
            old_value = lax.dynamic_slice_in_dim(value_acc, key_start, TOK_DEV, 0)
            value_acc = lax.dynamic_update_slice_in_dim(value_acc, old_value + value_part, key_start, 0)
        return (key_acc, value_acc), query_total.astype(jnp.bfloat16)

    zeros = jnp.zeros((TOKENS, HEAD_DIM), jnp.float32)
    (key_acc, value_acc), query_parts = lax.scan(one_holder, (zeros, zeros), jnp.arange(holders, dtype=jnp.int32))
    query_grad = query_parts.reshape(TOKENS, HEADS, HEAD_DIM)
    return query_grad, key_acc.astype(jnp.bfloat16), value_acc.astype(jnp.bfloat16)
```

```python
import functools
import math

import jax
import jax.numpy as jnp
from jax import lax
from jax.experimental import pallas as pl
from jax.experimental.pallas import tpu as pltpu
from jax.sharding import PartitionSpec as P

STEPS = 3
NT = (((1,), (1,)), ((), ()))
NN = (((1,), (0,)), ((), ()))
TN = (((0,), (0,)), ((), ()))


def dot(a, b, dims):
    return lax.dot_general(a, b, dims, preferred_element_type=jnp.float32)


def three_terms(x):
    high = x.astype(jnp.bfloat16)
    rest = x - high.astype(jnp.float32)
    mid = rest.astype(jnp.bfloat16)
    low = (rest - mid.astype(jnp.float32)).astype(jnp.bfloat16)
    return high, mid, low


def row_terms(heads, tile, refs, out, norm_ref):
    grad_ref, outputs_ref = refs
    rows = grad_ref.shape[0]
    toks = tile // heads
    spread = (
        lax.broadcasted_iota(jnp.int32, (toks, tile), 1) // heads
        == lax.broadcasted_iota(jnp.int32, (toks, tile), 0)
    ).astype(jnp.bfloat16)
    mine = (
        lax.broadcasted_iota(jnp.int32, (heads, tile), 1) % heads
        == lax.broadcasted_iota(jnp.int32, (heads, tile), 0)
    )
    ones = jnp.ones((8, grad_ref.shape[1]), jnp.bfloat16)
    for index in range(rows // tile):
        norm = norm_ref[:, pl.ds(index * toks, toks)] * math.log2(math.e)
        wide = sum(dot(part, spread, NN) for part in three_terms(norm))
        out[0:1, pl.ds(index * tile, tile)] = jnp.sum(
            jnp.where(mine, wide, 0.0), axis=0, keepdims=True
        )
        prod = grad_ref[pl.ds(index * tile, tile), :].astype(jnp.float32) * outputs_ref[
            pl.ds(index * tile, tile), :
        ].astype(jnp.float32)
        high = prod.astype(jnp.bfloat16)
        low = (prod - high.astype(jnp.float32)).astype(jnp.bfloat16)
        out[1:2, pl.ds(index * tile, tile)] = (dot(ones, high, NT) + dot(ones, low, NT))[0:1]


def tile_grads(
    refs, accs, row, key, length, scale, triangle=None
):
    query_ref, grad_ref, key_ref, value_ref, terms_ref, tile = refs
    query_acc, key_acc, value_acc = accs
    q = query_ref[pl.ds(row, tile), :]
    g = grad_ref[pl.ds(row, tile), :]
    k = key_ref[pl.ds(key, length), :]
    v = value_ref[pl.ds(key, length), :]
    norm = terms_ref[0:1, pl.ds(row, tile)]
    delta = terms_ref[1:2, pl.ds(row, tile)]
    scores = dot(k, q, NT)
    prob = jnp.exp2(scores * (scale * math.log2(math.e)) - norm)
    if triangle is not None:
        edge = length - triangle.shape[0]
        last = jnp.where(triangle, prob[edge:], 0.0)
        prob = last if edge == 0 else jnp.concatenate([prob[:edge], last], axis=0)
    value_acc[pl.ds(key, length), :] += dot(prob.astype(jnp.bfloat16), g, NN)
    dprob = dot(v, g, NT)
    dscore = (prob * (dprob - delta)).astype(jnp.bfloat16)
    key_acc[pl.ds(key, length), :] += dot(dscore, q, NN)
    query_acc[pl.ds(row, tile), :] += dot(dscore, k, TN)


def own_kernel(heads, tile, scale, parts, places, *refs):
    query_ref, grad_ref, outputs_ref, norm_ref, key_ref, value_ref = refs[:6]
    query_acc, terms_ref, mine_ref = refs[6:9]
    sent = refs[9 : 8 + parts]
    key_acc, value_acc = refs[8 + parts :]
    half = key_ref.shape[0] // 2
    toks = tile // heads
    query_acc[...] = jnp.zeros_like(query_acc)
    key_acc[...] = jnp.zeros_like(key_acc)
    value_acc[...] = jnp.zeros_like(value_acc)
    row_terms(heads, tile, (grad_ref, outputs_ref), terms_ref, norm_ref)
    low = places[0]
    group = (query_ref, grad_ref, key_ref, value_ref, terms_ref, tile)
    accs = (query_acc, key_acc, value_acc)
    triangle = lax.broadcasted_iota(jnp.int32, (toks, tile), 0) <= (
        lax.broadcasted_iota(jnp.int32, (toks, tile), 1) // heads
    )

    @pl.loop(0, 2)
    def _(index):
        key = pl.multiple_of(index * half, half)
        for part in range(half // toks):
            row = pl.multiple_of(index * half * heads + part * tile, tile)
            tile_grads(group, accs, row, key, (part + 1) * toks, scale, triangle)

    @pl.loop(0, half // toks)
    def _(part):
        row = pl.multiple_of((1 - low) * half * heads + part * tile, tile)
        tile_grads(group, accs, row, pl.multiple_of(low * half, half), half, scale)

    share = key_ref.shape[0] // parts
    for away in range(parts):
        start = pl.multiple_of(lax.rem(places[1] + away, parts) * share, share)
        out = mine_ref if away == 0 else sent[away - 1]
        out[0:share, :] = (key_acc[pl.ds(start, share), :] * scale).astype(out.dtype)
        out[share : 2 * share, :] = value_acc[pl.ds(start, share), :].astype(out.dtype)


def far_kernel(heads, tile, scale, parts, last, places, *refs):
    query_ref, grad_ref, key_ref, value_ref, terms_ref, before_ref = refs[:6]
    query_out = refs[6]
    sent = refs[7 : 7 + parts]
    key_acc, value_acc = refs[7 + parts : 9 + parts]
    query_acc = refs[9 + parts] if last else query_out
    half = key_ref.shape[0] // 2
    key_acc[...] = jnp.zeros_like(key_acc)
    value_acc[...] = jnp.zeros_like(value_acc)
    query_acc[...] = before_ref[...]
    group = (query_ref, grad_ref, key_ref, value_ref, terms_ref, tile)
    accs = (query_acc, key_acc, value_acc)
    per = half * heads // tile

    @pl.loop(0, 2 * per)
    def _(index):
        item = index // per
        row_half = jnp.where(places[2] == 1, places[0], item)
        key_half = jnp.where(places[2] == 1, item, places[0])
        row = pl.multiple_of(row_half * half * heads + lax.rem(index, per) * tile, tile)
        tile_grads(group, accs, row, pl.multiple_of(key_half * half, half), half, scale)

    share = key_ref.shape[0] // parts
    for away in range(parts):
        start = pl.multiple_of(lax.rem(places[1] + away, parts) * share, share)
        out = sent[away]
        out[0:share, :] = (key_acc[pl.ds(start, share), :] * scale).astype(out.dtype)
        out[share : 2 * share, :] = value_acc[pl.ds(start, share), :].astype(out.dtype)
    if last:
        query_out[...] = (query_acc[...] * scale).astype(query_out.dtype)


VMEM = pl.BlockSpec(memory_space=pltpu.VMEM)
SMEM = pl.BlockSpec(memory_space=pltpu.SMEM)
PARAMS = pltpu.CompilerParams(vmem_limit_bytes=32 * 1024 * 1024)


def call(kernel, ins, outs, scratch, blocks, name):
    flops = blocks * 10 * 512 * 512 * 128
    return pl.pallas_call(
        kernel,
        out_shape=outs,
        in_specs=[SMEM] + [VMEM] * (len(ins) - 1),
        out_specs=[VMEM] * len(outs),
        scratch_shapes=scratch,
        compiler_params=PARAMS,
        name=name,
        cost_estimate=pl.CostEstimate(flops=int(flops), bytes_accessed=6 << 20, transcendentals=0),
    )(*ins)


def moved(block, back, away):
    holders, parts = lax.axis_size("ctx"), lax.axis_size("head")
    route = [
        (h * parts + x, ((h - back) % holders) * parts + (x + away) % parts)
        for h in range(holders)
        for x in range(parts)
    ]
    return lax.ppermute(block, ("ctx", "head"), route)


def local(queries, keys, values, outputs, out_grad, log_norm, span_ids):
    toks, heads, dim = queries.shape
    rows = toks * heads
    scale = dim ** (-0.5)
    holders, parts = lax.axis_size("ctx"), lax.axis_size("head")
    me, x = lax.axis_index("ctx"), lax.axis_index("head")
    tile = 512
    q = queries.reshape(rows, dim)
    g = out_grad.reshape(rows, dim)
    o = outputs.reshape(rows, dim)
    share = 2 * toks // parts
    f32, bf16 = jnp.float32, jnp.bfloat16

    def pair(holder):
        return lax.dynamic_slice_in_dim(span_ids, holder * 2, 2, 0)

    mine = pair(me)
    low = (mine[0] > mine[1]).astype(jnp.int32)

    def far_places(step):
        theirs = pair((me - step) % holders)
        high_only = jnp.min(mine) < jnp.min(theirs)
        their_low = (theirs[0] > theirs[1]).astype(jnp.int32)
        return jnp.stack(
            [jnp.where(high_only, 1 - low, their_low), x, high_only.astype(jnp.int32)]
        ).astype(jnp.int32)

    accs = [pltpu.VMEM((toks, dim), f32)] * 2
    key_1, value_1 = moved(keys, -1, 0), moved(values, -1, 0)
    key_2, value_2 = moved(key_1, -1, 0), moved(value_1, -1, 0)

    query_sum, terms, total, *sent = call(
        functools.partial(own_kernel, heads, tile, scale, parts),
        (jnp.stack([low, x]).astype(jnp.int32), q, g, o, log_norm, keys, values),
        [
            jax.ShapeDtypeStruct((rows, dim), f32),
            jax.ShapeDtypeStruct((8, rows), f32),
            jax.ShapeDtypeStruct((share, dim), f32),
        ]
        + [jax.ShapeDtypeStruct((share, dim), bf16)] * (parts - 1),
        accs,
        3 * heads,
        "own",
    )
    landed = [moved(block, 0, away + 1) for away, block in enumerate(sent)]
    for step, (key, value) in ((1, (key_1, value_1)), (2, (key_2, value_2))):
        last = step == STEPS - 1
        query_sum, *sent = call(
            functools.partial(far_kernel, heads, tile, scale, parts, last),
            (far_places(step), q, g, key, value, terms, query_sum),
            [jax.ShapeDtypeStruct((rows, dim), bf16 if last else f32)]
            + [jax.ShapeDtypeStruct((share, dim), bf16)] * parts,
            accs + ([pltpu.VMEM((rows, dim), f32)] if last else []),
            2 * heads,
            "far",
        )
        landed += [moved(block, step, away) for away, block in enumerate(sent)]
    for block in landed:
        total = total + block.astype(f32)
    total = total.astype(bf16)
    return query_sum.reshape(toks, heads, dim), total[: share // 2], total[share // 2 :]


def solution(mesh):
    in_specs = (
        P("ctx", "head", None),
        P("ctx", None),
        P("ctx", None),
        P("ctx", "head", None),
        P("ctx", "head", None),
        P("head", "ctx"),
        P(),
    )
    out_specs = (P("ctx", "head", None), P(("ctx", "head"), None), P(("ctx", "head"), None))
    return jax.shard_map(local, mesh=mesh, in_specs=in_specs, out_specs=out_specs, check_vma=False)
```

```python
import functools
import math

import jax
import jax.numpy as jnp
from jax import lax
from jax.experimental import pallas as pl
from jax.experimental.pallas import tpu as pltpu
from jax.sharding import PartitionSpec as P

STEPS = 3
NT = (((1,), (1,)), ((), ()))
NN = (((1,), (0,)), ((), ()))
TN = (((0,), (0,)), ((), ()))


def dot(a, b, dims):
    return lax.dot_general(a, b, dims, preferred_element_type=jnp.float32)


def three_terms(x):
    high = x.astype(jnp.bfloat16)
    rest = x - high.astype(jnp.float32)
    mid = rest.astype(jnp.bfloat16)
    low = (rest - mid.astype(jnp.float32)).astype(jnp.bfloat16)
    return high, mid, low


def row_terms(heads, tile, span, refs, out):
    grad_ref, outputs_ref, norm_ref = refs
    rows = grad_ref.shape[0] // 2
    toks = tile // heads
    spread = (
        lax.broadcasted_iota(jnp.int32, (toks, tile), 1) // heads
        == lax.broadcasted_iota(jnp.int32, (toks, tile), 0)
    ).astype(jnp.bfloat16)
    mine = (
        lax.broadcasted_iota(jnp.int32, (heads, tile), 1) % heads
        == lax.broadcasted_iota(jnp.int32, (heads, tile), 0)
    )
    ones = jnp.ones((8, grad_ref.shape[1]), jnp.bfloat16)
    for index in range(rows // tile):
        tok = pl.multiple_of(span * (rows // heads) + index * toks, toks)
        row = pl.multiple_of(span * rows + index * tile, tile)
        norm = norm_ref[:, pl.ds(tok, toks)] * math.log2(math.e)
        wide = sum(dot(part, spread, NN) for part in three_terms(norm))
        out[0:1, pl.ds(row, tile)] = jnp.sum(jnp.where(mine, wide, 0.0), axis=0, keepdims=True)
        prod = grad_ref[pl.ds(row, tile), :].astype(jnp.float32) * outputs_ref[
            pl.ds(row, tile), :
        ].astype(jnp.float32)
        high = prod.astype(jnp.bfloat16)
        low = (prod - high.astype(jnp.float32)).astype(jnp.bfloat16)
        out[1:2, pl.ds(row, tile)] = (dot(ones, high, NT) + dot(ones, low, NT))[0:1]


def tile_grads(
    refs, accs, row, key, length, scale, triangle=None
):
    query_ref, grad_ref, key_ref, value_ref, terms_ref, tile = refs
    query_acc, key_acc, value_acc = accs
    q = query_ref[pl.ds(row, tile), :]
    g = grad_ref[pl.ds(row, tile), :]
    k = key_ref[pl.ds(key, length), :]
    v = value_ref[pl.ds(key, length), :]
    norm = terms_ref[0:1, pl.ds(row, tile)]
    delta = terms_ref[1:2, pl.ds(row, tile)]
    scores = dot(k, q, NT)
    prob = jnp.exp2(scores * (scale * math.log2(math.e)) - norm)
    if triangle is not None:
        edge = length - triangle.shape[0]
        last = jnp.where(triangle, prob[edge:], 0.0)
        prob = last if edge == 0 else jnp.concatenate([prob[:edge], last], axis=0)
    value_acc[pl.ds(key, length), :] += dot(prob.astype(jnp.bfloat16), g, NN)
    dprob = dot(v, g, NT)
    dscore = (prob * (dprob - delta)).astype(jnp.bfloat16)
    key_acc[pl.ds(key, length), :] += dot(dscore, q, NN)
    query_acc[pl.ds(row, tile), :] += dot(dscore, k, TN)


def span_pair(span_ids, holder):
    return span_ids[2 * holder], span_ids[2 * holder + 1]


def put_shares(outs, key_acc, value_acc, scale):
    parts = len(outs)
    share = key_acc.shape[0] // parts
    x = lax.axis_index("head")
    for away, out in enumerate(outs):
        start = pl.multiple_of(lax.rem(x + away, parts) * share, share)
        out[0:share, :] = (key_acc[pl.ds(start, share), :] * scale).astype(out.dtype)
        out[share : 2 * share, :] = value_acc[pl.ds(start, share), :].astype(out.dtype)


def own_kernel(heads, tile, scale, parts, *refs):
    inputs, refs = refs[:7], refs[7:]
    query_acc, terms_ref, both_ref = refs[:3]
    outs, refs = refs[3 : 3 + parts], refs[3 + parts :]
    held, (key_acc, value_acc, sems) = refs[:5], refs[5:]
    query_ref, grad_ref, outputs_ref, norm_ref, span_ids = held
    toks = both_ref.shape[0] // 2
    key_ref, value_ref = both_ref.at[pl.ds(0, toks)], both_ref.at[pl.ds(toks, toks)]
    half = toks // 2
    rows = half * heads
    per = tile // heads
    whole = [
        pltpu.make_async_copy(a, b, sems.at[i, 2])
        for i, (a, b) in enumerate(zip(inputs[3:], (norm_ref, key_ref, value_ref, span_ids)))
    ]

    def halves(index):
        part = pl.ds(pl.multiple_of(index * rows, rows), rows)
        return [
            pltpu.make_async_copy(inputs[i].at[part], held[i].at[part], sems.at[i, index])
            for i in (1, 2, 0)
        ]

    for copy in whole + halves(0) + halves(1):
        copy.start()
    query_acc[...] = jnp.zeros_like(query_acc)
    key_acc[...] = jnp.zeros_like(key_acc)
    value_acc[...] = jnp.zeros_like(value_acc)
    group = (query_ref, grad_ref, key_ref, value_ref, terms_ref, tile)
    accs = (query_acc, key_acc, value_acc)
    triangle = lax.broadcasted_iota(jnp.int32, (per, tile), 0) <= (
        lax.broadcasted_iota(jnp.int32, (per, tile), 1) // heads
    )
    for copy in whole:
        copy.wait()

    @pl.loop(0, 2)
    def _(index):
        for copy in halves(index):
            copy.wait()
        row_terms(heads, tile, index, (grad_ref, outputs_ref, norm_ref), terms_ref)
        key = pl.multiple_of(index * half, half)
        for part in range(half // per):
            row = pl.multiple_of(index * rows + part * tile, tile)
            tile_grads(group, accs, row, key, (part + 1) * per, scale, triangle)

    first, second = span_pair(span_ids, lax.axis_index("ctx"))
    low = jnp.where(first > second, 1, 0)

    @pl.loop(0, rows // tile)
    def _(part):
        row = pl.multiple_of((1 - low) * rows + part * tile, tile)
        tile_grads(group, accs, row, pl.multiple_of(low * half, half), half, scale)

    put_shares(outs, key_acc, value_acc, scale)


def far_kernel(heads, tile, scale, parts, step, count, span_ids, *refs):
    query_ref, grad_ref, terms_ref = refs[:3]
    if count == 1:
        toks = refs[3].shape[0] // 2
        key_ref, value_ref = refs[3].at[pl.ds(0, toks)], refs[3].at[pl.ds(toks, toks)]
    else:
        key_ref, value_ref = refs[3:5]
    query_acc = refs[4 + count]
    outs = refs[5 + count : 5 + count + parts]
    key_acc, value_acc = refs[5 + count + parts :]
    half = key_ref.shape[0] // 2
    key_acc[...] = jnp.zeros_like(key_acc)
    value_acc[...] = jnp.zeros_like(value_acc)
    group = (query_ref, grad_ref, key_ref, value_ref, terms_ref, tile)
    accs = (query_acc, key_acc, value_acc)
    per = half * heads // tile
    me, holders = lax.axis_index("ctx"), lax.axis_size("ctx")
    mine = span_pair(span_ids, me)
    theirs = span_pair(span_ids, lax.rem(me + holders - step, holders))
    high_only = jnp.minimum(*mine) < jnp.minimum(*theirs)
    our_high = jnp.where(mine[0] > mine[1], 0, 1)
    their_low = jnp.where(theirs[0] > theirs[1], 1, 0)

    @pl.loop(0, 2 * per)
    def _(index):
        item = index // per
        row_half = jnp.where(high_only, our_high, item)
        key_half = jnp.where(high_only, item, their_low)
        row = pl.multiple_of(row_half * half * heads + lax.rem(index, per) * tile, tile)
        tile_grads(group, accs, row, pl.multiple_of(key_half * half, half), half, scale)

    put_shares(outs, key_acc, value_acc, scale)


VMEM = pl.BlockSpec(memory_space=pltpu.VMEM)
SMEM = pl.BlockSpec(memory_space=pltpu.SMEM)
HBM = pl.BlockSpec(memory_space=pltpu.HBM)
PARAMS = pltpu.CompilerParams(vmem_limit_bytes=20 * 1024 * 1024)


def call(kernel, ins, where, outs, scratch, blocks, name, aliases=None):
    flops = blocks * 40 * 512 * 512 * 128
    return pl.pallas_call(
        kernel,
        out_shape=outs,
        in_specs=where,
        out_specs=[VMEM] * len(outs),
        scratch_shapes=scratch,
        input_output_aliases=aliases or {},
        compiler_params=PARAMS,
        name=name,
        cost_estimate=pl.CostEstimate(flops=int(flops), bytes_accessed=6 << 20, transcendentals=0),
    )(*ins)


def moved(block, back, away):
    holders, parts = lax.axis_size("ctx"), lax.axis_size("head")
    route = [
        (h * parts + x, ((h - back) % holders) * parts + (x + away) % parts)
        for h in range(holders)
        for x in range(parts)
    ]
    return lax.ppermute(block, ("ctx", "head"), route)


def local(queries, keys, values, outputs, out_grad, log_norm, span_ids):
    toks, heads, dim = queries.shape
    rows = toks * heads
    scale = dim ** (-0.5)
    parts = lax.axis_size("head")
    tile = 512
    q = queries.reshape(rows, dim)
    g = out_grad.reshape(rows, dim)
    o = outputs.reshape(rows, dim)
    share = 2 * toks // parts
    f32, bf16 = jnp.float32, jnp.bfloat16
    shape = jax.ShapeDtypeStruct

    accs = [pltpu.VMEM((toks, dim), f32)] * 2
    far = moved(keys, 1 - STEPS, 0), moved(values, 1 - STEPS, 0)

    inputs = tuple(
        pltpu.with_memory_space_constraint(a, pltpu.HBM)
        for a in (q, g, o, log_norm, keys, values, span_ids)
    )
    query_sum, terms, both, total, *sent = call(
        functools.partial(own_kernel, heads, tile, scale, parts),
        inputs,
        [HBM] * len(inputs),
        [shape((rows, dim), f32), shape((8, rows), f32), shape((2 * toks, dim), bf16)]
        + [shape((share, dim), f32)]
        + [shape((share, dim), bf16)] * (parts - 1),
        [pltpu.VMEM(a.shape, a.dtype) for a in inputs[:4]]
        + [pltpu.SMEM(span_ids.shape, span_ids.dtype)]
        + accs
        + [pltpu.SemaphoreType.DMA((4, 3))],
        3 * heads,
        "own",
    )
    near = (moved(both, -1, 0),)
    landed = [moved(block, 0, away + 1) for away, block in enumerate(sent)]
    for step, held in ((2, far), (1, near)):
        query_sum, *sent = call(
            functools.partial(far_kernel, heads, tile, scale, parts, step, len(held)),
            (span_ids, q, g, terms, *held, query_sum),
            [SMEM] + [VMEM] * (4 + len(held)),
            [shape((rows, dim), f32)] + [shape((share, dim), bf16)] * parts,
            accs,
            2 * heads,
            "far",
            {4 + len(held): 0},
        )
        landed += [moved(block, step, away) for away, block in enumerate(sent)]
    for block in landed:
        total = total + block.astype(f32)
    total = total.astype(bf16)
    query_grad = (query_sum * scale).astype(bf16).reshape(toks, heads, dim)
    return query_grad, total[: share // 2], total[share // 2 :]


def solution(mesh):
    in_specs = (
        P("ctx", "head", None),
        P("ctx", None),
        P("ctx", None),
        P("ctx", "head", None),
        P("ctx", "head", None),
        P("head", "ctx"),
        P(),
    )
    out_specs = (P("ctx", "head", None), P(("ctx", "head"), None), P(("ctx", "head"), None))
    return jax.shard_map(local, mesh=mesh, in_specs=in_specs, out_specs=out_specs, check_vma=False)
```

```python
import functools
import math

import jax
import jax.numpy as jnp
from jax import lax
from jax.experimental import pallas as pl
from jax.experimental.pallas import tpu as pltpu
from jax.sharding import PartitionSpec as P

STEPS = 3
NT = (((1,), (1,)), ((), ()))
NN = (((1,), (0,)), ((), ()))
TN = (((0,), (0,)), ((), ()))


def dot(a, b, dims):
    return lax.dot_general(a, b, dims, preferred_element_type=jnp.float32)


def three_terms(x):
    high = x.astype(jnp.bfloat16)
    rest = x - high.astype(jnp.float32)
    mid = rest.astype(jnp.bfloat16)
    low = (rest - mid.astype(jnp.float32)).astype(jnp.bfloat16)
    return high, mid, low


def row_terms(heads, tile, span, refs, out):
    grad_ref, outputs_ref, norm_ref = refs
    rows = grad_ref.shape[0] // 2
    toks = tile // heads
    spread = (
        lax.broadcasted_iota(jnp.int32, (toks, tile), 1) // heads
        == lax.broadcasted_iota(jnp.int32, (toks, tile), 0)
    ).astype(jnp.bfloat16)
    mine = (
        lax.broadcasted_iota(jnp.int32, (heads, tile), 1) % heads
        == lax.broadcasted_iota(jnp.int32, (heads, tile), 0)
    )
    ones = jnp.ones((8, grad_ref.shape[1]), jnp.bfloat16)
    for index in range(rows // tile):
        tok = pl.multiple_of(span * (rows // heads) + index * toks, toks)
        row = pl.multiple_of(span * rows + index * tile, tile)
        norm = norm_ref[:, pl.ds(tok, toks)] * math.log2(math.e)
        wide = sum(dot(part, spread, NN) for part in three_terms(norm))
        out[0:1, pl.ds(row, tile)] = jnp.sum(jnp.where(mine, wide, 0.0), axis=0, keepdims=True)
        prod = grad_ref[pl.ds(row, tile), :].astype(jnp.float32) * outputs_ref[
            pl.ds(row, tile), :
        ].astype(jnp.float32)
        high = prod.astype(jnp.bfloat16)
        low = (prod - high.astype(jnp.float32)).astype(jnp.bfloat16)
        out[1:2, pl.ds(row, tile)] = (dot(ones, high, NT) + dot(ones, low, NT))[0:1]


def tile_grads(group, accs, scale, tiles):
    query_ref, grad_ref, key_ref, value_ref, terms_ref, tile = group
    query_acc, key_acc, value_acc = accs

    def opened(row, key, length, _):
        k = key_ref[pl.ds(key, length), :]
        v = value_ref[pl.ds(key, length), :]
        scores = dot(k, query_ref[pl.ds(row, tile), :], NT)
        return scores, dot(v, grad_ref[pl.ds(row, tile), :], NT)

    def closed(row, key, length, triangle, scores, dprob):
        norm = terms_ref[0:1, pl.ds(row, tile)]
        delta = terms_ref[1:2, pl.ds(row, tile)]
        prob = jnp.exp2(scores * (scale * math.log2(math.e)) - norm)
        if triangle is not None:
            edge = length - triangle.shape[0]
            last = jnp.where(triangle, prob[edge:], 0.0)
            prob = last if edge == 0 else jnp.concatenate([prob[:edge], last], axis=0)
        dscore = (prob * (dprob - delta)).astype(jnp.bfloat16)
        value_acc[pl.ds(key, length), :] += dot(
            prob.astype(jnp.bfloat16), grad_ref[pl.ds(row, tile), :], NN
        )
        key_acc[pl.ds(key, length), :] += dot(dscore, query_ref[pl.ds(row, tile), :], NN)
        query_acc[pl.ds(row, tile), :] += dot(dscore, key_ref[pl.ds(key, length), :], TN)

    ahead = opened(*tiles[0])
    for index, this in enumerate(tiles):
        now = ahead
        if index + 1 < len(tiles):
            ahead = opened(*tiles[index + 1])
        closed(*this, *now)


def span_pair(span_ids, holder):
    return span_ids[2 * holder], span_ids[2 * holder + 1]


def put_shares(outs, key_acc, value_acc, scale):
    parts = len(outs)
    share = key_acc.shape[0] // parts
    x = lax.axis_index("head")
    for away, out in enumerate(outs):
        start = pl.multiple_of(lax.rem(x + away, parts) * share, share)
        out[0:share, :] = (key_acc[pl.ds(start, share), :] * scale).astype(out.dtype)
        out[share : 2 * share, :] = value_acc[pl.ds(start, share), :].astype(out.dtype)


def own_kernel(heads, tile, scale, parts, *refs):
    inputs, refs = refs[:7], refs[7:]
    query_acc, terms_ref, both_ref = refs[:3]
    outs, refs = refs[3 : 3 + parts], refs[3 + parts :]
    held, (key_acc, value_acc, sems) = refs[:5], refs[5:]
    query_ref, grad_ref, outputs_ref, norm_ref, span_ids = held
    toks = both_ref.shape[0] // 2
    key_ref, value_ref = both_ref.at[pl.ds(0, toks)], both_ref.at[pl.ds(toks, toks)]
    half = toks // 2
    rows = half * heads
    per = tile // heads
    whole = [
        pltpu.make_async_copy(a, b, sems.at[i, 2])
        for i, (a, b) in enumerate(zip(inputs[3:], (norm_ref, key_ref, value_ref, span_ids)))
    ]

    def halves(index):
        part = pl.ds(pl.multiple_of(index * rows, rows), rows)
        return [
            pltpu.make_async_copy(inputs[i].at[part], held[i].at[part], sems.at[i, index])
            for i in (1, 2, 0)
        ]

    for copy in whole + halves(0) + halves(1):
        copy.start()
    query_acc[...] = jnp.zeros_like(query_acc)
    key_acc[...] = jnp.zeros_like(key_acc)
    value_acc[...] = jnp.zeros_like(value_acc)
    group = (query_ref, grad_ref, key_ref, value_ref, terms_ref, tile)
    accs = (query_acc, key_acc, value_acc)
    triangle = lax.broadcasted_iota(jnp.int32, (per, tile), 0) <= (
        lax.broadcasted_iota(jnp.int32, (per, tile), 1) // heads
    )
    for copy in whole:
        copy.wait()

    @pl.loop(0, 2)
    def _(index):
        for copy in halves(index):
            copy.wait()
        row_terms(heads, tile, index, (grad_ref, outputs_ref, norm_ref), terms_ref)
        key = pl.multiple_of(index * half, half)
        tiles = [
            (pl.multiple_of(index * rows + part * tile, tile), key, (part + 1) * per, triangle)
            for part in range(half // per)
        ]
        tile_grads(group, accs, scale, tiles)

    first, second = span_pair(span_ids, lax.axis_index("ctx"))
    low = jnp.where(first > second, 1, 0)

    key = pl.multiple_of(low * half, half)
    tiles = [
        (pl.multiple_of((1 - low) * rows + part * tile, tile), key, half, None)
        for part in range(rows // tile)
    ]
    tile_grads(group, accs, scale, tiles)
    put_shares(outs, key_acc, value_acc, scale)


def far_kernel(heads, tile, scale, parts, step, count, span_ids, *refs):
    query_ref, grad_ref, terms_ref = refs[:3]
    if count == 1:
        toks = refs[3].shape[0] // 2
        key_ref, value_ref = refs[3].at[pl.ds(0, toks)], refs[3].at[pl.ds(toks, toks)]
    else:
        key_ref, value_ref = refs[3:5]
    query_acc = refs[4 + count]
    outs = refs[5 + count : 5 + count + parts]
    key_acc, value_acc = refs[5 + count + parts :]
    half = key_ref.shape[0] // 2
    key_acc[...] = jnp.zeros_like(key_acc)
    value_acc[...] = jnp.zeros_like(value_acc)
    group = (query_ref, grad_ref, key_ref, value_ref, terms_ref, tile)
    accs = (query_acc, key_acc, value_acc)
    per = half * heads // tile
    me, holders = lax.axis_index("ctx"), lax.axis_size("ctx")
    mine = span_pair(span_ids, me)
    theirs = span_pair(span_ids, lax.rem(me + holders - step, holders))
    high_only = jnp.minimum(*mine) < jnp.minimum(*theirs)
    our_high = jnp.where(mine[0] > mine[1], 0, 1)
    their_low = jnp.where(theirs[0] > theirs[1], 1, 0)

    @pl.loop(0, 2)
    def _(item):
        row_half = jnp.where(high_only, our_high, item)
        key_half = jnp.where(high_only, item, their_low)
        row = pl.multiple_of(row_half * half * heads, half * heads)
        key = pl.multiple_of(key_half * half, half)
        tiles = [(pl.multiple_of(row + part * tile, tile), key, half, None) for part in range(per)]
        tile_grads(group, accs, scale, tiles)

    put_shares(outs, key_acc, value_acc, scale)


VMEM = pl.BlockSpec(memory_space=pltpu.VMEM)
SMEM = pl.BlockSpec(memory_space=pltpu.SMEM)
HBM = pl.BlockSpec(memory_space=pltpu.HBM)
PARAMS = pltpu.CompilerParams(vmem_limit_bytes=20 * 1024 * 1024)


def call(kernel, ins, where, outs, scratch, blocks, name, aliases=None):
    flops = blocks * 40 * 512 * 512 * 128
    return pl.pallas_call(
        kernel,
        out_shape=outs,
        in_specs=where,
        out_specs=[VMEM] * len(outs),
        scratch_shapes=scratch,
        input_output_aliases=aliases or {},
        compiler_params=PARAMS,
        name=name,
        cost_estimate=pl.CostEstimate(flops=int(flops), bytes_accessed=6 << 20, transcendentals=0),
    )(*ins)


def moved(block, back, away):
    holders, parts = lax.axis_size("ctx"), lax.axis_size("head")
    route = [
        (h * parts + x, ((h - back) % holders) * parts + (x + away) % parts)
        for h in range(holders)
        for x in range(parts)
    ]
    return lax.ppermute(block, ("ctx", "head"), route)


def local(queries, keys, values, outputs, out_grad, log_norm, span_ids):
    toks, heads, dim = queries.shape
    rows = toks * heads
    scale = dim ** (-0.5)
    parts = lax.axis_size("head")
    tile = 512
    q = queries.reshape(rows, dim)
    g = out_grad.reshape(rows, dim)
    o = outputs.reshape(rows, dim)
    share = 2 * toks // parts
    f32, bf16 = jnp.float32, jnp.bfloat16
    shape = jax.ShapeDtypeStruct

    accs = [pltpu.VMEM((toks, dim), f32)] * 2
    far = moved(keys, 1 - STEPS, 0), moved(values, 1 - STEPS, 0)

    inputs = tuple(
        pltpu.with_memory_space_constraint(a, pltpu.HBM)
        for a in (q, g, o, log_norm, keys, values, span_ids)
    )
    query_sum, terms, both, total, *sent = call(
        functools.partial(own_kernel, heads, tile, scale, parts),
        inputs,
        [HBM] * len(inputs),
        [shape((rows, dim), f32), shape((8, rows), f32), shape((2 * toks, dim), bf16)]
        + [shape((share, dim), f32)]
        + [shape((share, dim), bf16)] * (parts - 1),
        [pltpu.VMEM(a.shape, a.dtype) for a in inputs[:4]]
        + [pltpu.SMEM(span_ids.shape, span_ids.dtype)]
        + accs
        + [pltpu.SemaphoreType.DMA((4, 3))],
        3 * heads,
        "own",
    )
    near = (moved(both, -1, 0),)
    landed = [moved(block, 0, away + 1) for away, block in enumerate(sent)]
    for step, held in ((2, far), (1, near)):
        query_sum, *sent = call(
            functools.partial(far_kernel, heads, tile, scale, parts, step, len(held)),
            (span_ids, q, g, terms, *held, query_sum),
            [SMEM] + [VMEM] * (4 + len(held)),
            [shape((rows, dim), f32)] + [shape((share, dim), bf16)] * parts,
            accs,
            2 * heads,
            "far",
            {4 + len(held): 0},
        )
        landed += [moved(block, step, away) for away, block in enumerate(sent)]
    for block in landed:
        total = total + block.astype(f32)
    total = total.astype(bf16)
    query_grad = (query_sum * scale).astype(bf16).reshape(toks, heads, dim)
    return query_grad, total[: share // 2], total[share // 2 :]


def solution(mesh):
    in_specs = (
        P("ctx", "head", None),
        P("ctx", None),
        P("ctx", None),
        P("ctx", "head", None),
        P("ctx", "head", None),
        P("head", "ctx"),
        P(),
    )
    out_specs = (P("ctx", "head", None), P(("ctx", "head"), None), P(("ctx", "head"), None))
    return jax.shard_map(local, mesh=mesh, in_specs=in_specs, out_specs=out_specs, check_vma=False)
```

```python
import functools
import math

import jax
import jax.numpy as jnp
from jax import lax
from jax.experimental import pallas as pl
from jax.experimental.pallas import tpu as pltpu
from jax.sharding import PartitionSpec as P

STEPS = 3
NT = (((1,), (1,)), ((), ()))
NN = (((1,), (0,)), ((), ()))
TN = (((0,), (0,)), ((), ()))


def dot(a, b, dims):
    return lax.dot_general(a, b, dims, preferred_element_type=jnp.float32)


def three_terms(x):
    high = x.astype(jnp.bfloat16)
    rest = x - high.astype(jnp.float32)
    mid = rest.astype(jnp.bfloat16)
    low = (rest - mid.astype(jnp.float32)).astype(jnp.bfloat16)
    return high, mid, low


def row_terms(heads, tile, span, refs, out):
    grad_ref, outputs_ref, norm_ref = refs
    rows = grad_ref.shape[0] // 2
    toks = tile // heads
    spread = (
        lax.broadcasted_iota(jnp.int32, (toks, tile), 1) // heads
        == lax.broadcasted_iota(jnp.int32, (toks, tile), 0)
    ).astype(jnp.bfloat16)
    mine = (
        lax.broadcasted_iota(jnp.int32, (heads, tile), 1) % heads
        == lax.broadcasted_iota(jnp.int32, (heads, tile), 0)
    )
    ones = jnp.ones((8, grad_ref.shape[1]), jnp.bfloat16)
    for index in range(rows // tile):
        tok = pl.multiple_of(span * (rows // heads) + index * toks, toks)
        row = pl.multiple_of(span * rows + index * tile, tile)
        norm = norm_ref[:, pl.ds(tok, toks)] * math.log2(math.e)
        wide = sum(dot(part, spread, NN) for part in three_terms(norm))
        out[0:1, pl.ds(row, tile)] = jnp.sum(jnp.where(mine, wide, 0.0), axis=0, keepdims=True)
        prod = grad_ref[pl.ds(row, tile), :].astype(jnp.float32) * outputs_ref[
            pl.ds(row, tile), :
        ].astype(jnp.float32)
        high = prod.astype(jnp.bfloat16)
        low = (prod - high.astype(jnp.float32)).astype(jnp.bfloat16)
        out[1:2, pl.ds(row, tile)] = (dot(ones, high, NT) + dot(ones, low, NT))[0:1]


def tile_grads(group, accs, scale, tiles):
    query_ref, grad_ref, key_ref, value_ref, terms_ref, tile = group
    query_acc, key_acc, value_acc = accs

    def opened(row, key, length, _):
        k = key_ref[pl.ds(key, length), :]
        v = value_ref[pl.ds(key, length), :]
        scores = dot(k, query_ref[pl.ds(row, tile), :], NT)
        return scores, dot(v, grad_ref[pl.ds(row, tile), :], NT)

    def closed(row, key, length, triangle, scores, dprob):
        norm = terms_ref[0:1, pl.ds(row, tile)]
        delta = terms_ref[1:2, pl.ds(row, tile)]
        prob = jnp.exp2(scores * (scale * math.log2(math.e)) - norm)
        if triangle is not None:
            edge = length - triangle.shape[0]
            last = jnp.where(triangle, prob[edge:], 0.0)
            prob = last if edge == 0 else jnp.concatenate([prob[:edge], last], axis=0)
        dscore = (prob * (dprob - delta)).astype(jnp.bfloat16)
        value_acc[pl.ds(key, length), :] += dot(
            prob.astype(jnp.bfloat16), grad_ref[pl.ds(row, tile), :], NN
        )
        key_acc[pl.ds(key, length), :] += dot(dscore, query_ref[pl.ds(row, tile), :], NN)
        query_acc[pl.ds(row, tile), :] += dot(dscore, key_ref[pl.ds(key, length), :], TN)

    ahead = opened(*tiles[0])
    for index, this in enumerate(tiles):
        now = ahead
        if index + 1 < len(tiles):
            ahead = opened(*tiles[index + 1])
        closed(*this, *now)


def span_pair(span_ids, holder):
    return span_ids[2 * holder], span_ids[2 * holder + 1]


def put_shares(outs, key_acc, value_acc, scale, more=None):
    parts = len(outs)
    share = key_acc.shape[0] // parts
    x = lax.axis_index("head")
    for away, out in enumerate(outs):
        start = pl.multiple_of(lax.rem(x + away, parts) * share, share)
        for low, part in (
            (0, key_acc[pl.ds(start, share), :] * scale),
            (share, value_acc[pl.ds(start, share), :]),
        ):
            if more is not None:
                part = part + more[away, low : low + share, :].astype(jnp.float32)
            out[low : low + share, :] = part.astype(out.dtype)


def first_kernel(heads, tile, scale, *refs):
    inputs, refs = refs[:6], refs[6:]
    query_ref, grad_ref, both_ref, terms_ref, query_acc, key_acc, value_acc = refs[:7]
    outputs_ref, norm_ref, sems = refs[7:]
    toks = both_ref.shape[0] // 2
    key_ref, value_ref = both_ref.at[pl.ds(0, toks)], both_ref.at[pl.ds(toks, toks)]
    half = toks // 2
    rows = half * heads
    per = tile // heads
    whole = [
        pltpu.make_async_copy(a, b, sems.at[i, 2])
        for i, (a, b) in enumerate(zip(inputs[3:], (norm_ref, key_ref, value_ref)))
    ]

    def halves(index):
        part = pl.ds(pl.multiple_of(index * rows, rows), rows)
        return [
            pltpu.make_async_copy(a.at[part], b.at[part], sems.at[i, index])
            for i, (a, b) in enumerate(zip(inputs, (grad_ref, outputs_ref, query_ref)))
        ]

    for copy in whole + halves(0) + halves(1):
        copy.start()
    query_acc[...] = jnp.zeros_like(query_acc)
    key_acc[...] = jnp.zeros_like(key_acc)
    value_acc[...] = jnp.zeros_like(value_acc)
    group = (query_ref, grad_ref, key_ref, value_ref, terms_ref, tile)
    accs = (query_acc, key_acc, value_acc)
    triangle = lax.broadcasted_iota(jnp.int32, (per, tile), 0) <= (
        lax.broadcasted_iota(jnp.int32, (per, tile), 1) // heads
    )
    for copy in whole:
        copy.wait()

    @pl.loop(0, 2)
    def _(index):
        for copy in halves(index):
            copy.wait()
        row_terms(heads, tile, index, (grad_ref, outputs_ref, norm_ref), terms_ref)
        key = pl.multiple_of(index * half, half)
        tiles = [
            (pl.multiple_of(index * rows + part * tile, tile), key, (part + 1) * per, triangle)
            for part in range(half // per)
        ]
        tile_grads(group, accs, scale, tiles)


def last_kernel(heads, tile, scale, parts, span_ids, *refs):
    query_ref, grad_ref, terms_ref, both_ref, joined_ref = refs[:5]
    query_acc, key_acc, value_acc = refs[8:11]
    outs, more = refs[11 : 11 + parts], refs[11 + parts]
    toks = both_ref.shape[0] // 2
    key_ref, value_ref = both_ref.at[pl.ds(0, toks)], both_ref.at[pl.ds(toks, toks)]
    half = toks // 2
    me = lax.axis_index("ctx")
    even = lax.rem(me, 2) == 0

    @pl.when(even)
    def _():
        more[...] = joined_ref[...]

    @pl.when(jnp.logical_not(even))
    def _():
        more[...] = jnp.zeros_like(more)

    first, second = span_pair(span_ids, me)
    low = jnp.where(first > second, 1, 0)
    key = pl.multiple_of(low * half, half)
    rows = half * heads
    tiles = [
        (pl.multiple_of((1 - low) * rows + part * tile, tile), key, half, None)
        for part in range(rows // tile)
    ]
    group = (query_ref, grad_ref, key_ref, value_ref, terms_ref, tile)
    tile_grads(group, (query_acc, key_acc, value_acc), scale, tiles)
    put_shares(outs, key_acc, value_acc, scale, more)


def far_kernel(heads, tile, scale, parts, step, span_ids, *refs):
    query_ref, grad_ref, terms_ref, key_ref, value_ref = refs[:5]
    query_acc, outs = refs[6], refs[7:-2]
    key_acc, value_acc = refs[-2:]
    half = key_ref.shape[0] // 2
    key_acc[...] = jnp.zeros_like(key_acc)
    value_acc[...] = jnp.zeros_like(value_acc)
    group = (query_ref, grad_ref, key_ref, value_ref, terms_ref, tile)
    accs = (query_acc, key_acc, value_acc)
    per = half * heads // tile
    me, holders = lax.axis_index("ctx"), lax.axis_size("ctx")
    mine = span_pair(span_ids, me)
    theirs = span_pair(span_ids, lax.rem(me + holders - step, holders))
    high_only = jnp.minimum(*mine) < jnp.minimum(*theirs)
    our_high = jnp.where(mine[0] > mine[1], 0, 1)
    their_low = jnp.where(theirs[0] > theirs[1], 1, 0)

    @pl.loop(0, 2)
    def _(item):
        row_half = jnp.where(high_only, our_high, item)
        key_half = jnp.where(high_only, item, their_low)
        row = pl.multiple_of(row_half * half * heads, half * heads)
        key = pl.multiple_of(key_half * half, half)
        tiles = [(pl.multiple_of(row + part * tile, tile), key, half, None) for part in range(per)]
        tile_grads(group, accs, scale, tiles)

    if len(outs) == 1:
        outs = [outs[0].at[away] for away in range(parts)]
    put_shares(outs, key_acc, value_acc, scale)


VMEM = pl.BlockSpec(memory_space=pltpu.VMEM)
SMEM = pl.BlockSpec(memory_space=pltpu.SMEM)
HBM = pl.BlockSpec(memory_space=pltpu.HBM)
PARAMS = pltpu.CompilerParams(vmem_limit_bytes=20 * 1024 * 1024)


def call(kernel, ins, where, outs, scratch, blocks, name, aliases=None):
    flops = blocks * 40 * 512 * 512 * 128
    return pl.pallas_call(
        kernel,
        out_shape=outs,
        in_specs=where,
        out_specs=[VMEM] * len(outs),
        scratch_shapes=scratch,
        input_output_aliases=aliases or {},
        compiler_params=PARAMS,
        name=name,
        cost_estimate=pl.CostEstimate(flops=int(flops), bytes_accessed=6 << 20, transcendentals=0),
    )(*ins)


def moved(block, back, away):
    holders, parts = lax.axis_size("ctx"), lax.axis_size("head")
    route = [
        (h * parts + x, ((h - back[h % 2]) % holders) * parts + (x + away) % parts)
        for h in range(holders)
        for x in range(parts)
    ]
    return lax.ppermute(block, ("ctx", "head"), route)


def local(queries, keys, values, outputs, out_grad, log_norm, span_ids):
    toks, heads, dim = queries.shape
    rows = toks * heads
    scale = dim ** (-0.5)
    parts = lax.axis_size("head")
    tile = 512
    q = queries.reshape(rows, dim)
    g = out_grad.reshape(rows, dim)
    o = outputs.reshape(rows, dim)
    share = 2 * toks // parts
    f32, bf16 = jnp.float32, jnp.bfloat16
    shape = jax.ShapeDtypeStruct
    grads = [shape((share, dim), bf16)] * parts
    sums = [shape((rows, dim), f32), shape((toks, dim), f32), shape((toks, dim), f32)]

    key_1, value_1 = moved(keys, (-1, -1), 0), moved(values, (-1, -1), 0)
    inputs = tuple(
        pltpu.with_memory_space_constraint(a, pltpu.HBM) for a in (g, o, q, log_norm, keys, values)
    )
    q, g, both, terms, query_sum, key_sum, value_sum = call(
        functools.partial(first_kernel, heads, tile, scale),
        inputs,
        [HBM] * len(inputs),
        [shape((rows, dim), bf16), shape((rows, dim), bf16), shape((2 * toks, dim), bf16)]
        + [shape((8, rows), f32)]
        + sums,
        [pltpu.VMEM(a.shape, a.dtype) for a in (o, log_norm)] + [pltpu.SemaphoreType.DMA((3, 3))],
        1.25 * heads,
        "first",
    )
    key_2, value_2 = moved(key_1, (-1, -1), 0), moved(value_1, (-1, -1), 0)

    def far(step, key, value, query_sum, grads):
        return call(
            functools.partial(far_kernel, heads, tile, scale, parts, step),
            (span_ids, q, g, terms, key, value, query_sum),
            [SMEM] + [VMEM] * 6,
            [shape((rows, dim), f32)] + grads,
            [pltpu.VMEM((toks, dim), f32)] * 2,
            2 * heads,
            "far",
            {6: 0},
        )

    query_sum, near = far(1, key_1, value_1, query_sum, [shape((parts, share, dim), bf16)])
    joined = moved(near, (-1, 1), 0)
    query_sum, *sent = far(2, key_2, value_2, query_sum, grads)
    odd = lax.axis_index("ctx") % 2 == 1
    landed = []
    for away, block in enumerate(sent):
        more = jnp.where(odd, joined[away], jnp.zeros_like(block))
        block = (block.astype(f32) + more.astype(f32)).astype(bf16)
        landed.append(moved(block, (2, 2), away))
    query_sum, _, _, total, *sent = call(
        functools.partial(last_kernel, heads, tile, scale, parts),
        (span_ids, q, g, terms, both, joined, query_sum, key_sum, value_sum),
        [SMEM] + [VMEM] * 8,
        sums + [shape((share, dim), f32)] + grads[1:],
        [pltpu.VMEM((parts, share, dim), bf16)],
        heads,
        "last",
        {6: 0, 7: 1, 8: 2},
    )
    landed += [moved(block, (0, 0), away + 1) for away, block in enumerate(sent)]
    for block in landed:
        total = total + block.astype(f32)
    total = total.astype(bf16)
    query_grad = (query_sum * scale).astype(bf16).reshape(toks, heads, dim)
    return query_grad, total[: share // 2], total[share // 2 :]


def solution(mesh):
    in_specs = (
        P("ctx", "head", None),
        P("ctx", None),
        P("ctx", None),
        P("ctx", "head", None),
        P("ctx", "head", None),
        P("head", "ctx"),
        P(),
    )
    out_specs = (P("ctx", "head", None), P(("ctx", "head"), None), P(("ctx", "head"), None))
    return jax.shard_map(local, mesh=mesh, in_specs=in_specs, out_specs=out_specs, check_vma=False)
```

```python
import functools
import math

import jax
import jax.numpy as jnp
from jax import lax
from jax.experimental import pallas as pl
from jax.experimental.pallas import tpu as pltpu
from jax.sharding import PartitionSpec as P

STEPS = 3
NT = (((1,), (1,)), ((), ()))
NN = (((1,), (0,)), ((), ()))
TN = (((0,), (0,)), ((), ()))


def dot(a, b, dims):
    return lax.dot_general(a, b, dims, preferred_element_type=jnp.float32)


def three_terms(x):
    high = x.astype(jnp.bfloat16)
    rest = x - high.astype(jnp.float32)
    mid = rest.astype(jnp.bfloat16)
    low = (rest - mid.astype(jnp.float32)).astype(jnp.bfloat16)
    return high, mid, low


def row_terms(heads, tile, span, refs, out):
    grad_ref, outputs_ref, norm_ref = refs
    rows = grad_ref.shape[0] // 2
    toks = tile // heads
    spread = (
        lax.broadcasted_iota(jnp.int32, (toks, tile), 1) // heads
        == lax.broadcasted_iota(jnp.int32, (toks, tile), 0)
    ).astype(jnp.bfloat16)
    mine = (
        lax.broadcasted_iota(jnp.int32, (heads, tile), 1) % heads
        == lax.broadcasted_iota(jnp.int32, (heads, tile), 0)
    )
    ones = jnp.ones((8, grad_ref.shape[1]), jnp.bfloat16)
    for index in range(rows // tile):
        tok = pl.multiple_of(span * (rows // heads) + index * toks, toks)
        row = pl.multiple_of(span * rows + index * tile, tile)
        norm = norm_ref[:, pl.ds(tok, toks)] * math.log2(math.e)
        wide = sum(dot(part, spread, NN) for part in three_terms(norm))
        out[0:1, pl.ds(row, tile)] = jnp.sum(jnp.where(mine, wide, 0.0), axis=0, keepdims=True)
        prod = grad_ref[pl.ds(row, tile), :].astype(jnp.float32) * outputs_ref[
            pl.ds(row, tile), :
        ].astype(jnp.float32)
        high = prod.astype(jnp.bfloat16)
        low = (prod - high.astype(jnp.float32)).astype(jnp.bfloat16)
        out[1:2, pl.ds(row, tile)] = (dot(ones, high, NT) + dot(ones, low, NT))[0:1]


def tile_grads(group, accs, scale, tiles):
    query_ref, grad_ref, key_ref, value_ref, terms_ref, tile = group
    key_acc, value_acc = accs

    def opened(row, key, length, *_):
        k = key_ref[pl.ds(key, length), :]
        v = value_ref[pl.ds(key, length), :]
        scores = dot(k, query_ref[pl.ds(row, tile), :], NT)
        return scores, dot(v, grad_ref[pl.ds(row, tile), :], NT)

    def closed(row, key, length, triangle, kept, scores, dprob):
        norm = terms_ref[0:1, pl.ds(row, tile)]
        delta = terms_ref[1:2, pl.ds(row, tile)]
        prob = jnp.exp2(scores * (scale * math.log2(math.e)) - norm)
        if triangle is not None:
            edge = length - triangle.shape[0]
            last = jnp.where(triangle, prob[edge:], 0.0)
            prob = last if edge == 0 else jnp.concatenate([prob[:edge], last], axis=0)
        dscore = (prob * (dprob - delta)).astype(jnp.bfloat16)
        kept[...] = dscore
        value_acc[pl.ds(key, length), :] += dot(
            prob.astype(jnp.bfloat16), grad_ref[pl.ds(row, tile), :], NN
        )
        key_acc[pl.ds(key, length), :] += dot(dscore, query_ref[pl.ds(row, tile), :], NN)

    ahead = opened(*tiles[0])
    for index, this in enumerate(tiles):
        now = ahead
        if index + 1 < len(tiles):
            ahead = opened(*tiles[index + 1])
        closed(*this, *now)


def span_pair(span_ids, holder):
    return span_ids[2 * holder], span_ids[2 * holder + 1]


def far_halves(span_ids, step):
    me, holders = lax.axis_index("ctx"), lax.axis_size("ctx")
    mine = span_pair(span_ids, me)
    theirs = span_pair(span_ids, lax.rem(me + holders - step, holders))
    high_only = jnp.minimum(*mine) < jnp.minimum(*theirs)
    our_high = jnp.where(mine[0] > mine[1], 0, 1)
    their_low = jnp.where(theirs[0] > theirs[1], 1, 0)
    return lambda item: (
        jnp.where(high_only, our_high, item),
        jnp.where(high_only, item, their_low),
    )


def put_shares(outs, key_acc, value_acc, scale):
    parts = len(outs)
    share = key_acc.shape[0] // parts
    x = lax.axis_index("head")
    for away, out in enumerate(outs):
        start = pl.multiple_of(lax.rem(x + away, parts) * share, share)
        out[0:share, :] = (key_acc[pl.ds(start, share), :] * scale).astype(out.dtype)
        out[share : 2 * share, :] = value_acc[pl.ds(start, share), :].astype(out.dtype)


def own_kernel(heads, tile, scale, parts, *refs):
    inputs, refs = refs[:7], refs[7:]
    terms_ref, both_ref, kept_ref = refs[:3]
    outs, refs = refs[3 : 3 + parts], refs[3 + parts :]
    held, (key_acc, value_acc, sems) = refs[:5], refs[5:]
    query_ref, grad_ref, outputs_ref, norm_ref, span_ids = held
    toks = both_ref.shape[0] // 2
    key_ref, value_ref = both_ref.at[pl.ds(0, toks)], both_ref.at[pl.ds(toks, toks)]
    half = toks // 2
    rows = half * heads
    per = tile // heads
    whole = [
        pltpu.make_async_copy(a, b, sems.at[i, 2])
        for i, (a, b) in enumerate(zip(inputs[3:], (norm_ref, key_ref, value_ref, span_ids)))
    ]

    def halves(index):
        part = pl.ds(pl.multiple_of(index * rows, rows), rows)
        return [
            pltpu.make_async_copy(inputs[i].at[part], held[i].at[part], sems.at[i, index])
            for i in (1, 2, 0)
        ]

    for copy in whole + halves(0) + halves(1):
        copy.start()
    key_acc[...] = jnp.zeros_like(key_acc)
    value_acc[...] = jnp.zeros_like(value_acc)
    group = (query_ref, grad_ref, key_ref, value_ref, terms_ref, tile)
    accs = (key_acc, value_acc)
    triangle = lax.broadcasted_iota(jnp.int32, (per, tile), 0) <= (
        lax.broadcasted_iota(jnp.int32, (per, tile), 1) // heads
    )

    def placed(row, key, length, triangle):
        return row, key, length, triangle, kept_ref.at[pl.ds(key, length), pl.ds(row, tile)]

    for copy in whole:
        copy.wait()

    @pl.loop(0, 2)
    def _(index):
        for copy in halves(index):
            copy.wait()
        row_terms(heads, tile, index, (grad_ref, outputs_ref, norm_ref), terms_ref)
        key = pl.multiple_of(index * half, half)
        tiles = [
            placed(pl.multiple_of(index * rows + p * tile, tile), key, (p + 1) * per, triangle)
            for p in range(half // per)
        ]
        tile_grads(group, accs, scale, tiles)

    first, second = span_pair(span_ids, lax.axis_index("ctx"))
    low = jnp.where(first > second, 1, 0)
    key = pl.multiple_of(low * half, half)
    tiles = [
        placed(pl.multiple_of((1 - low) * rows + p * tile, tile), key, half, None)
        for p in range(rows // tile)
    ]
    tile_grads(group, accs, scale, tiles)
    put_shares(outs, key_acc, value_acc, scale)


def far_kernel(heads, tile, scale, parts, step, span_ids, *refs):
    query_ref, grad_ref, terms_ref, key_ref, value_ref, kept_ref = refs[:6]
    outs = refs[6:-2]
    key_acc, value_acc = refs[-2:]
    half = key_ref.shape[0] // 2
    rows = half * heads
    key_acc[...] = jnp.zeros_like(key_acc)
    value_acc[...] = jnp.zeros_like(value_acc)
    group = (query_ref, grad_ref, key_ref, value_ref, terms_ref, tile)
    halves = far_halves(span_ids, step)

    @pl.loop(0, 2)
    def _(item):
        row_half, key_half = halves(item)
        row = pl.multiple_of(row_half * rows, rows)
        key = pl.multiple_of(key_half * half, half)
        tiles = [
            (
                pl.multiple_of(row + p * tile, tile),
                key,
                half,
                None,
                kept_ref.at[item, :, pl.ds(p * tile, tile)],
            )
            for p in range(rows // tile)
        ]
        tile_grads(group, (key_acc, value_acc), scale, tiles)

    put_shares(outs, key_acc, value_acc, scale)


def query_kernel(heads, tile, scale, span_ids, both_ref, own_ref, *refs):
    far_refs, (out_ref, acc) = refs[:-2], refs[-2:]
    toks = both_ref.shape[0] // 2
    half = toks // 2
    rows = half * heads
    per = tile // heads

    @pl.loop(0, 2)
    def _(index):
        key = pl.multiple_of(index * half, half)
        for p in range(half // per):
            row = pl.multiple_of(index * rows + p * tile, tile)
            length = (p + 1) * per
            acc[pl.ds(row, tile), :] = dot(
                own_ref[pl.ds(key, length), pl.ds(row, tile)], both_ref[pl.ds(key, length), :], TN
            )

    first, second = span_pair(span_ids, lax.axis_index("ctx"))
    low = jnp.where(first > second, 1, 0)
    key = pl.multiple_of(low * half, half)
    for p in range(rows // tile):
        row = pl.multiple_of((1 - low) * rows + p * tile, tile)
        acc[pl.ds(row, tile), :] += dot(
            own_ref[pl.ds(key, half), pl.ds(row, tile)], both_ref[pl.ds(key, half), :], TN
        )
    for step in range(1, STEPS):
        key_ref, kept_ref = far_refs[2 * step - 2 : 2 * step]
        halves = far_halves(span_ids, step)

        @pl.loop(0, 2)
        def _(item):
            row_half, key_half = halves(item)
            key = pl.multiple_of(key_half * half, half)
            for p in range(rows // tile):
                row = pl.multiple_of(row_half * rows + p * tile, tile)
                acc[pl.ds(row, tile), :] += dot(
                    kept_ref[item, :, p * tile : (p + 1) * tile], key_ref[pl.ds(key, half), :], TN
                )

    out_ref[...] = (acc[...] * scale).astype(out_ref.dtype)


VMEM = pl.BlockSpec(memory_space=pltpu.VMEM)
SMEM = pl.BlockSpec(memory_space=pltpu.SMEM)
HBM = pl.BlockSpec(memory_space=pltpu.HBM)
MIB = 1024 * 1024


def call(kernel, ins, where, outs, scratch, blocks, limit, name):
    flops = blocks * 40 * 512 * 512 * 128
    return pl.pallas_call(
        kernel,
        out_shape=outs,
        in_specs=where,
        out_specs=[VMEM] * len(outs),
        scratch_shapes=scratch,
        compiler_params=pltpu.CompilerParams(vmem_limit_bytes=limit * MIB),
        name=name,
        cost_estimate=pl.CostEstimate(flops=int(flops), bytes_accessed=6 << 20, transcendentals=0),
    )(*ins)


def moved(block, back, away):
    holders, parts = lax.axis_size("ctx"), lax.axis_size("head")
    route = [
        (h * parts + x, ((h - back[h % 2]) % holders) * parts + (x + away) % parts)
        for h in range(holders)
        for x in range(parts)
    ]
    return lax.ppermute(block, ("ctx", "head"), route)


def local(queries, keys, values, outputs, out_grad, log_norm, span_ids):
    toks, heads, dim = queries.shape
    rows = toks * heads
    scale = dim ** (-0.5)
    parts = lax.axis_size("head")
    tile = 512
    q = queries.reshape(rows, dim)
    g = out_grad.reshape(rows, dim)
    o = outputs.reshape(rows, dim)
    share = 2 * toks // parts
    f32, bf16 = jnp.float32, jnp.bfloat16
    shape = jax.ShapeDtypeStruct
    grads = [shape((share, dim), bf16)] * parts
    accs = [pltpu.VMEM((toks, dim), f32)] * 2

    key_1, value_1 = moved(keys, (-1, -1), 0), moved(values, (-1, -1), 0)
    inputs = tuple(
        pltpu.with_memory_space_constraint(a, pltpu.HBM)
        for a in (q, g, o, log_norm, keys, values, span_ids)
    )
    terms, both, kept, total, *sent = call(
        functools.partial(own_kernel, heads, tile, scale, parts),
        inputs,
        [HBM] * len(inputs),
        [shape((8, rows), f32), shape((2 * toks, dim), bf16), shape((toks, rows), bf16)]
        + [shape((share, dim), f32)]
        + grads[1:],
        [pltpu.VMEM(a.shape, a.dtype) for a in inputs[:4]]
        + [pltpu.SMEM(span_ids.shape, span_ids.dtype)]
        + accs
        + [pltpu.SemaphoreType.DMA((4, 3))],
        2.25 * heads,
        20,
        "own",
    )
    landed = [moved(block, (0, 0), away + 1) for away, block in enumerate(sent)]
    key_2, value_2 = moved(key_1, (-1, -1), 0), moved(value_1, (-1, -1), 0)

    def far(step, key, value):
        return call(
            functools.partial(far_kernel, heads, tile, scale, parts, step),
            (span_ids, q, g, terms, key, value),
            [SMEM] + [VMEM] * 5,
            [shape((2, toks // 2, rows // 2), bf16)] + grads,
            accs,
            2 * heads,
            14,
            "far",
        )

    kept_1, *sent = far(1, key_1, value_1)
    joined = [moved(block, (-1, 1), away) for away, block in enumerate(sent)]
    kept_2, *sent = far(2, key_2, value_2)
    odd = lax.axis_index("ctx") % 2 == 1
    joined = sum(block.astype(f32) for block in joined)
    straight = sent[0].astype(f32) + jnp.where(odd, joined, 0.0)
    total = total + jnp.where(odd, 0.0, joined)
    for away, block in enumerate([straight.astype(bf16)] + sent[1:]):
        landed.append(moved(block, (2, 2), away))
    (query_grad,) = call(
        functools.partial(query_kernel, heads, tile, scale),
        (span_ids, both, kept, key_1, kept_1, key_2, kept_2),
        [SMEM] + [VMEM] * 6,
        [shape((rows, dim), bf16)],
        [pltpu.VMEM((rows, dim), f32)],
        1.25 * heads,
        28,
        "queries",
    )
    for block in landed:
        total = total + block.astype(f32)
    total = total.astype(bf16)
    return query_grad.reshape(toks, heads, dim), total[: share // 2], total[share // 2 :]


def solution(mesh):
    in_specs = (
        P("ctx", "head", None),
        P("ctx", None),
        P("ctx", None),
        P("ctx", "head", None),
        P("ctx", "head", None),
        P("head", "ctx"),
        P(),
    )
    out_specs = (P("ctx", "head", None), P(("ctx", "head"), None), P(("ctx", "head"), None))
    return jax.shard_map(local, mesh=mesh, in_specs=in_specs, out_specs=out_specs, check_vma=False)
```

```python
import functools
import math

import jax
import jax.numpy as jnp
from jax import lax
from jax.experimental import pallas as pl
from jax.experimental.pallas import tpu as pltpu
from jax.sharding import PartitionSpec as P

STEPS = 3
NT = (((1,), (1,)), ((), ()))
NN = (((1,), (0,)), ((), ()))
TN = (((0,), (0,)), ((), ()))


def dot(a, b, dims):
    return lax.dot_general(a, b, dims, preferred_element_type=jnp.float32)


def three_terms(x):
    high = x.astype(jnp.bfloat16)
    rest = x - high.astype(jnp.float32)
    mid = rest.astype(jnp.bfloat16)
    low = (rest - mid.astype(jnp.float32)).astype(jnp.bfloat16)
    return high, mid, low


def row_terms(heads, tile, span, refs, out):
    grad_ref, outputs_ref, norm_ref = refs
    rows = grad_ref.shape[0] // 2
    toks = tile // heads
    spread = (
        lax.broadcasted_iota(jnp.int32, (toks, tile), 1) // heads
        == lax.broadcasted_iota(jnp.int32, (toks, tile), 0)
    ).astype(jnp.bfloat16)
    mine = (
        lax.broadcasted_iota(jnp.int32, (heads, tile), 1) % heads
        == lax.broadcasted_iota(jnp.int32, (heads, tile), 0)
    )
    ones = jnp.ones((8, grad_ref.shape[1]), jnp.bfloat16)
    for index in range(rows // tile):
        tok = pl.multiple_of(span * (rows // heads) + index * toks, toks)
        row = pl.multiple_of(span * rows + index * tile, tile)
        norm = norm_ref[:, pl.ds(tok, toks)] * math.log2(math.e)
        wide = sum(dot(part, spread, NN) for part in three_terms(norm))
        out[0:1, pl.ds(row, tile)] = jnp.sum(jnp.where(mine, wide, 0.0), axis=0, keepdims=True)
        prod = grad_ref[pl.ds(row, tile), :].astype(jnp.float32) * outputs_ref[
            pl.ds(row, tile), :
        ].astype(jnp.float32)
        high = prod.astype(jnp.bfloat16)
        low = (prod - high.astype(jnp.float32)).astype(jnp.bfloat16)
        out[1:2, pl.ds(row, tile)] = (dot(ones, high, NT) + dot(ones, low, NT))[0:1]


def tile_grads(group, accs, scale, tiles):
    query_ref, grad_ref, key_ref, value_ref, terms_ref, tile = group
    key_acc, value_acc = accs

    def opened(row, key, length, *_):
        k = key_ref[pl.ds(key, length), :]
        v = value_ref[pl.ds(key, length), :]
        scores = dot(k, query_ref[pl.ds(row, tile), :], NT)
        return scores, dot(v, grad_ref[pl.ds(row, tile), :], NT)

    def closed(row, key, length, triangle, kept, scores, dprob):
        norm = terms_ref[0:1, pl.ds(row, tile)]
        delta = terms_ref[1:2, pl.ds(row, tile)]
        prob = jnp.exp2(scores * (scale * math.log2(math.e)) - norm)
        if triangle is not None:
            edge = length - triangle.shape[0]
            last = jnp.where(triangle, prob[edge:], 0.0)
            prob = last if edge == 0 else jnp.concatenate([prob[:edge], last], axis=0)
        dscore = (prob * (dprob - delta)).astype(jnp.bfloat16)
        kept[...] = dscore
        value_acc[pl.ds(key, length), :] += dot(
            prob.astype(jnp.bfloat16), grad_ref[pl.ds(row, tile), :], NN
        )
        key_acc[pl.ds(key, length), :] += dot(dscore, query_ref[pl.ds(row, tile), :], NN)

    ahead = opened(*tiles[0])
    for index, this in enumerate(tiles):
        now = ahead
        if index + 1 < len(tiles):
            ahead = opened(*tiles[index + 1])
        closed(*this, *now)


def span_pair(span_ids, holder):
    return span_ids[2 * holder], span_ids[2 * holder + 1]


def far_halves(span_ids, step):
    me, holders = lax.axis_index("ctx"), lax.axis_size("ctx")
    mine = span_pair(span_ids, me)
    theirs = span_pair(span_ids, lax.rem(me + holders - step, holders))
    high_only = jnp.minimum(*mine) < jnp.minimum(*theirs)
    our_high = jnp.where(mine[0] > mine[1], 0, 1)
    their_low = jnp.where(theirs[0] > theirs[1], 1, 0)
    return lambda item: (
        jnp.where(high_only, our_high, item),
        jnp.where(high_only, item, their_low),
    )


def put_shares(outs, key_acc, value_acc, scale, more=None):
    parts = len(outs)
    share = key_acc.shape[0] // parts
    x = lax.axis_index("head")
    for away, out in enumerate(outs):
        start = pl.multiple_of(lax.rem(x + away, parts) * share, share)
        for low, part in (
            (0, key_acc[pl.ds(start, share), :] * scale),
            (share, value_acc[pl.ds(start, share), :]),
        ):
            if more is not None:
                part = part + more(away, low, share)
            out[low : low + share, :] = part.astype(out.dtype)


def first_kernel(heads, tile, scale, *refs):
    inputs, refs = refs[:6], refs[6:]
    terms_ref, both_ref, kept_ref, key_acc, value_acc = refs[:5]
    held, sems = refs[5:-1], refs[-1]
    grad_ref, outputs_ref, query_ref, norm_ref = held
    toks = both_ref.shape[0] // 2
    key_ref, value_ref = both_ref.at[pl.ds(0, toks)], both_ref.at[pl.ds(toks, toks)]
    half = toks // 2
    rows = half * heads
    per = tile // heads
    whole = [
        pltpu.make_async_copy(a, b, sems.at[i, 2])
        for i, (a, b) in enumerate(zip(inputs[3:], (norm_ref, key_ref, value_ref)))
    ]

    def halves(index):
        part = pl.ds(pl.multiple_of(index * rows, rows), rows)
        return [
            pltpu.make_async_copy(inputs[i].at[part], held[i].at[part], sems.at[i, index])
            for i in range(3)
        ]

    for copy in whole + halves(0) + halves(1):
        copy.start()
    key_acc[...] = jnp.zeros_like(key_acc)
    value_acc[...] = jnp.zeros_like(value_acc)
    group = (query_ref, grad_ref, key_ref, value_ref, terms_ref, tile)
    triangle = lax.broadcasted_iota(jnp.int32, (per, tile), 0) <= (
        lax.broadcasted_iota(jnp.int32, (per, tile), 1) // heads
    )
    for copy in whole:
        copy.wait()

    @pl.loop(0, 2)
    def _(index):
        for copy in halves(index):
            copy.wait()
        row_terms(heads, tile, index, (grad_ref, outputs_ref, norm_ref), terms_ref)
        key = pl.multiple_of(index * half, half)
        tiles = []
        for p in range(half // per):
            row, length = pl.multiple_of(index * rows + p * tile, tile), (p + 1) * per
            kept = kept_ref.at[pl.ds(key, length), pl.ds(row, tile)]
            tiles.append((row, key, length, triangle, kept))
        tile_grads(group, (key_acc, value_acc), scale, tiles)


def far_kernel(heads, tile, scale, parts, step, span_ids, *refs):
    query_ref, grad_ref, terms_ref, key_ref, value_ref, kept_ref = refs[:6]
    outs = refs[6:-2]
    key_acc, value_acc = refs[-2:]
    half = key_ref.shape[0] // 2
    rows = half * heads
    key_acc[...] = jnp.zeros_like(key_acc)
    value_acc[...] = jnp.zeros_like(value_acc)
    group = (query_ref, grad_ref, key_ref, value_ref, terms_ref, tile)
    halves = far_halves(span_ids, step)

    @pl.loop(0, 2)
    def _(item):
        row_half, key_half = halves(item)
        row = pl.multiple_of(row_half * rows, rows)
        key = pl.multiple_of(key_half * half, half)
        tiles = [
            (
                pl.multiple_of(row + p * tile, tile),
                key,
                half,
                None,
                kept_ref.at[item, :, pl.ds(p * tile, tile)],
            )
            for p in range(rows // tile)
        ]
        tile_grads(group, (key_acc, value_acc), scale, tiles)

    if len(outs) == 1:
        outs = [outs[0].at[away] for away in range(parts)]
    put_shares(outs, key_acc, value_acc, scale)


def join_kernel(swapped_ref, *refs):
    ins, outs = refs[: len(refs) // 2], refs[len(refs) // 2 :]
    odd = lax.rem(lax.axis_index("ctx"), 2).astype(jnp.float32)
    for away, (this, out) in enumerate(zip(ins, outs)):
        more = swapped_ref[away].astype(jnp.float32) * odd
        out[...] = (this[...].astype(jnp.float32) + more).astype(out.dtype)


def last_kernel(heads, tile, scale, parts, span_ids, *refs):
    query_ref, grad_ref, terms_ref, both_ref, swapped_ref = refs[:5]
    kept_ref, key_acc, value_acc = refs[8:11]
    outs = refs[11:]
    toks = both_ref.shape[0] // 2
    key_ref, value_ref = both_ref.at[pl.ds(0, toks)], both_ref.at[pl.ds(toks, toks)]
    half = toks // 2
    rows = half * heads
    me = lax.axis_index("ctx")
    first, second = span_pair(span_ids, me)
    low = jnp.where(first > second, 1, 0)
    key = pl.multiple_of(low * half, half)
    tiles = []
    for p in range(rows // tile):
        row = pl.multiple_of((1 - low) * rows + p * tile, tile)
        tiles.append((row, key, half, None, kept_ref.at[pl.ds(key, half), pl.ds(row, tile)]))
    group = (query_ref, grad_ref, key_ref, value_ref, terms_ref, tile)
    tile_grads(group, (key_acc, value_acc), scale, tiles)
    even = 1.0 - lax.rem(me, 2).astype(jnp.float32)

    def more(away, start, count):
        return swapped_ref[away, start : start + count, :].astype(jnp.float32) * even

    put_shares(outs, key_acc, value_acc, scale, more)


def total_kernel(total_ref, *refs):
    ins, (key_out, value_out) = refs[:-2], refs[-2:]
    share = key_out.shape[0]
    for low, out in ((0, key_out), (share, value_out)):
        part = total_ref[low : low + share, :]
        for ref in ins:
            part = part + ref[low : low + share, :].astype(jnp.float32)
        out[...] = part.astype(out.dtype)


def query_kernel(heads, tile, scale, span_ids, both_ref, own_ref, *refs):
    far_refs, (out_ref, acc) = refs[:-2], refs[-2:]
    toks = both_ref.shape[0] // 2
    half = toks // 2
    rows = half * heads
    per = tile // heads

    @pl.loop(0, 2)
    def _(index):
        key = pl.multiple_of(index * half, half)
        for p in range(half // per):
            row = pl.multiple_of(index * rows + p * tile, tile)
            length = (p + 1) * per
            acc[pl.ds(row, tile), :] = dot(
                own_ref[pl.ds(key, length), pl.ds(row, tile)], both_ref[pl.ds(key, length), :], TN
            )

    first, second = span_pair(span_ids, lax.axis_index("ctx"))
    low = jnp.where(first > second, 1, 0)
    key = pl.multiple_of(low * half, half)
    for p in range(rows // tile):
        row = pl.multiple_of((1 - low) * rows + p * tile, tile)
        acc[pl.ds(row, tile), :] += dot(
            own_ref[pl.ds(key, half), pl.ds(row, tile)], both_ref[pl.ds(key, half), :], TN
        )
    for step in range(1, STEPS):
        key_ref, kept_ref = far_refs[2 * step - 2 : 2 * step]
        halves = far_halves(span_ids, step)

        @pl.loop(0, 2)
        def _(item):
            row_half, key_half = halves(item)
            key = pl.multiple_of(key_half * half, half)
            for p in range(rows // tile):
                row = pl.multiple_of(row_half * rows + p * tile, tile)
                acc[pl.ds(row, tile), :] += dot(
                    kept_ref[item, :, p * tile : (p + 1) * tile], key_ref[pl.ds(key, half), :], TN
                )

    out_ref[...] = (acc[...] * scale).astype(out_ref.dtype)


VMEM = pl.BlockSpec(memory_space=pltpu.VMEM)
SMEM = pl.BlockSpec(memory_space=pltpu.SMEM)
HBM = pl.BlockSpec(memory_space=pltpu.HBM)
MIB = 1024 * 1024


def call(kernel, ins, where, outs, scratch, blocks, limit, name, aliases=None):
    flops = blocks * 40 * 512 * 512 * 128
    return pl.pallas_call(
        kernel,
        out_shape=outs,
        in_specs=where,
        out_specs=[VMEM] * len(outs),
        scratch_shapes=scratch,
        input_output_aliases=aliases or {},
        compiler_params=pltpu.CompilerParams(vmem_limit_bytes=limit * MIB),
        name=name,
        cost_estimate=pl.CostEstimate(flops=int(flops), bytes_accessed=6 << 20, transcendentals=0),
    )(*ins)


def moved(block, back, away):
    holders, parts = lax.axis_size("ctx"), lax.axis_size("head")
    route = [
        (h * parts + x, ((h - back[h % 2]) % holders) * parts + (x + away) % parts)
        for h in range(holders)
        for x in range(parts)
    ]
    return lax.ppermute(block, ("ctx", "head"), route)


def local(queries, keys, values, outputs, out_grad, log_norm, span_ids):
    toks, heads, dim = queries.shape
    rows = toks * heads
    scale = dim ** (-0.5)
    parts = lax.axis_size("head")
    tile = 512
    q = queries.reshape(rows, dim)
    g = out_grad.reshape(rows, dim)
    o = outputs.reshape(rows, dim)
    share = 2 * toks // parts
    f32, bf16 = jnp.float32, jnp.bfloat16
    shape = jax.ShapeDtypeStruct
    grads = [shape((share, dim), bf16)] * parts
    packed = [shape((parts, share, dim), bf16)]
    accs = [pltpu.VMEM((toks, dim), f32)] * 2

    key_1, value_1 = moved(keys, (-1, -1), 0), moved(values, (-1, -1), 0)
    inputs = tuple(
        pltpu.with_memory_space_constraint(a, pltpu.HBM) for a in (g, o, q, log_norm, keys, values)
    )
    sums = [shape((toks, rows), bf16), shape((toks, dim), f32), shape((toks, dim), f32)]
    terms, both, kept, key_sum, value_sum = call(
        functools.partial(first_kernel, heads, tile, scale),
        inputs,
        [HBM] * len(inputs),
        [shape((8, rows), f32), shape((2 * toks, dim), bf16)] + sums,
        [pltpu.VMEM(a.shape, a.dtype) for a in inputs[:4]] + [pltpu.SemaphoreType.DMA((3, 3))],
        1.25 * heads,
        20,
        "first",
    )
    key_2, value_2 = moved(key_1, (-1, -1), 0), moved(value_1, (-1, -1), 0)

    def far(step, key, value, grads):
        return call(
            functools.partial(far_kernel, heads, tile, scale, parts, step),
            (span_ids, q, g, terms, key, value),
            [SMEM] + [VMEM] * 5,
            [shape((2, toks // 2, rows // 2), bf16)] + grads,
            accs,
            2 * heads,
            14,
            "far",
        )

    kept_1, near = far(1, key_1, value_1, packed)
    swapped = moved(near, (-1, 1), 0)
    kept_2, *sent = far(2, key_2, value_2, grads)
    sent = call(join_kernel, (swapped, *sent), [VMEM] * (1 + parts), grads, [], 0.01, 4, "join")
    landed = [moved(block, (2, 2), away) for away, block in enumerate(sent)]
    kept, _, _, total, *sent = call(
        functools.partial(last_kernel, heads, tile, scale, parts),
        (span_ids, q, g, terms, both, swapped, kept, key_sum, value_sum),
        [SMEM] + [VMEM] * 8,
        sums + [shape((share, dim), f32)] + grads[1:],
        [],
        heads,
        20,
        "last",
        {6: 0, 7: 1, 8: 2},
    )
    landed += [moved(block, (0, 0), away + 1) for away, block in enumerate(sent)]
    (query_grad,) = call(
        functools.partial(query_kernel, heads, tile, scale),
        (span_ids, both, kept, key_1, kept_1, key_2, kept_2),
        [SMEM] + [VMEM] * 6,
        [shape((rows, dim), bf16)],
        [pltpu.VMEM((rows, dim), f32)],
        1.25 * heads,
        28,
        "queries",
    )
    key_grad, value_grad = call(
        total_kernel,
        (total, *landed),
        [VMEM] * (1 + len(landed)),
        [shape((share // 2, dim), bf16)] * 2,
        [],
        0.01,
        8,
        "total",
    )
    return query_grad.reshape(toks, heads, dim), key_grad, value_grad


def solution(mesh):
    in_specs = (
        P("ctx", "head", None),
        P("ctx", None),
        P("ctx", None),
        P("ctx", "head", None),
        P("ctx", "head", None),
        P("head", "ctx"),
        P(),
    )
    out_specs = (P("ctx", "head", None), P(("ctx", "head"), None), P(("ctx", "head"), None))
    return jax.shard_map(local, mesh=mesh, in_specs=in_specs, out_specs=out_specs, check_vma=False)
```

```python
import functools
import math

import jax
import jax.numpy as jnp
from jax import lax
from jax.experimental import pallas as pl
from jax.experimental.pallas import tpu as pltpu
from jax.sharding import PartitionSpec as P

STEPS = 3
NT = (((1,), (1,)), ((), ()))
NN = (((1,), (0,)), ((), ()))
TN = (((0,), (0,)), ((), ()))


def dot(a, b, dims):
    return lax.dot_general(a, b, dims, preferred_element_type=jnp.float32)


def three_terms(x):
    high = x.astype(jnp.bfloat16)
    rest = x - high.astype(jnp.float32)
    mid = rest.astype(jnp.bfloat16)
    low = (rest - mid.astype(jnp.float32)).astype(jnp.bfloat16)
    return high, mid, low


def row_terms(heads, tile, span, refs, out):
    grad_ref, outputs_ref, norm_ref = refs
    rows = grad_ref.shape[0] // 2
    toks = tile // heads
    spread = (
        lax.broadcasted_iota(jnp.int32, (toks, tile), 1) // heads
        == lax.broadcasted_iota(jnp.int32, (toks, tile), 0)
    ).astype(jnp.bfloat16)
    mine = (
        lax.broadcasted_iota(jnp.int32, (heads, tile), 1) % heads
        == lax.broadcasted_iota(jnp.int32, (heads, tile), 0)
    )
    ones = jnp.ones((8, grad_ref.shape[1]), jnp.bfloat16)
    for index in range(rows // tile):
        tok = pl.multiple_of(span * (rows // heads) + index * toks, toks)
        row = pl.multiple_of(span * rows + index * tile, tile)
        norm = norm_ref[:, pl.ds(tok, toks)] * math.log2(math.e)
        wide = sum(dot(part, spread, NN) for part in three_terms(norm))
        out[0:1, pl.ds(row, tile)] = jnp.sum(jnp.where(mine, wide, 0.0), axis=0, keepdims=True)
        prod = grad_ref[pl.ds(row, tile), :].astype(jnp.float32) * outputs_ref[
            pl.ds(row, tile), :
        ].astype(jnp.float32)
        high = prod.astype(jnp.bfloat16)
        low = (prod - high.astype(jnp.float32)).astype(jnp.bfloat16)
        out[1:2, pl.ds(row, tile)] = (dot(ones, high, NT) + dot(ones, low, NT))[0:1]


def tile_grads(group, accs, scale, tiles):
    query_ref, grad_ref, key_ref, value_ref, terms_ref, tile = group
    key_acc, value_acc = accs

    def opened(row, key, length, *_):
        k = key_ref[pl.ds(key, length), :]
        v = value_ref[pl.ds(key, length), :]
        scores = dot(k, query_ref[pl.ds(row, tile), :], NT)
        return scores, dot(v, grad_ref[pl.ds(row, tile), :], NT)

    def closed(row, key, length, triangle, kept, scores, dprob):
        norm = terms_ref[0:1, pl.ds(row, tile)]
        delta = terms_ref[1:2, pl.ds(row, tile)]
        prob = jnp.exp2(scores * (scale * math.log2(math.e)) - norm)
        if triangle is not None:
            edge = length - triangle.shape[0]
            last = jnp.where(triangle, prob[edge:], 0.0)
            prob = last if edge == 0 else jnp.concatenate([prob[:edge], last], axis=0)
        dscore = (prob * (dprob - delta)).astype(jnp.bfloat16)
        kept[...] = dscore
        value_acc[pl.ds(key, length), :] += dot(
            prob.astype(jnp.bfloat16), grad_ref[pl.ds(row, tile), :], NN
        )
        key_acc[pl.ds(key, length), :] += dot(dscore, query_ref[pl.ds(row, tile), :], NN)

    ahead = opened(*tiles[0])
    for index, this in enumerate(tiles):
        now = ahead
        if index + 1 < len(tiles):
            ahead = opened(*tiles[index + 1])
        closed(*this, *now)


def span_pair(span_ids, holder):
    return span_ids[2 * holder], span_ids[2 * holder + 1]


def far_halves(span_ids, step):
    me, holders = lax.axis_index("ctx"), lax.axis_size("ctx")
    mine = span_pair(span_ids, me)
    theirs = span_pair(span_ids, lax.rem(me + holders - step, holders))
    high_only = jnp.minimum(*mine) < jnp.minimum(*theirs)
    our_high = jnp.where(mine[0] > mine[1], 0, 1)
    their_low = jnp.where(theirs[0] > theirs[1], 1, 0)
    return lambda item: (
        jnp.where(high_only, our_high, item),
        jnp.where(high_only, item, their_low),
    )


def put_shares(outs, key_acc, value_acc, scale, first=0, parts=None):
    parts = parts or len(outs) + first
    share = key_acc.shape[0] // parts
    x = lax.axis_index("head")
    for away, out in enumerate(outs, first):
        start = pl.multiple_of(lax.rem(x + away, parts) * share, share)
        out[0:share, :] = (key_acc[pl.ds(start, share), :] * scale).astype(out.dtype)
        out[share : 2 * share, :] = value_acc[pl.ds(start, share), :].astype(out.dtype)


def own_tiles(group, accs, scale, span_ids, kept_ref, heads, halves):
    tile = group[-1]
    toks, rows = kept_ref.shape
    half, span_rows, per = toks // 2, rows // 2, tile // heads
    first, second = span_pair(span_ids, lax.axis_index("ctx"))
    low = jnp.where(first > second, 1, 0)
    triangle = lax.broadcasted_iota(jnp.int32, (per, tile), 0) <= (
        lax.broadcasted_iota(jnp.int32, (per, tile), 1) // heads
    )

    def placed(row, key, length, triangle):
        return row, key, length, triangle, kept_ref.at[pl.ds(key, length), pl.ds(row, tile)]

    for before, which in halves:
        before()
        key = pl.multiple_of(which * half, half)
        tiles = []
        for p in range(span_rows // tile):
            row = pl.multiple_of(which * span_rows + p * tile, tile)
            tiles.append(placed(row, key, (p + 1) * per, triangle))
        tile_grads(group, accs, scale, tiles)

    def square():
        key = pl.multiple_of(low * half, half)
        tiles = []
        for p in range(span_rows // tile):
            row = pl.multiple_of((1 - low) * span_rows + p * tile, tile)
            tiles.append(placed(row, key, half, None))
        tile_grads(group, accs, scale, tiles)

    return low, square


def first_kernel(heads, tile, scale, parts, *refs):
    inputs, refs = refs[:7], refs[7:]
    terms_ref, both_ref, kept_ref, key_acc, value_acc = refs[:5]
    outs, refs = refs[5 : 4 + parts], refs[4 + parts :]
    held, span_ids, sems = refs[:-2], refs[-2], refs[-1]
    grad_ref, outputs_ref, query_ref, norm_ref = held
    toks = both_ref.shape[0] // 2
    key_ref, value_ref = both_ref.at[pl.ds(0, toks)], both_ref.at[pl.ds(toks, toks)]
    rows = toks * heads // 2
    whole = [
        pltpu.make_async_copy(a, b, sems.at[i, 2])
        for i, (a, b) in enumerate(zip(inputs[3:], (norm_ref, key_ref, value_ref, span_ids)))
    ]

    def halves(slot, index):
        part = pl.ds(pl.multiple_of(index * rows, rows), rows)
        return [
            pltpu.make_async_copy(inputs[i].at[part], held[i].at[part], sems.at[i, slot])
            for i in range(3)
        ]

    x = lax.axis_index("head")
    order = (1 - x, x) if parts == 2 else (0, 1)
    for copy in whole + halves(0, order[0]) + halves(1, order[1]):
        copy.start()
    key_acc[...] = jnp.zeros_like(key_acc)
    value_acc[...] = jnp.zeros_like(value_acc)
    for copy in whole:
        copy.wait()

    def arrive(slot):
        for copy in halves(slot, order[slot]):
            copy.wait()
        row_terms(heads, tile, order[slot], (grad_ref, outputs_ref, norm_ref), terms_ref)

    group = (query_ref, grad_ref, key_ref, value_ref, terms_ref, tile)
    accs = (key_acc, value_acc)
    todo = [(functools.partial(arrive, slot), order[slot]) for slot in range(2)]
    if parts == 2:
        low, square = own_tiles(group, accs, scale, span_ids, kept_ref, heads, todo[:1])
        arrive(1)
        pl.when(low == order[0])(square)
    else:
        _, square = own_tiles(group, accs, scale, span_ids, kept_ref, heads, todo)
        square()
    put_shares(outs, key_acc, value_acc, scale, 1)


def last_kernel(heads, tile, scale, parts, span_ids, *refs):
    query_ref, grad_ref, terms_ref, both_ref = refs[:4]
    kept_ref, key_acc, value_acc, total_ref = refs[8:]
    if parts == 2:
        toks = both_ref.shape[0] // 2
        key_ref, value_ref = both_ref.at[pl.ds(0, toks)], both_ref.at[pl.ds(toks, toks)]
        group = (query_ref, grad_ref, key_ref, value_ref, terms_ref, tile)
        x = lax.axis_index("head")
        low, square = own_tiles(
            group, (key_acc, value_acc), scale, span_ids, kept_ref, heads, [(lambda: None, x)]
        )
        pl.when(low == x)(square)
    put_shares([total_ref], key_acc, value_acc, scale, 0, parts)


def far_kernel(heads, tile, scale, parts, step, span_ids, *refs):
    query_ref, grad_ref, terms_ref, key_ref, value_ref, kept_ref = refs[:6]
    outs = refs[6:-2]
    key_acc, value_acc = refs[-2:]
    half = key_ref.shape[0] // 2
    rows = half * heads
    key_acc[...] = jnp.zeros_like(key_acc)
    value_acc[...] = jnp.zeros_like(value_acc)
    group = (query_ref, grad_ref, key_ref, value_ref, terms_ref, tile)
    halves = far_halves(span_ids, step)

    @pl.loop(0, 2)
    def _(item):
        row_half, key_half = halves(item)
        row = pl.multiple_of(row_half * rows, rows)
        key = pl.multiple_of(key_half * half, half)
        tiles = [
            (
                pl.multiple_of(row + p * tile, tile),
                key,
                half,
                None,
                kept_ref.at[item, :, pl.ds(p * tile, tile)],
            )
            for p in range(rows // tile)
        ]
        tile_grads(group, (key_acc, value_acc), scale, tiles)

    put_shares(outs, key_acc, value_acc, scale)


def join_kernel(*refs):
    this_ref, out_ref = refs[0], refs[-1]
    odd = lax.rem(lax.axis_index("ctx"), 2).astype(jnp.float32)
    more = sum(ref[...].astype(jnp.float32) for ref in refs[1:-1])
    out_ref[...] = (this_ref[...].astype(jnp.float32) + more * odd).astype(out_ref.dtype)


def total_kernel(parts, total_ref, *refs):
    ins, (key_out, value_out) = refs[:-2], refs[-2:]
    share = key_out.shape[0]
    even = 1.0 - lax.rem(lax.axis_index("ctx"), 2).astype(jnp.float32)
    for low, out in ((0, key_out), (share, value_out)):
        joined, landed = (
            sum(ref[low : low + share, :].astype(jnp.float32) for ref in some)
            for some in (ins[:parts], ins[parts:])
        )
        out[...] = (total_ref[low : low + share, :] + joined * even + landed).astype(out.dtype)


def query_kernel(heads, tile, scale, span_ids, both_ref, own_ref, *refs):
    far_refs, (out_ref, acc) = refs[:-2], refs[-2:]
    toks = both_ref.shape[0] // 2
    half = toks // 2
    rows = half * heads
    per = tile // heads

    @pl.loop(0, 2)
    def _(index):
        key = pl.multiple_of(index * half, half)
        for p in range(half // per):
            row = pl.multiple_of(index * rows + p * tile, tile)
            length = (p + 1) * per
            acc[pl.ds(row, tile), :] = dot(
                own_ref[pl.ds(key, length), pl.ds(row, tile)], both_ref[pl.ds(key, length), :], TN
            )

    first, second = span_pair(span_ids, lax.axis_index("ctx"))
    low = jnp.where(first > second, 1, 0)
    key = pl.multiple_of(low * half, half)
    for p in range(rows // tile):
        row = pl.multiple_of((1 - low) * rows + p * tile, tile)
        acc[pl.ds(row, tile), :] += dot(
            own_ref[pl.ds(key, half), pl.ds(row, tile)], both_ref[pl.ds(key, half), :], TN
        )
    for step in range(1, STEPS):
        key_ref, kept_ref = far_refs[2 * step - 2 : 2 * step]
        halves = far_halves(span_ids, step)

        @pl.loop(0, 2)
        def _(item):
            row_half, key_half = halves(item)
            key = pl.multiple_of(key_half * half, half)
            for p in range(rows // tile):
                row = pl.multiple_of(row_half * rows + p * tile, tile)
                acc[pl.ds(row, tile), :] += dot(
                    kept_ref[item, :, p * tile : (p + 1) * tile], key_ref[pl.ds(key, half), :], TN
                )

    out_ref[...] = (acc[...] * scale).astype(out_ref.dtype)


VMEM = pl.BlockSpec(memory_space=pltpu.VMEM)
SMEM = pl.BlockSpec(memory_space=pltpu.SMEM)
HBM = pl.BlockSpec(memory_space=pltpu.HBM)
ANY = pl.BlockSpec(memory_space=pl.ANY)
MIB = 1024 * 1024


def call(kernel, ins, where, outs, scratch, blocks, limit, name, aliases=None):
    flops = blocks * 40 * 512 * 512 * 128
    return pl.pallas_call(
        kernel,
        out_shape=outs,
        in_specs=where,
        out_specs=[VMEM] * len(outs),
        scratch_shapes=scratch,
        input_output_aliases=aliases or {},
        compiler_params=pltpu.CompilerParams(vmem_limit_bytes=limit * MIB),
        name=name,
        cost_estimate=pl.CostEstimate(flops=int(flops), bytes_accessed=int(blocks * (1 << 20)), transcendentals=0),
    )(*ins)


def moved(block, back, away):
    holders, parts = lax.axis_size("ctx"), lax.axis_size("head")
    route = [
        (h * parts + x, ((h - back[h % 2]) % holders) * parts + (x + away) % parts)
        for h in range(holders)
        for x in range(parts)
    ]
    return lax.ppermute(block, ("ctx", "head"), route)


def local(queries, keys, values, outputs, out_grad, log_norm, span_ids):
    toks, heads, dim = queries.shape
    rows = toks * heads
    scale = dim ** (-0.5)
    parts = lax.axis_size("head")
    tile = 512
    q = queries.reshape(rows, dim)
    g = out_grad.reshape(rows, dim)
    o = outputs.reshape(rows, dim)
    share = 2 * toks // parts
    f32, bf16 = jnp.float32, jnp.bfloat16
    shape = jax.ShapeDtypeStruct
    grads = [shape((share, dim), bf16)] * parts
    accs = [pltpu.VMEM((toks, dim), f32)] * 2

    key_1, value_1 = moved(keys, (-1, -1), 0), moved(values, (-1, -1), 0)
    inputs = tuple(
        pltpu.with_memory_space_constraint(a, pltpu.HBM)
        for a in (g, o, q, log_norm, keys, values, span_ids)
    )
    sums = [shape((toks, rows), bf16), shape((toks, dim), f32), shape((toks, dim), f32)]
    terms, both, kept, key_sum, value_sum, *sent = call(
        functools.partial(first_kernel, heads, tile, scale, parts),
        inputs,
        [HBM] * len(inputs),
        [shape((8, rows), f32), shape((2 * toks, dim), bf16)] + sums + grads[1:],
        [pltpu.VMEM(a.shape, a.dtype) for a in inputs[:4]]
        + [pltpu.SMEM(span_ids.shape, span_ids.dtype), pltpu.SemaphoreType.DMA((4, 3))],
        1.625 * heads,
        20,
        "first",
    )
    landed = [moved(block, (0, 0), away + 1) for away, block in enumerate(sent)]
    key_2, value_2 = moved(key_1, (-1, -1), 0), moved(value_1, (-1, -1), 0)

    def far(step, key, value):
        return call(
            functools.partial(far_kernel, heads, tile, scale, parts, step),
            (span_ids, q, g, terms, key, value),
            [SMEM] + [VMEM] * 5,
            [shape((2, toks // 2, rows // 2), bf16)] + grads,
            accs,
            2 * heads,
            14,
            "far",
        )

    kept_1, *sent = far(1, key_1, value_1)
    joined = [moved(block, (-1, 1), away) for away, block in enumerate(sent)]
    kept_2, *sent = far(2, key_2, value_2)
    sent[:1] = call(
        join_kernel, (sent[0], *joined), [VMEM] * (1 + parts), grads[:1], [], 0.01, 4, "join"
    )
    landed += [moved(block, (2, 2), away) for away, block in enumerate(sent)]
    kept, _, _, total = call(
        functools.partial(last_kernel, heads, tile, scale, parts),
        (span_ids, q, g, terms, both, kept, key_sum, value_sum, sent[0]),
        [SMEM] + [VMEM] * 7 + [ANY],
        sums + [shape((share, dim), f32)],
        [],
        1.625 * heads,
        20,
        "last",
        {5: 0, 6: 1, 7: 2},
    )
    (query_grad,) = call(
        functools.partial(query_kernel, heads, tile, scale),
        (span_ids, both, kept, key_1, kept_1, key_2, kept_2),
        [SMEM] + [VMEM] * 6,
        [shape((rows, dim), bf16)],
        [pltpu.VMEM((rows, dim), f32)],
        1.25 * heads,
        28,
        "queries",
    )
    key_grad, value_grad = call(
        functools.partial(total_kernel, parts),
        (total, *joined, *landed),
        [VMEM] * (1 + len(joined) + len(landed)),
        [shape((share // 2, dim), bf16)] * 2,
        [],
        0.01,
        8,
        "total",
    )
    return query_grad.reshape(toks, heads, dim), key_grad, value_grad


def solution(mesh):
    in_specs = (
        P("ctx", "head", None),
        P("ctx", None),
        P("ctx", None),
        P("ctx", "head", None),
        P("ctx", "head", None),
        P("head", "ctx"),
        P(),
    )
    out_specs = (P("ctx", "head", None), P(("ctx", "head"), None), P(("ctx", "head"), None))
    return jax.shard_map(local, mesh=mesh, in_specs=in_specs, out_specs=out_specs, check_vma=False)
```

```python
import functools
import math

import jax
import jax.numpy as jnp
from jax import lax
from jax.experimental import pallas as pl
from jax.experimental.pallas import tpu as pltpu
from jax.sharding import PartitionSpec as P

STEPS = 3
NT = (((1,), (1,)), ((), ()))
NN = (((1,), (0,)), ((), ()))
TN = (((0,), (0,)), ((), ()))


def dot(a, b, dims):
    return lax.dot_general(a, b, dims, preferred_element_type=jnp.float32)


def three_terms(x):
    high = x.astype(jnp.bfloat16)
    rest = x - high.astype(jnp.float32)
    mid = rest.astype(jnp.bfloat16)
    low = (rest - mid.astype(jnp.float32)).astype(jnp.bfloat16)
    return high, mid, low


def row_terms(heads, tile, span, refs, out):
    grad_ref, outputs_ref, norm_ref = refs
    rows = grad_ref.shape[0] // 2
    toks = tile // heads
    spread = (
        lax.broadcasted_iota(jnp.int32, (toks, tile), 1) // heads
        == lax.broadcasted_iota(jnp.int32, (toks, tile), 0)
    ).astype(jnp.bfloat16)
    mine = (
        lax.broadcasted_iota(jnp.int32, (heads, tile), 1) % heads
        == lax.broadcasted_iota(jnp.int32, (heads, tile), 0)
    )
    ones = jnp.ones((8, grad_ref.shape[1]), jnp.bfloat16)
    for index in range(rows // tile):
        tok = pl.multiple_of(span * (rows // heads) + index * toks, toks)
        row = pl.multiple_of(span * rows + index * tile, tile)
        norm = norm_ref[:, pl.ds(tok, toks)] * math.log2(math.e)
        wide = sum(dot(part, spread, NN) for part in three_terms(norm))
        out[0:1, pl.ds(row, tile)] = jnp.sum(jnp.where(mine, wide, 0.0), axis=0, keepdims=True)
        prod = grad_ref[pl.ds(row, tile), :].astype(jnp.float32) * outputs_ref[
            pl.ds(row, tile), :
        ].astype(jnp.float32)
        high = prod.astype(jnp.bfloat16)
        low = (prod - high.astype(jnp.float32)).astype(jnp.bfloat16)
        out[1:2, pl.ds(row, tile)] = (dot(ones, high, NT) + dot(ones, low, NT))[0:1]


def tile_grads(group, accs, scale, tiles):
    query_ref, grad_ref, key_ref, value_ref, terms_ref, tile = group
    key_acc, value_acc = accs

    def opened(row, key, length, *_):
        k = key_ref[pl.ds(key, length), :]
        v = value_ref[pl.ds(key, length), :]
        scores = dot(k, query_ref[pl.ds(row, tile), :], NT)
        return scores, dot(v, grad_ref[pl.ds(row, tile), :], NT)

    def closed(row, key, length, triangle, kept, scores, dprob):
        norm = terms_ref[0:1, pl.ds(row, tile)]
        delta = terms_ref[1:2, pl.ds(row, tile)]
        prob = jnp.exp2(scores * (scale * math.log2(math.e)) - norm)
        if triangle is not None:
            edge = length - triangle.shape[0]
            last = jnp.where(triangle, prob[edge:], 0.0)
            prob = last if edge == 0 else jnp.concatenate([prob[:edge], last], axis=0)
        dscore = (prob * (dprob - delta)).astype(jnp.bfloat16)
        kept[...] = dscore
        value_acc[pl.ds(key, length), :] += dot(
            prob.astype(jnp.bfloat16), grad_ref[pl.ds(row, tile), :], NN
        )
        key_acc[pl.ds(key, length), :] += dot(dscore, query_ref[pl.ds(row, tile), :], NN)

    ahead = opened(*tiles[0])
    for index, this in enumerate(tiles):
        now = ahead
        if index + 1 < len(tiles):
            ahead = opened(*tiles[index + 1])
        closed(*this, *now)


def span_pair(span_ids, holder):
    return span_ids[2 * holder], span_ids[2 * holder + 1]


def far_halves(span_ids, step):
    me, holders = lax.axis_index("ctx"), lax.axis_size("ctx")
    mine = span_pair(span_ids, me)
    theirs = span_pair(span_ids, lax.rem(me + holders - step, holders))
    high_only = jnp.minimum(*mine) < jnp.minimum(*theirs)
    our_high = jnp.where(mine[0] > mine[1], 0, 1)
    their_low = jnp.where(theirs[0] > theirs[1], 1, 0)
    return lambda item: (
        jnp.where(high_only, our_high, item),
        jnp.where(high_only, item, their_low),
    )


def put_shares(outs, key_acc, value_acc, scale, first=0, parts=None):
    parts = parts or len(outs) + first
    share = key_acc.shape[0] // parts
    x = lax.axis_index("head")
    for away, out in enumerate(outs, first):
        start = pl.multiple_of(lax.rem(x + away, parts) * share, share)
        out[0:share, :] = (key_acc[pl.ds(start, share), :] * scale).astype(out.dtype)
        out[share : 2 * share, :] = value_acc[pl.ds(start, share), :].astype(out.dtype)


def own_tiles(group, accs, scale, span_ids, kept_ref, heads, halves):
    tile = group[-1]
    toks, rows = kept_ref.shape
    half, span_rows, per = toks // 2, rows // 2, tile // heads
    first, second = span_pair(span_ids, lax.axis_index("ctx"))
    low = jnp.where(first > second, 1, 0)
    triangle = lax.broadcasted_iota(jnp.int32, (per, tile), 0) <= (
        lax.broadcasted_iota(jnp.int32, (per, tile), 1) // heads
    )

    def placed(row, key, length, triangle):
        return row, key, length, triangle, kept_ref.at[pl.ds(key, length), pl.ds(row, tile)]

    for before, which in halves:
        before()
        key = pl.multiple_of(which * half, half)
        tiles = []
        for p in range(span_rows // tile):
            row = pl.multiple_of(which * span_rows + p * tile, tile)
            tiles.append(placed(row, key, (p + 1) * per, triangle))
        tile_grads(group, accs, scale, tiles)

    def square():
        key = pl.multiple_of(low * half, half)
        tiles = []
        for p in range(span_rows // tile):
            row = pl.multiple_of((1 - low) * span_rows + p * tile, tile)
            tiles.append(placed(row, key, half, None))
        tile_grads(group, accs, scale, tiles)

    return low, square


def first_kernel(heads, tile, scale, parts, *refs):
    inputs, refs = refs[:7], refs[7:]
    terms_ref, both_ref, kept_ref, key_acc, value_acc = refs[:5]
    held, span_ids, sems = refs[5:-2], refs[-2], refs[-1]
    grad_ref, outputs_ref, query_ref, norm_ref = held
    toks = both_ref.shape[0] // 2
    key_ref, value_ref = both_ref.at[pl.ds(0, toks)], both_ref.at[pl.ds(toks, toks)]
    rows = toks * heads // 2
    whole = [
        pltpu.make_async_copy(a, b, sems.at[i, 2])
        for i, (a, b) in enumerate(zip(inputs[3:], (norm_ref, key_ref, value_ref, span_ids)))
    ]

    def halves(slot, index):
        part = pl.ds(pl.multiple_of(index * rows, rows), rows)
        return [
            pltpu.make_async_copy(inputs[i].at[part], held[i].at[part], sems.at[i, slot])
            for i in range(3)
        ]

    x = lax.axis_index("head")
    order = (1 - x, x) if parts == 2 else (0, 1)
    for copy in whole + halves(0, order[0]) + halves(1, order[1]):
        copy.start()
    key_acc[...] = jnp.zeros_like(key_acc)
    value_acc[...] = jnp.zeros_like(value_acc)
    for copy in whole:
        copy.wait()

    def arrive(slot):
        for copy in halves(slot, order[slot]):
            copy.wait()
        row_terms(heads, tile, order[slot], (grad_ref, outputs_ref, norm_ref), terms_ref)

    group = (query_ref, grad_ref, key_ref, value_ref, terms_ref, tile)
    accs = (key_acc, value_acc)
    todo = [(functools.partial(arrive, slot), order[slot]) for slot in range(2)]
    if parts == 2:
        low, square = own_tiles(group, accs, scale, span_ids, kept_ref, heads, todo[:1])
        arrive(1)
        pl.when(low == order[0])(square)
    else:
        _, square = own_tiles(group, accs, scale, span_ids, kept_ref, heads, todo)
        square()


def last_kernel(heads, tile, scale, parts, span_ids, *refs):
    query_ref, grad_ref, terms_ref, both_ref = refs[:4]
    kept_ref, key_acc, value_acc, total_ref = refs[8:]
    if parts == 2:
        toks = both_ref.shape[0] // 2
        key_ref, value_ref = both_ref.at[pl.ds(0, toks)], both_ref.at[pl.ds(toks, toks)]
        group = (query_ref, grad_ref, key_ref, value_ref, terms_ref, tile)
        x = lax.axis_index("head")
        low, square = own_tiles(
            group, (key_acc, value_acc), scale, span_ids, kept_ref, heads, [(lambda: None, x)]
        )
        pl.when(low == x)(square)
    put_shares([total_ref], key_acc, value_acc, scale, 0, parts)


def far_kernel(heads, tile, scale, parts, step, span_ids, *refs):
    query_ref, grad_ref, terms_ref, key_ref, value_ref = refs[:5]
    own, refs = (refs[5:7], refs[7:]) if step == 1 else (None, refs[5:])
    kept_ref, outs, own_outs = refs[0], refs[1 : 1 + parts], refs[1 + parts : -2]
    key_acc, value_acc = refs[-2:]
    if own:
        put_shares(own_outs, *own, scale, 1)
    half = key_ref.shape[0] // 2
    rows = half * heads
    key_acc[...] = jnp.zeros_like(key_acc)
    value_acc[...] = jnp.zeros_like(value_acc)
    group = (query_ref, grad_ref, key_ref, value_ref, terms_ref, tile)
    halves = far_halves(span_ids, step)

    @pl.loop(0, 2)
    def _(item):
        row_half, key_half = halves(item)
        row = pl.multiple_of(row_half * rows, rows)
        key = pl.multiple_of(key_half * half, half)
        tiles = [
            (
                pl.multiple_of(row + p * tile, tile),
                key,
                half,
                None,
                kept_ref.at[item, :, pl.ds(p * tile, tile)],
            )
            for p in range(rows // tile)
        ]
        tile_grads(group, (key_acc, value_acc), scale, tiles)

    put_shares(outs, key_acc, value_acc, scale)


def join_kernel(*refs):
    this_ref, out_ref = refs[0], refs[-1]
    odd = lax.rem(lax.axis_index("ctx"), 2).astype(jnp.float32)
    more = sum(ref[...].astype(jnp.float32) for ref in refs[1:-1])
    out_ref[...] = (this_ref[...].astype(jnp.float32) + more * odd).astype(out_ref.dtype)


def total_kernel(parts, total_ref, *refs):
    ins, (key_out, value_out) = refs[:-2], refs[-2:]
    share = key_out.shape[0]
    even = 1.0 - lax.rem(lax.axis_index("ctx"), 2).astype(jnp.float32)
    for low, out in ((0, key_out), (share, value_out)):
        joined, landed = (
            sum(ref[low : low + share, :].astype(jnp.float32) for ref in some)
            for some in (ins[:parts], ins[parts:])
        )
        out[...] = (total_ref[low : low + share, :] + joined * even + landed).astype(out.dtype)


def query_kernel(heads, tile, scale, span_ids, both_ref, own_ref, *refs):
    far_refs, (out_ref, acc, turned) = refs[:-3], refs[-3:]
    toks = both_ref.shape[0] // 2
    half = toks // 2
    rows = half * heads
    per = tile // heads
    for index, key_ref in enumerate([both_ref] + list(far_refs[::2])):
        for low in range(0, toks, half):
            turned[index, :, low : low + half] = key_ref[low : low + half, :].T

    @pl.loop(0, 2)
    def _(index):
        key = pl.multiple_of(index * half, half)
        for p in range(half // per):
            row = pl.multiple_of(index * rows + p * tile, tile)
            length = (p + 1) * per
            acc[:, pl.ds(row, tile)] = dot(
                turned[0, :, pl.ds(key, length)], own_ref[pl.ds(key, length), pl.ds(row, tile)], NN
            )

    first, second = span_pair(span_ids, lax.axis_index("ctx"))
    low = jnp.where(first > second, 1, 0)
    key = pl.multiple_of(low * half, half)
    for p in range(rows // tile):
        row = pl.multiple_of((1 - low) * rows + p * tile, tile)
        acc[:, pl.ds(row, tile)] += dot(
            turned[0, :, pl.ds(key, half)], own_ref[pl.ds(key, half), pl.ds(row, tile)], NN
        )
    for step in range(1, STEPS):
        kept_ref = far_refs[2 * step - 1]
        halves = far_halves(span_ids, step)

        @pl.loop(0, 2)
        def _(item):
            row_half, key_half = halves(item)
            key = pl.multiple_of(key_half * half, half)
            for p in range(rows // tile):
                row = pl.multiple_of(row_half * rows + p * tile, tile)
                acc[:, pl.ds(row, tile)] += dot(
                    turned[step, :, pl.ds(key, half)],
                    kept_ref[item, :, p * tile : (p + 1) * tile],
                    NN,
                )

    for row in range(0, 2 * rows, tile):
        out_ref[row : row + tile, :] = (acc[:, row : row + tile] * scale).T.astype(out_ref.dtype)


VMEM = pl.BlockSpec(memory_space=pltpu.VMEM)
SMEM = pl.BlockSpec(memory_space=pltpu.SMEM)
HBM = pl.BlockSpec(memory_space=pltpu.HBM)
ANY = pl.BlockSpec(memory_space=pl.ANY)
MIB = 1024 * 1024


def call(kernel, ins, where, outs, scratch, blocks, limit, name, aliases=None):
    flops = blocks * 40 * 512 * 512 * 128
    return pl.pallas_call(
        kernel,
        out_shape=outs,
        in_specs=where,
        out_specs=[VMEM] * len(outs),
        scratch_shapes=scratch,
        input_output_aliases=aliases or {},
        compiler_params=pltpu.CompilerParams(vmem_limit_bytes=limit * MIB),
        name=name,
        cost_estimate=pl.CostEstimate(flops=int(flops), bytes_accessed=int(blocks * (1 << 20)), transcendentals=0),
    )(*ins)


def moved(block, back, away):
    holders, parts = lax.axis_size("ctx"), lax.axis_size("head")
    route = [
        (h * parts + x, ((h - back[h % 2]) % holders) * parts + (x + away) % parts)
        for h in range(holders)
        for x in range(parts)
    ]
    return lax.ppermute(block, ("ctx", "head"), route)


def local(queries, keys, values, outputs, out_grad, log_norm, span_ids):
    toks, heads, dim = queries.shape
    rows = toks * heads
    scale = dim ** (-0.5)
    parts = lax.axis_size("head")
    tile = 512
    q = queries.reshape(rows, dim)
    g = out_grad.reshape(rows, dim)
    o = outputs.reshape(rows, dim)
    share = 2 * toks // parts
    f32, bf16 = jnp.float32, jnp.bfloat16
    shape = jax.ShapeDtypeStruct
    grads = [shape((share, dim), bf16)] * parts
    accs = [pltpu.VMEM((toks, dim), f32)] * 2

    key_1, value_1 = moved(keys, (-1, -1), 0), moved(values, (-1, -1), 0)
    inputs = tuple(
        pltpu.with_memory_space_constraint(a, pltpu.HBM)
        for a in (g, o, q, log_norm, keys, values, span_ids)
    )
    sums = [shape((toks, rows), bf16), shape((toks, dim), f32), shape((toks, dim), f32)]
    terms, both, kept, key_sum, value_sum = call(
        functools.partial(first_kernel, heads, tile, scale, parts),
        inputs,
        [HBM] * len(inputs),
        [shape((8, rows), f32), shape((2 * toks, dim), bf16)] + sums,
        [pltpu.VMEM(a.shape, a.dtype) for a in inputs[:4]]
        + [pltpu.SMEM(span_ids.shape, span_ids.dtype), pltpu.SemaphoreType.DMA((4, 3))],
        1.625 * heads,
        20,
        "first",
    )
    key_2, value_2 = moved(key_1, (-1, -1), 0), moved(value_1, (-1, -1), 0)

    def far(step, key, value, *own):
        return call(
            functools.partial(far_kernel, heads, tile, scale, parts, step),
            (span_ids, q, g, terms, key, value, *own),
            [SMEM] + [VMEM] * (5 + len(own)),
            [shape((2, toks // 2, rows // 2), bf16)] + grads + (grads[1:] if own else []),
            accs,
            2 * heads,
            14,
            "far",
        )

    kept_1, *sent = far(1, key_1, value_1, key_sum, value_sum)
    joined = [moved(block, (-1, 1), away) for away, block in enumerate(sent[:parts])]
    landed = [moved(block, (0, 0), away + 1) for away, block in enumerate(sent[parts:])]
    kept_2, *sent = far(2, key_2, value_2)
    sent[:1] = call(
        join_kernel, (sent[0], *joined), [VMEM] * (1 + parts), grads[:1], [], 0.01, 4, "join"
    )
    landed += [moved(block, (2, 2), away) for away, block in enumerate(sent)]
    kept, _, _, total = call(
        functools.partial(last_kernel, heads, tile, scale, parts),
        (span_ids, q, g, terms, both, kept, key_sum, value_sum, sent[0]),
        [SMEM] + [VMEM] * 7 + [ANY],
        sums + [shape((share, dim), f32)],
        [],
        1.625 * heads,
        20,
        "last",
        {5: 0, 6: 1, 7: 2},
    )
    (query_grad,) = call(
        functools.partial(query_kernel, heads, tile, scale),
        (span_ids, both, kept, key_1, kept_1, key_2, kept_2),
        [SMEM] + [VMEM] * 6,
        [shape((rows, dim), bf16)],
        [pltpu.VMEM((dim, rows), f32), pltpu.VMEM((STEPS, dim, toks), bf16)],
        1.25 * heads,
        28,
        "queries",
    )
    key_grad, value_grad = call(
        functools.partial(total_kernel, parts),
        (total, *joined, *landed),
        [VMEM] * (1 + len(joined) + len(landed)),
        [shape((share // 2, dim), bf16)] * 2,
        [],
        0.01,
        8,
        "total",
    )
    return query_grad.reshape(toks, heads, dim), key_grad, value_grad


def solution(mesh):
    in_specs = (
        P("ctx", "head", None),
        P("ctx", None),
        P("ctx", None),
        P("ctx", "head", None),
        P("ctx", "head", None),
        P("head", "ctx"),
        P(),
    )
    out_specs = (P("ctx", "head", None), P(("ctx", "head"), None), P(("ctx", "head"), None))
    return jax.shard_map(local, mesh=mesh, in_specs=in_specs, out_specs=out_specs, check_vma=False)
```

```python
import functools
import math

import jax
import jax.numpy as jnp
from jax import lax
from jax.experimental import pallas as pl
from jax.experimental.pallas import tpu as pltpu
from jax.sharding import PartitionSpec as P

STEPS = 3
NT = (((1,), (1,)), ((), ()))
NN = (((1,), (0,)), ((), ()))
TN = (((0,), (0,)), ((), ()))


def dot(a, b, dims):
    return lax.dot_general(a, b, dims, preferred_element_type=jnp.float32)


def three_terms(x):
    high = x.astype(jnp.bfloat16)
    rest = x - high.astype(jnp.float32)
    mid = rest.astype(jnp.bfloat16)
    low = (rest - mid.astype(jnp.float32)).astype(jnp.bfloat16)
    return high, mid, low


def row_terms(heads, tile, span, refs, out):
    grad_ref, outputs_ref, norm_ref = refs
    rows = grad_ref.shape[0] // 2
    toks = tile // heads
    spread = (
        lax.broadcasted_iota(jnp.int32, (toks, tile), 1) // heads
        == lax.broadcasted_iota(jnp.int32, (toks, tile), 0)
    ).astype(jnp.bfloat16)
    mine = (
        lax.broadcasted_iota(jnp.int32, (heads, tile), 1) % heads
        == lax.broadcasted_iota(jnp.int32, (heads, tile), 0)
    )
    ones = jnp.ones((8, grad_ref.shape[1]), jnp.bfloat16)
    for index in range(rows // tile):
        tok = pl.multiple_of(span * (rows // heads) + index * toks, toks)
        row = pl.multiple_of(span * rows + index * tile, tile)
        norm = norm_ref[:, pl.ds(tok, toks)] * math.log2(math.e)
        wide = sum(dot(part, spread, NN) for part in three_terms(norm))
        out[0:1, pl.ds(row, tile)] = jnp.sum(jnp.where(mine, wide, 0.0), axis=0, keepdims=True)
        prod = grad_ref[pl.ds(row, tile), :].astype(jnp.float32) * outputs_ref[
            pl.ds(row, tile), :
        ].astype(jnp.float32)
        high = prod.astype(jnp.bfloat16)
        low = (prod - high.astype(jnp.float32)).astype(jnp.bfloat16)
        out[1:2, pl.ds(row, tile)] = (dot(ones, high, NT) + dot(ones, low, NT))[0:1]


def opened(group, row, key, length):
    query_ref, grad_ref, key_ref, value_ref, _, tile = group
    k = key_ref[pl.ds(key, length), :]
    v = value_ref[pl.ds(key, length), :]
    scores = dot(k, query_ref[pl.ds(row, tile), :], NT)
    return scores, dot(v, grad_ref[pl.ds(row, tile), :], NT)


def closed(group, scale, row, triangle, scores, dprob):
    terms_ref, tile = group[4:]
    norm = terms_ref[0:1, pl.ds(row, tile)]
    delta = terms_ref[1:2, pl.ds(row, tile)]
    prob = jnp.exp2(scores * (scale * math.log2(math.e)) - norm)
    if triangle is not None:
        edge = prob.shape[0] - triangle.shape[0]
        last = jnp.where(triangle, prob[edge:], 0.0)
        prob = last if edge == 0 else jnp.concatenate([prob[:edge], last], axis=0)
    return prob.astype(jnp.bfloat16), (prob * (dprob - delta)).astype(jnp.bfloat16)


def triangle_grads(group, accs, scale, row, key, half, triangle, kept_ref):
    query_ref, grad_ref, tile = group[0], group[1], group[-1]
    key_acc, value_acc = accs
    per = triangle.shape[0]
    tiles = [(pl.multiple_of(row + p * tile, tile), (p + 1) * per) for p in range(half // per)]
    ahead = opened(group, tiles[0][0], key, tiles[0][1])
    for index, (row, length) in enumerate(tiles):
        now = ahead
        if index + 1 < len(tiles):
            ahead = opened(group, tiles[index + 1][0], key, tiles[index + 1][1])
        prob, dscore = closed(group, scale, row, triangle, *now)
        kept_ref[pl.ds(key, length), pl.ds(row, tile)] = dscore
        value_acc[pl.ds(key, length), :] += dot(prob, grad_ref[pl.ds(row, tile), :], NN)
        key_acc[pl.ds(key, length), :] += dot(dscore, query_ref[pl.ds(row, tile), :], NN)


def block_grads(group, accs, scale, rows, blocks):
    query_ref, grad_ref, tile = group[0], group[1], group[-1]
    key_acc, value_acc = accs
    count = rows // tile
    tiles = [(block, p) for block in blocks for p in range(count)]

    def start(block, p):
        row, key, length = block[:3]
        return opened(group, pl.multiple_of(row + p * tile, tile), key, length)

    ahead = start(*tiles[0])
    for index, (block, p) in enumerate(tiles):
        now = ahead
        if index + 1 < len(tiles):
            ahead = start(*tiles[index + 1])
        row, key, length, kept, probs = block
        prob, dscore = closed(group, scale, pl.multiple_of(row + p * tile, tile), None, *now)
        probs[:, p * tile : (p + 1) * tile] = prob
        kept[:, p * tile : (p + 1) * tile] = dscore
        if p == count - 1:
            value_acc[pl.ds(key, length), :] += dot(probs[...], grad_ref[pl.ds(row, rows), :], NN)
            key_acc[pl.ds(key, length), :] += dot(kept[...], query_ref[pl.ds(row, rows), :], NN)


def span_pair(span_ids, holder):
    return span_ids[2 * holder], span_ids[2 * holder + 1]


def far_halves(span_ids, step):
    me, holders = lax.axis_index("ctx"), lax.axis_size("ctx")
    mine = span_pair(span_ids, me)
    theirs = span_pair(span_ids, lax.rem(me + holders - step, holders))
    high_only = jnp.minimum(*mine) < jnp.minimum(*theirs)
    our_high = jnp.where(mine[0] > mine[1], 0, 1)
    their_low = jnp.where(theirs[0] > theirs[1], 1, 0)
    return lambda item: (
        jnp.where(high_only, our_high, item),
        jnp.where(high_only, item, their_low),
    )


def put_shares(outs, key_acc, value_acc, scale, first=0, parts=None):
    parts = parts or len(outs) + first
    share = key_acc.shape[0] // parts
    x = lax.axis_index("head")
    for away, out in enumerate(outs, first):
        start = pl.multiple_of(lax.rem(x + away, parts) * share, share)
        out[0:share, :] = (key_acc[pl.ds(start, share), :] * scale).astype(out.dtype)
        out[share : 2 * share, :] = value_acc[pl.ds(start, share), :].astype(out.dtype)


def own_work(group, accs, scale, span_ids, kept_ref, probs_ref, heads):
    tile = group[-1]
    toks, rows = kept_ref.shape
    half, span_rows, per = toks // 2, rows // 2, tile // heads
    first, second = span_pair(span_ids, lax.axis_index("ctx"))
    low = jnp.where(first > second, 1, 0)
    triangle = lax.broadcasted_iota(jnp.int32, (per, tile), 0) <= (
        lax.broadcasted_iota(jnp.int32, (per, tile), 1) // heads
    )

    def corner(which):
        key = pl.multiple_of(which * half, half)
        row = pl.multiple_of(which * span_rows, span_rows)
        triangle_grads(group, accs, scale, row, key, half, triangle, kept_ref)

    def square():
        key = pl.multiple_of(low * half, half)
        row = pl.multiple_of((1 - low) * span_rows, span_rows)
        kept = kept_ref.at[pl.ds(key, half), pl.ds(row, span_rows)]
        block_grads(group, accs, scale, span_rows, [(row, key, half, kept, probs_ref)])

    return low, corner, square


def first_kernel(heads, tile, scale, parts, *refs):
    inputs, refs = refs[:7], refs[7:]
    terms_ref, both_ref, kept_ref, key_acc, value_acc = refs[:5]
    held, (probs_ref, span_ids, sems) = refs[5:-3], refs[-3:]
    grad_ref, outputs_ref, query_ref, norm_ref = held
    toks = both_ref.shape[0] // 2
    key_ref, value_ref = both_ref.at[pl.ds(0, toks)], both_ref.at[pl.ds(toks, toks)]
    rows = toks * heads // 2
    whole = [
        pltpu.make_async_copy(a, b, sems.at[i, 2])
        for i, (a, b) in enumerate(zip(inputs[3:], (norm_ref, key_ref, value_ref, span_ids)))
    ]

    def halves(slot, index):
        part = pl.ds(pl.multiple_of(index * rows, rows), rows)
        return [
            pltpu.make_async_copy(inputs[i].at[part], held[i].at[part], sems.at[i, slot])
            for i in range(3)
        ]

    x = lax.axis_index("head")
    order = (1 - x, x) if parts == 2 else (0, 1)
    for copy in whole + halves(0, order[0]) + halves(1, order[1]):
        copy.start()
    key_acc[...] = jnp.zeros_like(key_acc)
    value_acc[...] = jnp.zeros_like(value_acc)
    for copy in whole:
        copy.wait()

    def arrive(slot):
        for copy in halves(slot, order[slot]):
            copy.wait()
        row_terms(heads, tile, order[slot], (grad_ref, outputs_ref, norm_ref), terms_ref)

    group = (query_ref, grad_ref, key_ref, value_ref, terms_ref, tile)
    accs = (key_acc, value_acc)
    low, corner, square = own_work(group, accs, scale, span_ids, kept_ref, probs_ref, heads)
    arrive(0)
    corner(order[0])
    arrive(1)
    if parts == 2:
        pl.when(low == order[0])(square)
        pl.when(low == order[1])(lambda: corner(order[1]))
    else:
        corner(order[1])
        square()


def last_kernel(heads, tile, scale, parts, span_ids, *refs):
    query_ref, grad_ref, terms_ref, both_ref = refs[:4]
    kept_ref, key_acc, value_acc, total_ref, probs_ref = refs[8:]
    if parts == 2:
        toks = both_ref.shape[0] // 2
        key_ref, value_ref = both_ref.at[pl.ds(0, toks)], both_ref.at[pl.ds(toks, toks)]
        group = (query_ref, grad_ref, key_ref, value_ref, terms_ref, tile)
        accs = (key_acc, value_acc)
        x = lax.axis_index("head")
        low, corner, square = own_work(group, accs, scale, span_ids, kept_ref, probs_ref, heads)
        pl.when(low == x)(square)
        pl.when(low != x)(lambda: corner(x))
    put_shares([total_ref], key_acc, value_acc, scale, 0, parts)


def far_kernel(heads, tile, scale, parts, step, span_ids, *refs):
    query_ref, grad_ref, terms_ref, key_ref, value_ref = refs[:5]
    own, refs = (refs[5:7], refs[7:]) if step == 1 else (None, refs[5:])
    kept_ref, outs, own_outs = refs[0], refs[1 : 1 + parts], refs[1 + parts : -3]
    key_acc, value_acc, probs_ref = refs[-3:]
    if own:
        put_shares(own_outs, *own, scale, 1)
    half = key_ref.shape[0] // 2
    rows = half * heads
    key_acc[...] = jnp.zeros_like(key_acc)
    value_acc[...] = jnp.zeros_like(value_acc)
    group = (query_ref, grad_ref, key_ref, value_ref, terms_ref, tile)
    halves = far_halves(span_ids, step)

    blocks = []
    for item in range(2):
        row_half, key_half = halves(item)
        row = pl.multiple_of(row_half * rows, rows)
        key = pl.multiple_of(key_half * half, half)
        blocks.append((row, key, half, kept_ref.at[item], probs_ref.at[item]))
    block_grads(group, (key_acc, value_acc), scale, rows, blocks)
    put_shares(outs, key_acc, value_acc, scale)


def join_kernel(*refs):
    this_ref, out_ref = refs[0], refs[-1]
    odd = lax.rem(lax.axis_index("ctx"), 2).astype(jnp.float32)
    more = sum(ref[...].astype(jnp.float32) for ref in refs[1:-1])
    out_ref[...] = (this_ref[...].astype(jnp.float32) + more * odd).astype(out_ref.dtype)


def total_kernel(parts, total_ref, *refs):
    ins, (key_out, value_out) = refs[:-2], refs[-2:]
    share = key_out.shape[0]
    even = 1.0 - lax.rem(lax.axis_index("ctx"), 2).astype(jnp.float32)
    for low, out in ((0, key_out), (share, value_out)):
        joined, landed = (
            sum(ref[low : low + share, :].astype(jnp.float32) for ref in some)
            for some in (ins[:parts], ins[parts:])
        )
        out[...] = (total_ref[low : low + share, :] + joined * even + landed).astype(out.dtype)


def query_kernel(heads, tile, scale, span_ids, both_ref, own_ref, *refs):
    far_refs, (out_ref, acc, turned) = refs[:-3], refs[-3:]
    toks = both_ref.shape[0] // 2
    half = toks // 2
    rows = half * heads
    per = tile // heads
    for index, key_ref in enumerate([both_ref] + list(far_refs[::2])):
        for low in range(0, toks, half):
            turned[index, :, low : low + half] = key_ref[low : low + half, :].T

    @pl.loop(0, 2)
    def _(index):
        key = pl.multiple_of(index * half, half)
        for p in range(half // per):
            row = pl.multiple_of(index * rows + p * tile, tile)
            length = (p + 1) * per
            acc[:, pl.ds(row, tile)] = dot(
                turned[0, :, pl.ds(key, length)], own_ref[pl.ds(key, length), pl.ds(row, tile)], NN
            )

    first, second = span_pair(span_ids, lax.axis_index("ctx"))
    low = jnp.where(first > second, 1, 0)
    key = pl.multiple_of(low * half, half)
    for p in range(rows // tile):
        row = pl.multiple_of((1 - low) * rows + p * tile, tile)
        acc[:, pl.ds(row, tile)] += dot(
            turned[0, :, pl.ds(key, half)], own_ref[pl.ds(key, half), pl.ds(row, tile)], NN
        )
    for step in range(1, STEPS):
        kept_ref = far_refs[2 * step - 1]
        halves = far_halves(span_ids, step)

        @pl.loop(0, 2)
        def _(item):
            row_half, key_half = halves(item)
            key = pl.multiple_of(key_half * half, half)
            for p in range(rows // tile):
                row = pl.multiple_of(row_half * rows + p * tile, tile)
                acc[:, pl.ds(row, tile)] += dot(
                    turned[step, :, pl.ds(key, half)],
                    kept_ref[item, :, p * tile : (p + 1) * tile],
                    NN,
                )

    for row in range(0, 2 * rows, tile):
        out_ref[row : row + tile, :] = (acc[:, row : row + tile] * scale).T.astype(out_ref.dtype)


VMEM = pl.BlockSpec(memory_space=pltpu.VMEM)
SMEM = pl.BlockSpec(memory_space=pltpu.SMEM)
HBM = pl.BlockSpec(memory_space=pltpu.HBM)
ANY = pl.BlockSpec(memory_space=pl.ANY)
MIB = 1024 * 1024


def call(kernel, ins, where, outs, scratch, blocks, limit, name, aliases=None):
    flops = blocks * 40 * 512 * 512 * 128
    return pl.pallas_call(
        kernel,
        out_shape=outs,
        in_specs=where,
        out_specs=[VMEM] * len(outs),
        scratch_shapes=scratch,
        input_output_aliases=aliases or {},
        compiler_params=pltpu.CompilerParams(vmem_limit_bytes=limit * MIB),
        name=name,
        cost_estimate=pl.CostEstimate(flops=int(flops), bytes_accessed=int(blocks * (1 << 20)), transcendentals=0),
    )(*ins)


def moved(block, back, away):
    holders, parts = lax.axis_size("ctx"), lax.axis_size("head")
    route = [
        (h * parts + x, ((h - back[h % 2]) % holders) * parts + (x + away) % parts)
        for h in range(holders)
        for x in range(parts)
    ]
    return lax.ppermute(block, ("ctx", "head"), route)


def local(queries, keys, values, outputs, out_grad, log_norm, span_ids):
    toks, heads, dim = queries.shape
    rows = toks * heads
    scale = dim ** (-0.5)
    parts = lax.axis_size("head")
    tile = 512
    q = queries.reshape(rows, dim)
    g = out_grad.reshape(rows, dim)
    o = outputs.reshape(rows, dim)
    share = 2 * toks // parts
    f32, bf16 = jnp.float32, jnp.bfloat16
    shape = jax.ShapeDtypeStruct
    grads = [shape((share, dim), bf16)] * parts
    accs = [pltpu.VMEM((toks, dim), f32)] * 2
    probs = pltpu.VMEM((toks // 2, rows // 2), bf16)

    key_1, value_1 = moved(keys, (-1, -1), 0), moved(values, (-1, -1), 0)
    inputs = tuple(
        pltpu.with_memory_space_constraint(a, pltpu.HBM)
        for a in (g, o, q, log_norm, keys, values, span_ids)
    )
    sums = [shape((toks, rows), bf16), shape((toks, dim), f32), shape((toks, dim), f32)]
    terms, both, kept, key_sum, value_sum = call(
        functools.partial(first_kernel, heads, tile, scale, parts),
        inputs,
        [HBM] * len(inputs),
        [shape((8, rows), f32), shape((2 * toks, dim), bf16)] + sums,
        [pltpu.VMEM(a.shape, a.dtype) for a in inputs[:4]]
        + [probs, pltpu.SMEM(span_ids.shape, span_ids.dtype), pltpu.SemaphoreType.DMA((4, 3))],
        1.625 * heads,
        20,
        "first",
    )
    key_2, value_2 = moved(key_1, (-1, -1), 0), moved(value_1, (-1, -1), 0)

    def far(step, key, value, *own):
        return call(
            functools.partial(far_kernel, heads, tile, scale, parts, step),
            (span_ids, q, g, terms, key, value, *own),
            [SMEM] + [VMEM] * (5 + len(own)),
            [shape((2, toks // 2, rows // 2), bf16)] + grads + (grads[1:] if own else []),
            accs + [pltpu.VMEM((2, toks // 2, rows // 2), bf16)],
            2 * heads,
            18,
            "far",
        )

    kept_1, *sent = far(1, key_1, value_1, key_sum, value_sum)
    joined = [moved(block, (-1, 1), away) for away, block in enumerate(sent[:parts])]
    landed = [moved(block, (0, 0), away + 1) for away, block in enumerate(sent[parts:])]
    kept_2, *sent = far(2, key_2, value_2)
    sent[:1] = call(
        join_kernel, (sent[0], *joined), [VMEM] * (1 + parts), grads[:1], [], 0.01, 4, "join"
    )
    landed += [moved(block, (2, 2), away) for away, block in enumerate(sent)]
    kept, _, _, total = call(
        functools.partial(last_kernel, heads, tile, scale, parts),
        (span_ids, q, g, terms, both, kept, key_sum, value_sum, sent[0]),
        [SMEM] + [VMEM] * 7 + [ANY],
        sums + [shape((share, dim), f32)],
        [probs],
        1.625 * heads,
        20,
        "last",
        {5: 0, 6: 1, 7: 2},
    )
    (query_grad,) = call(
        functools.partial(query_kernel, heads, tile, scale),
        (span_ids, both, kept, key_1, kept_1, key_2, kept_2),
        [SMEM] + [VMEM] * 6,
        [shape((rows, dim), bf16)],
        [pltpu.VMEM((dim, rows), f32), pltpu.VMEM((STEPS, dim, toks), bf16)],
        1.25 * heads,
        28,
        "queries",
    )
    key_grad, value_grad = call(
        functools.partial(total_kernel, parts),
        (total, *joined, *landed),
        [VMEM] * (1 + len(joined) + len(landed)),
        [shape((share // 2, dim), bf16)] * 2,
        [],
        0.01,
        8,
        "total",
    )
    return query_grad.reshape(toks, heads, dim), key_grad, value_grad


def solution(mesh):
    in_specs = (
        P("ctx", "head", None),
        P("ctx", None),
        P("ctx", None),
        P("ctx", "head", None),
        P("ctx", "head", None),
        P("head", "ctx"),
        P(),
    )
    out_specs = (P("ctx", "head", None), P(("ctx", "head"), None), P(("ctx", "head"), None))
    return jax.shard_map(local, mesh=mesh, in_specs=in_specs, out_specs=out_specs, check_vma=False)
```

```python
import functools
import math

import jax
import jax.numpy as jnp
from jax import lax
from jax.experimental import pallas as pl
from jax.experimental.pallas import tpu as pltpu
from jax.sharding import PartitionSpec as P

STEPS = 3
NT = (((1,), (1,)), ((), ()))
NN = (((1,), (0,)), ((), ()))
TN = (((0,), (0,)), ((), ()))


def dot(a, b, dims):
    return lax.dot_general(a, b, dims, preferred_element_type=jnp.float32)


def three_terms(x):
    high = x.astype(jnp.bfloat16)
    rest = x - high.astype(jnp.float32)
    mid = rest.astype(jnp.bfloat16)
    low = (rest - mid.astype(jnp.float32)).astype(jnp.bfloat16)
    return high, mid, low


def row_terms(heads, tile, span, refs, out):
    grad_ref, outputs_ref, norm_ref = refs
    rows = grad_ref.shape[0] // 2
    toks = tile // heads
    spread = (
        lax.broadcasted_iota(jnp.int32, (toks, tile), 1) // heads
        == lax.broadcasted_iota(jnp.int32, (toks, tile), 0)
    ).astype(jnp.bfloat16)
    mine = (
        lax.broadcasted_iota(jnp.int32, (heads, tile), 1) % heads
        == lax.broadcasted_iota(jnp.int32, (heads, tile), 0)
    )
    ones = jnp.ones((8, grad_ref.shape[1]), jnp.bfloat16)
    for index in range(rows // tile):
        tok = pl.multiple_of(span * (rows // heads) + index * toks, toks)
        row = pl.multiple_of(span * rows + index * tile, tile)
        norm = norm_ref[:, pl.ds(tok, toks)] * math.log2(math.e)
        wide = sum(dot(part, spread, NN) for part in three_terms(norm))
        out[0:1, pl.ds(row, tile)] = jnp.sum(jnp.where(mine, wide, 0.0), axis=0, keepdims=True)
        prod = grad_ref[pl.ds(row, tile), :].astype(jnp.float32) * outputs_ref[
            pl.ds(row, tile), :
        ].astype(jnp.float32)
        high = prod.astype(jnp.bfloat16)
        low = (prod - high.astype(jnp.float32)).astype(jnp.bfloat16)
        out[1:2, pl.ds(row, tile)] = (dot(ones, high, NT) + dot(ones, low, NT))[0:1]


def opened(group, row, key, length):
    query_ref, grad_ref, key_ref, value_ref, _, tile = group
    k = key_ref[pl.ds(key, length), :]
    v = value_ref[pl.ds(key, length), :]
    scores = dot(k, query_ref[pl.ds(row, tile), :], NT)
    return scores, dot(v, grad_ref[pl.ds(row, tile), :], NT)


def closed(group, scale, row, triangle, scores, dprob):
    terms_ref, tile = group[4:]
    norm = terms_ref[0:1, pl.ds(row, tile)]
    delta = terms_ref[1:2, pl.ds(row, tile)]
    prob = jnp.exp2(scores * (scale * math.log2(math.e)) - norm)
    if triangle is not None:
        edge = prob.shape[0] - triangle.shape[0]
        last = jnp.where(triangle, prob[edge:], 0.0)
        prob = last if edge == 0 else jnp.concatenate([prob[:edge], last], axis=0)
    return prob.astype(jnp.bfloat16), (prob * (dprob - delta)).astype(jnp.bfloat16)


def triangle_grads(group, accs, scale, row, key, half, triangle, kept_ref):
    query_ref, grad_ref, tile = group[0], group[1], group[-1]
    key_acc, value_acc = accs
    per = triangle.shape[0]
    tiles = [(pl.multiple_of(row + p * tile, tile), (p + 1) * per) for p in range(half // per)]
    ahead = opened(group, tiles[0][0], key, tiles[0][1])
    for index, (row, length) in enumerate(tiles):
        now = ahead
        if index + 1 < len(tiles):
            ahead = opened(group, tiles[index + 1][0], key, tiles[index + 1][1])
        prob, dscore = closed(group, scale, row, triangle, *now)
        kept_ref[pl.ds(key, length), pl.ds(row, tile)] = dscore
        value_acc[pl.ds(key, length), :] += dot(prob, grad_ref[pl.ds(row, tile), :], NN)
        key_acc[pl.ds(key, length), :] += dot(dscore, query_ref[pl.ds(row, tile), :], NN)


def block_grads(group, accs, scale, rows, blocks):
    query_ref, grad_ref, tile = group[0], group[1], group[-1]
    key_acc, value_acc = accs
    count = rows // tile
    tiles = [(block, p) for block in blocks for p in range(count)]

    def start(block, p):
        row, key, length = block[:3]
        return opened(group, pl.multiple_of(row + p * tile, tile), key, length)

    ahead = start(*tiles[0])
    for index, (block, p) in enumerate(tiles):
        now = ahead
        if index + 1 < len(tiles):
            ahead = start(*tiles[index + 1])
        row, _, length, kept, probs, place = block
        prob, dscore = closed(group, scale, pl.multiple_of(row + p * tile, tile), None, *now)
        probs[:, p * tile : (p + 1) * tile] = prob
        kept[:, p * tile : (p + 1) * tile] = dscore
        if p == count - 1:
            value_acc[pl.ds(place, length), :] += dot(probs[...], grad_ref[pl.ds(row, rows), :], NN)
            key_acc[pl.ds(place, length), :] += dot(kept[...], query_ref[pl.ds(row, rows), :], NN)


def span_pair(span_ids, holder):
    return span_ids[2 * holder], span_ids[2 * holder + 1]


def far_halves(span_ids, step):
    me, holders = lax.axis_index("ctx"), lax.axis_size("ctx")
    mine = span_pair(span_ids, me)
    theirs = span_pair(span_ids, lax.rem(me + holders - step, holders))
    high_only = jnp.minimum(*mine) < jnp.minimum(*theirs)
    our_high = jnp.where(mine[0] > mine[1], 0, 1)
    their_low = jnp.where(theirs[0] > theirs[1], 1, 0)
    return lambda item: (
        jnp.where(high_only, our_high, item),
        jnp.where(high_only, item, their_low),
    )


def put_shares(outs, key_acc, value_acc, scale, first=0, parts=None, more=None):
    parts = parts or len(outs) + first
    share = key_acc.shape[0] // parts
    x = lax.axis_index("head")
    for away, out in enumerate(outs, first):
        start = pl.multiple_of(lax.rem(x + away, parts) * share, share)
        for low, part in (
            (0, key_acc[pl.ds(start, share), :] * scale),
            (share, value_acc[pl.ds(start, share), :]),
        ):
            if more is not None:
                part = part + more(away, low, share)
            out[low : low + share, :] = part.astype(out.dtype)


def own_work(group, accs, scale, span_ids, kept_ref, probs_ref, heads):
    tile = group[-1]
    toks, rows = kept_ref.shape
    half, span_rows, per = toks // 2, rows // 2, tile // heads
    first, second = span_pair(span_ids, lax.axis_index("ctx"))
    low = jnp.where(first > second, 1, 0)
    triangle = lax.broadcasted_iota(jnp.int32, (per, tile), 0) <= (
        lax.broadcasted_iota(jnp.int32, (per, tile), 1) // heads
    )

    def corner(which):
        key = pl.multiple_of(which * half, half)
        row = pl.multiple_of(which * span_rows, span_rows)
        triangle_grads(group, accs, scale, row, key, half, triangle, kept_ref)

    def square():
        key = pl.multiple_of(low * half, half)
        row = pl.multiple_of((1 - low) * span_rows, span_rows)
        kept = kept_ref.at[pl.ds(key, half), pl.ds(row, span_rows)]
        block_grads(group, accs, scale, span_rows, [(row, key, half, kept, probs_ref, key)])

    return low, corner, square


def first_kernel(heads, tile, scale, parts, *refs):
    inputs, refs = refs[:7], refs[7:]
    terms_ref, both_ref, kept_ref, key_acc, value_acc = refs[:5]
    held, (probs_ref, span_ids, sems) = refs[5:-3], refs[-3:]
    grad_ref, outputs_ref, query_ref, norm_ref = held
    toks = both_ref.shape[0] // 2
    key_ref, value_ref = both_ref.at[pl.ds(0, toks)], both_ref.at[pl.ds(toks, toks)]
    rows = toks * heads // 2
    whole = [
        pltpu.make_async_copy(a, b, sems.at[i, 2])
        for i, (a, b) in enumerate(zip(inputs[3:], (norm_ref, key_ref, value_ref, span_ids)))
    ]

    def halves(slot, index):
        part = pl.ds(pl.multiple_of(index * rows, rows), rows)
        return [
            pltpu.make_async_copy(inputs[i].at[part], held[i].at[part], sems.at[i, slot])
            for i in range(3)
        ]

    x = lax.axis_index("head")
    order = (1 - x, x) if parts == 2 else (0, 1)
    for copy in whole + halves(0, order[0]) + halves(1, order[1]):
        copy.start()
    key_acc[...] = jnp.zeros_like(key_acc)
    value_acc[...] = jnp.zeros_like(value_acc)
    for copy in whole:
        copy.wait()

    def arrive(slot):
        for copy in halves(slot, order[slot]):
            copy.wait()
        row_terms(heads, tile, order[slot], (grad_ref, outputs_ref, norm_ref), terms_ref)

    group = (query_ref, grad_ref, key_ref, value_ref, terms_ref, tile)
    accs = (key_acc, value_acc)
    low, corner, square = own_work(group, accs, scale, span_ids, kept_ref, probs_ref, heads)
    arrive(0)
    corner(order[0])
    arrive(1)
    if parts == 2:
        pl.when(low == order[0])(square)
        pl.when(low == order[1])(lambda: corner(order[1]))
    else:
        corner(order[1])
        square()


def last_kernel(heads, tile, scale, parts, span_ids, *refs):
    query_ref, grad_ref, terms_ref, both_ref = refs[:4]
    kept_ref, key_acc, value_acc, total_ref, probs_ref = refs[8:]
    if parts == 2:
        toks = both_ref.shape[0] // 2
        key_ref, value_ref = both_ref.at[pl.ds(0, toks)], both_ref.at[pl.ds(toks, toks)]
        group = (query_ref, grad_ref, key_ref, value_ref, terms_ref, tile)
        accs = (key_acc, value_acc)
        x = lax.axis_index("head")
        low, corner, square = own_work(group, accs, scale, span_ids, kept_ref, probs_ref, heads)
        pl.when(low == x)(square)
        pl.when(low != x)(lambda: corner(x))
    put_shares([total_ref], key_acc, value_acc, scale, 0, parts)


def near_kernel(heads, tile, scale, parts, span_ids, *refs):
    query_ref, grad_ref, terms_ref, key_ref, value_ref, own_keys, own_values, _, kept_ref = refs[:9]
    outs, own_outs, (key_acc, value_acc, probs_ref) = refs[9 : 9 + parts], refs[9 + parts : -3], refs[-3:]
    put_shares(own_outs, own_keys, own_values, scale, 1)
    group = (query_ref, grad_ref, key_ref, value_ref, terms_ref, tile)
    far_work(group, (key_acc, value_acc), scale, span_ids, kept_ref, probs_ref, heads, 1, 0, 1)
    put_shares(outs, key_acc, value_acc, scale)


def pack_kernel(key_ref, value_ref, out_ref):
    toks = key_ref.shape[0]
    out_ref[0:toks, :] = key_ref[...]
    out_ref[toks : 2 * toks, :] = value_ref[...]


def far_kernel(heads, tile, scale, piece, pieces, span_ids, *refs):
    query_ref, grad_ref, terms_ref, both_ref, _ = refs[:5]
    parts = (len(refs) - 9) // 2
    swapped, kept_ref = refs[5 : 5 + parts], refs[5 + parts]
    outs, (key_acc, value_acc, probs_ref) = refs[6 + parts : -3], refs[-3:]
    toks = both_ref.shape[0] // 2
    key_ref, value_ref = both_ref.at[pl.ds(0, toks)], both_ref.at[pl.ds(toks, toks)]
    group = (query_ref, grad_ref, key_ref, value_ref, terms_ref, tile)
    far_work(
        group, (key_acc, value_acc), scale, span_ids, kept_ref, probs_ref, heads, 2, piece, pieces
    )
    odd = lax.rem(lax.axis_index("ctx"), 2).astype(jnp.float32)

    def more(away, low, share):
        start = low * pieces + piece * share
        return swapped[away][start : start + share, :].astype(jnp.float32) * odd

    put_shares(outs, key_acc, value_acc, scale, more=more)


def far_work(group, accs, scale, span_ids, kept_ref, probs_ref, heads, step, piece, pieces):
    key_acc, value_acc = accs
    key_acc[...] = jnp.zeros_like(key_acc)
    value_acc[...] = jnp.zeros_like(value_acc)
    half = group[2].shape[0] // 2
    rows, length = half * heads, half // pieces
    halves = far_halves(span_ids, step)
    blocks = []
    for item in range(2):
        row_half, key_half = halves(item)
        row = pl.multiple_of(row_half * rows, rows)
        key = pl.multiple_of(key_half * half + piece * length, length)
        place = pl.multiple_of(key_half * length, length)
        blocks.append((row, key, length, kept_ref.at[item], probs_ref.at[item], place))
    block_grads(group, accs, scale, rows, blocks)


def join_kernel(*refs):
    count = len(refs) // 3
    even = 1.0 - lax.rem(lax.axis_index("ctx"), 2).astype(jnp.float32)
    for swapped, this, out in zip(refs, refs[count:], refs[2 * count :]):
        more = swapped[...].astype(jnp.float32) * even
        out[...] = (this[...].astype(jnp.float32) + more).astype(out.dtype)


def total_kernel(pieces, total_ref, swapped_ref, *refs):
    ins, (key_out, value_out) = refs[:-2], refs[-2:]
    share = key_out.shape[0]
    even = 1.0 - lax.rem(lax.axis_index("ctx"), 2).astype(jnp.float32)
    length = share // pieces
    whole = [ref for ref in ins if ref.shape[0] == 2 * share]
    cut = [ref for ref in ins if ref.shape[0] != 2 * share]
    for which, out in enumerate((key_out, value_out)):
        for piece in range(pieces):
            here = piece * length
            low = which * share + here
            part = total_ref[low : low + length, :]
            part = part + swapped_ref[low : low + length, :].astype(jnp.float32) * even
            for ref in whole:
                part = part + ref[low : low + length, :].astype(jnp.float32)
            for ref in cut[piece * len(cut) // pieces : (piece + 1) * len(cut) // pieces]:
                part = part + ref[which * length : (which + 1) * length, :].astype(jnp.float32)
            out[here : here + length, :] = part.astype(out.dtype)


def query_kernel(heads, tile, scale, pieces, span_ids, both_ref, own_ref, *refs):
    (key_1, both_2), kept_refs, (out_ref, acc, turned) = refs[:2], refs[2:-3], refs[-3:]
    toks = both_ref.shape[0] // 2
    half = toks // 2
    rows = half * heads
    per = tile // heads
    for index, key_ref in enumerate((both_ref, key_1, both_2)):
        for low in range(0, toks, half):
            turned[index, :, low : low + half] = key_ref[low : low + half, :].T

    @pl.loop(0, 2)
    def _(index):
        key = pl.multiple_of(index * half, half)
        for p in range(half // per):
            row = pl.multiple_of(index * rows + p * tile, tile)
            length = (p + 1) * per
            acc[:, pl.ds(row, tile)] = dot(
                turned[0, :, pl.ds(key, length)], own_ref[pl.ds(key, length), pl.ds(row, tile)], NN
            )

    first, second = span_pair(span_ids, lax.axis_index("ctx"))
    low = jnp.where(first > second, 1, 0)
    key = pl.multiple_of(low * half, half)
    for p in range(rows // tile):
        row = pl.multiple_of((1 - low) * rows + p * tile, tile)
        acc[:, pl.ds(row, tile)] += dot(
            turned[0, :, pl.ds(key, half)], own_ref[pl.ds(key, half), pl.ds(row, tile)], NN
        )
    for index, kept_ref in enumerate(kept_refs):
        step, piece = (1, 0) if index == 0 else (2, index - 1)
        length = kept_ref.shape[1]
        halves = far_halves(span_ids, step)

        @pl.loop(0, 2)
        def _(item):
            row_half, key_half = halves(item)
            key = pl.multiple_of(key_half * half + piece * length, length)
            for p in range(rows // tile):
                row = pl.multiple_of(row_half * rows + p * tile, tile)
                acc[:, pl.ds(row, tile)] += dot(
                    turned[step, :, pl.ds(key, length)],
                    kept_ref[item, :, p * tile : (p + 1) * tile],
                    NN,
                )

    for row in range(0, 2 * rows, tile):
        out_ref[row : row + tile, :] = (acc[:, row : row + tile] * scale).T.astype(out_ref.dtype)


VMEM = pl.BlockSpec(memory_space=pltpu.VMEM)
SMEM = pl.BlockSpec(memory_space=pltpu.SMEM)
HBM = pl.BlockSpec(memory_space=pltpu.HBM)
ANY = pl.BlockSpec(memory_space=pl.ANY)
MIB = 1024 * 1024


def call(kernel, ins, where, outs, scratch, blocks, limit, name, aliases=None):
    flops = blocks * 40 * 512 * 512 * 128
    return pl.pallas_call(
        kernel,
        out_shape=outs,
        in_specs=where,
        out_specs=[VMEM] * len(outs),
        scratch_shapes=scratch,
        input_output_aliases=aliases or {},
        compiler_params=pltpu.CompilerParams(vmem_limit_bytes=limit * MIB),
        name=name,
        cost_estimate=pl.CostEstimate(flops=int(flops), bytes_accessed=int(blocks * (1 << 20)), transcendentals=0),
    )(*ins)


def moved(block, back, away):
    holders, parts = lax.axis_size("ctx"), lax.axis_size("head")
    route = [
        (h * parts + x, ((h - back[h % 2]) % holders) * parts + (x + away) % parts)
        for h in range(holders)
        for x in range(parts)
    ]
    return lax.ppermute(block, ("ctx", "head"), route)


def local(queries, keys, values, outputs, out_grad, log_norm, span_ids):
    toks, heads, dim = queries.shape
    rows = toks * heads
    scale = dim ** (-0.5)
    parts = lax.axis_size("head")
    tile = 512
    q = queries.reshape(rows, dim)
    g = out_grad.reshape(rows, dim)
    o = outputs.reshape(rows, dim)
    share = 2 * toks // parts
    f32, bf16 = jnp.float32, jnp.bfloat16
    shape = jax.ShapeDtypeStruct
    grads = [shape((share, dim), bf16)] * parts
    accs = [pltpu.VMEM((toks, dim), f32)] * 2
    probs = pltpu.VMEM((toks // 2, rows // 2), bf16)

    key_1, value_1 = moved(keys, (-1, -1), 0), moved(values, (-1, -1), 0)
    inputs = tuple(
        pltpu.with_memory_space_constraint(a, pltpu.HBM)
        for a in (g, o, q, log_norm, keys, values, span_ids)
    )
    sums = [shape((toks, rows), bf16), shape((toks, dim), f32), shape((toks, dim), f32)]
    terms, both, kept, key_sum, value_sum = call(
        functools.partial(first_kernel, heads, tile, scale, parts),
        inputs,
        [HBM] * len(inputs),
        [shape((8, rows), f32), shape((2 * toks, dim), bf16)] + sums,
        [pltpu.VMEM(a.shape, a.dtype) for a in inputs[:4]]
        + [probs, pltpu.SMEM(span_ids.shape, span_ids.dtype), pltpu.SemaphoreType.DMA((4, 3))],
        1.625 * heads,
        20,
        "first",
    )
    (both_1,) = call(
        pack_kernel, (key_1, value_1), [VMEM] * 2, [shape((2 * toks, dim), bf16)], [], 0.01, 4, "pack"
    )
    both_2 = moved(both_1, (-1, -1), 0)

    block = (toks // 2, rows // 2)
    kept_1, *sent = call(
        functools.partial(near_kernel, heads, tile, scale, parts),
        (span_ids, q, g, terms, key_1, value_1, key_sum, value_sum, both_1),
        [SMEM] + [VMEM] * 7 + [ANY],
        [shape((2,) + block, bf16)] + grads + grads[1:],
        accs + [pltpu.VMEM((2,) + block, bf16)],
        2 * heads,
        18,
        "near",
    )
    swapped = [moved(part, (-1, 1), 0) for part in sent[:parts]]
    sent = call(
        join_kernel,
        (*swapped[1:], *sent[parts:]),
        [VMEM] * (2 * parts - 2),
        grads[1:],
        [],
        0.01,
        4,
        "join",
    )
    whole = [moved(part, (0, 0), away) for away, part in enumerate(sent, 1)]
    pieces = 2 if parts == 2 else 1
    small = (2, toks // 2 // pieces, rows // 2)
    kept_2, cut, last = [], [], sent[0]
    for piece in range(pieces):
        kept_piece, *sent = call(
            functools.partial(far_kernel, heads, tile, scale, piece, pieces),
            (span_ids, q, g, terms, both_2, last, *swapped),
            [SMEM] + [VMEM] * 4 + [ANY] + [VMEM] * parts,
            [shape(small, bf16)] + [shape((share // pieces, dim), bf16)] * parts,
            [pltpu.VMEM((toks // pieces, dim), f32)] * 2 + [pltpu.VMEM(small, bf16)],
            2 * heads / pieces,
            18,
            "far",
        )
        kept_2.append(kept_piece)
        cut += [moved(part, (2, 2), away) for away, part in enumerate(sent)]
        last = sent[0]
    kept, _, _, total = call(
        functools.partial(last_kernel, heads, tile, scale, parts),
        (span_ids, q, g, terms, both, kept, key_sum, value_sum, last),
        [SMEM] + [VMEM] * 7 + [ANY],
        sums + [shape((share, dim), f32)],
        [probs],
        1.625 * heads,
        20,
        "last",
        {5: 0, 6: 1, 7: 2},
    )
    (query_grad,) = call(
        functools.partial(query_kernel, heads, tile, scale, pieces),
        (span_ids, both, kept, key_1, both_2, kept_1, *kept_2),
        [SMEM] + [VMEM] * (5 + pieces),
        [shape((rows, dim), bf16)],
        [pltpu.VMEM((dim, rows), f32), pltpu.VMEM((STEPS, dim, toks), bf16)],
        1.25 * heads,
        28,
        "queries",
    )
    key_grad, value_grad = call(
        functools.partial(total_kernel, pieces),
        (total, swapped[0], *whole, *cut),
        [VMEM] * (2 + len(whole) + len(cut)),
        [shape((share // 2, dim), bf16)] * 2,
        [],
        0.01,
        8,
        "total",
    )
    return query_grad.reshape(toks, heads, dim), key_grad, value_grad


def solution(mesh):
    in_specs = (
        P("ctx", "head", None),
        P("ctx", None),
        P("ctx", None),
        P("ctx", "head", None),
        P("ctx", "head", None),
        P("head", "ctx"),
        P(),
    )
    out_specs = (P("ctx", "head", None), P(("ctx", "head"), None), P(("ctx", "head"), None))
    return jax.shard_map(local, mesh=mesh, in_specs=in_specs, out_specs=out_specs, check_vma=False)
```

```python
import functools
import math

import jax
import jax.numpy as jnp
from jax import lax
from jax.experimental import pallas as pl
from jax.experimental.pallas import tpu as pltpu
from jax.sharding import PartitionSpec as P

STEPS = 3
NT = (((1,), (1,)), ((), ()))
NN = (((1,), (0,)), ((), ()))
TN = (((0,), (0,)), ((), ()))


def dot(a, b, dims):
    return lax.dot_general(a, b, dims, preferred_element_type=jnp.float32)


def three_terms(x):
    high = x.astype(jnp.bfloat16)
    rest = x - high.astype(jnp.float32)
    mid = rest.astype(jnp.bfloat16)
    low = (rest - mid.astype(jnp.float32)).astype(jnp.bfloat16)
    return high, mid, low


def row_terms(heads, tile, span, refs, out):
    grad_ref, outputs_ref, norm_ref = refs
    rows = grad_ref.shape[0] // 2
    toks = tile // heads
    spread = (
        lax.broadcasted_iota(jnp.int32, (toks, tile), 1) // heads
        == lax.broadcasted_iota(jnp.int32, (toks, tile), 0)
    ).astype(jnp.bfloat16)
    mine = (
        lax.broadcasted_iota(jnp.int32, (heads, tile), 1) % heads
        == lax.broadcasted_iota(jnp.int32, (heads, tile), 0)
    )
    ones = jnp.ones((8, grad_ref.shape[1]), jnp.bfloat16)
    for index in range(rows // tile):
        tok = pl.multiple_of(span * (rows // heads) + index * toks, toks)
        row = pl.multiple_of(span * rows + index * tile, tile)
        norm = norm_ref[:, pl.ds(tok, toks)] * math.log2(math.e)
        wide = sum(dot(part, spread, NN) for part in three_terms(norm))
        out[0:1, pl.ds(row, tile)] = jnp.sum(jnp.where(mine, wide, 0.0), axis=0, keepdims=True)
        prod = grad_ref[pl.ds(row, tile), :].astype(jnp.float32) * outputs_ref[
            pl.ds(row, tile), :
        ].astype(jnp.float32)
        high = prod.astype(jnp.bfloat16)
        low = (prod - high.astype(jnp.float32)).astype(jnp.bfloat16)
        out[1:2, pl.ds(row, tile)] = (dot(ones, high, NT) + dot(ones, low, NT))[0:1]


def opened(group, row, key, length):
    query_ref, grad_ref, key_ref, value_ref, _, tile = group
    k = key_ref[pl.ds(key, length), :]
    v = value_ref[pl.ds(key, length), :]
    scores = dot(k, query_ref[pl.ds(row, tile), :], NT)
    return scores, dot(v, grad_ref[pl.ds(row, tile), :], NT)


def closed(group, scale, row, triangle, scores, dprob):
    terms_ref, tile = group[4:]
    norm = terms_ref[0:1, pl.ds(row, tile)]
    delta = terms_ref[1:2, pl.ds(row, tile)]
    prob = jnp.exp2(scores * (scale * math.log2(math.e)) - norm)
    if triangle is not None:
        edge = prob.shape[0] - triangle.shape[0]
        last = jnp.where(triangle, prob[edge:], 0.0)
        prob = last if edge == 0 else jnp.concatenate([prob[:edge], last], axis=0)
    return prob.astype(jnp.bfloat16), (prob * (dprob - delta)).astype(jnp.bfloat16)


def triangle_grads(group, accs, scale, row, key, half, triangle, kept_ref):
    query_ref, grad_ref, tile = group[0], group[1], group[-1]
    key_acc, value_acc = accs
    per = triangle.shape[0]
    tiles = [(pl.multiple_of(row + p * tile, tile), (p + 1) * per) for p in range(half // per)]
    ahead = opened(group, tiles[0][0], key, tiles[0][1])
    for index, (row, length) in enumerate(tiles):
        now = ahead
        if index + 1 < len(tiles):
            ahead = opened(group, tiles[index + 1][0], key, tiles[index + 1][1])
        prob, dscore = closed(group, scale, row, triangle, *now)
        kept_ref[pl.ds(key, length), pl.ds(row, tile)] = dscore
        value_acc[pl.ds(key, length), :] += dot(prob, grad_ref[pl.ds(row, tile), :], NN)
        key_acc[pl.ds(key, length), :] += dot(dscore, query_ref[pl.ds(row, tile), :], NN)


def block_grads(group, accs, scale, rows, blocks):
    query_ref, grad_ref, tile = group[0], group[1], group[-1]
    key_acc, value_acc = accs
    count = rows // tile
    tiles = [(block, p) for block in blocks for p in range(count)]

    def start(block, p):
        row, key, length = block[:3]
        return opened(group, pl.multiple_of(row + p * tile, tile), key, length)

    ahead = start(*tiles[0])
    for index, (block, p) in enumerate(tiles):
        now = ahead
        if index + 1 < len(tiles):
            ahead = start(*tiles[index + 1])
        row, _, length, kept, probs, place = block
        prob, dscore = closed(group, scale, pl.multiple_of(row + p * tile, tile), None, *now)
        probs[:, p * tile : (p + 1) * tile] = prob
        kept[:, p * tile : (p + 1) * tile] = dscore
        if p == count - 1:
            value_acc[pl.ds(place, length), :] += dot(probs[...], grad_ref[pl.ds(row, rows), :], NN)
            key_acc[pl.ds(place, length), :] += dot(kept[...], query_ref[pl.ds(row, rows), :], NN)


def span_pair(span_ids, holder):
    return span_ids[2 * holder], span_ids[2 * holder + 1]


def far_halves(span_ids, step):
    me, holders = lax.axis_index("ctx"), lax.axis_size("ctx")
    mine = span_pair(span_ids, me)
    theirs = span_pair(span_ids, lax.rem(me + holders - step, holders))
    high_only = jnp.minimum(*mine) < jnp.minimum(*theirs)
    our_high = jnp.where(mine[0] > mine[1], 0, 1)
    their_low = jnp.where(theirs[0] > theirs[1], 1, 0)
    return lambda item: (
        jnp.where(high_only, our_high, item),
        jnp.where(high_only, item, their_low),
    )


def put_shares(outs, key_acc, value_acc, scale, first=0, parts=None, more=None):
    parts = parts or len(outs) + first
    share = key_acc.shape[0] // parts
    x = lax.axis_index("head")
    for away, out in enumerate(outs, first):
        start = pl.multiple_of(lax.rem(x + away, parts) * share, share)
        for low, part in (
            (0, key_acc[pl.ds(start, share), :] * scale),
            (share, value_acc[pl.ds(start, share), :]),
        ):
            if more is not None:
                part = part + more(away, low, share)
            out[low : low + share, :] = part.astype(out.dtype)


def own_work(group, accs, scale, span_ids, kept_ref, probs_ref, heads):
    tile = group[-1]
    toks, rows = kept_ref.shape
    half, span_rows, per = toks // 2, rows // 2, tile // heads
    first, second = span_pair(span_ids, lax.axis_index("ctx"))
    low = jnp.where(first > second, 1, 0)
    triangle = lax.broadcasted_iota(jnp.int32, (per, tile), 0) <= (
        lax.broadcasted_iota(jnp.int32, (per, tile), 1) // heads
    )

    def corner(which):
        key = pl.multiple_of(which * half, half)
        row = pl.multiple_of(which * span_rows, span_rows)
        triangle_grads(group, accs, scale, row, key, half, triangle, kept_ref)

    def square():
        key = pl.multiple_of(low * half, half)
        row = pl.multiple_of((1 - low) * span_rows, span_rows)
        kept = kept_ref.at[pl.ds(key, half), pl.ds(row, span_rows)]
        block_grads(group, accs, scale, span_rows, [(row, key, half, kept, probs_ref, key)])

    return low, corner, square


def first_kernel(heads, tile, scale, parts, *refs):
    inputs, refs = refs[:7], refs[7:]
    terms_ref, both_ref, kept_ref, key_acc, value_acc = refs[:5]
    held, (probs_ref, span_ids, sems) = refs[5:-3], refs[-3:]
    grad_ref, outputs_ref, query_ref, norm_ref = held
    toks = both_ref.shape[0] // 2
    key_ref, value_ref = both_ref.at[pl.ds(0, toks)], both_ref.at[pl.ds(toks, toks)]
    rows = toks * heads // 2
    whole = [
        pltpu.make_async_copy(a, b, sems.at[i, 2])
        for i, (a, b) in enumerate(zip(inputs[3:], (norm_ref, key_ref, value_ref, span_ids)))
    ]

    def halves(slot, index):
        part = pl.ds(pl.multiple_of(index * rows, rows), rows)
        return [
            pltpu.make_async_copy(inputs[i].at[part], held[i].at[part], sems.at[i, slot])
            for i in range(3)
        ]

    x = lax.axis_index("head")
    order = (1 - x, x) if parts == 2 else (0, 1)
    for copy in whole + halves(0, order[0]) + halves(1, order[1]):
        copy.start()
    key_acc[...] = jnp.zeros_like(key_acc)
    value_acc[...] = jnp.zeros_like(value_acc)
    for copy in whole:
        copy.wait()

    def arrive(slot):
        for copy in halves(slot, order[slot]):
            copy.wait()
        row_terms(heads, tile, order[slot], (grad_ref, outputs_ref, norm_ref), terms_ref)

    group = (query_ref, grad_ref, key_ref, value_ref, terms_ref, tile)
    accs = (key_acc, value_acc)
    low, corner, square = own_work(group, accs, scale, span_ids, kept_ref, probs_ref, heads)
    arrive(0)
    corner(order[0])
    arrive(1)
    if parts == 2:
        pl.when(low == order[0])(square)
        pl.when(low == order[1])(lambda: corner(order[1]))
    else:
        corner(order[1])
        square()


def last_kernel(heads, tile, scale, parts, span_ids, *refs):
    query_ref, grad_ref, terms_ref, both_ref = refs[:4]
    kept_ref, key_acc, value_acc, total_ref, probs_ref = refs[8:]
    if parts == 2:
        toks = both_ref.shape[0] // 2
        key_ref, value_ref = both_ref.at[pl.ds(0, toks)], both_ref.at[pl.ds(toks, toks)]
        group = (query_ref, grad_ref, key_ref, value_ref, terms_ref, tile)
        accs = (key_acc, value_acc)
        x = lax.axis_index("head")
        low, corner, square = own_work(group, accs, scale, span_ids, kept_ref, probs_ref, heads)
        pl.when(low == x)(square)
        pl.when(low != x)(lambda: corner(x))
    put_shares([total_ref], key_acc, value_acc, scale, 0, parts)


def near_kernel(heads, tile, scale, parts, span_ids, *refs):
    query_ref, grad_ref, terms_ref, key_ref, value_ref, own_keys, own_values, _, kept_ref = refs[:9]
    outs, own_outs, (key_acc, value_acc, probs_ref) = refs[9 : 9 + parts], refs[9 + parts : -3], refs[-3:]
    put_shares(own_outs, own_keys, own_values, scale, 1)
    group = (query_ref, grad_ref, key_ref, value_ref, terms_ref, tile)
    far_work(group, (key_acc, value_acc), scale, span_ids, kept_ref, probs_ref, heads, 1, 0, 1)
    put_shares(outs, key_acc, value_acc, scale)


def pack_kernel(key_ref, value_ref, out_ref):
    toks = key_ref.shape[0]
    out_ref[0:toks, :] = key_ref[...]
    out_ref[toks : 2 * toks, :] = value_ref[...]


def far_kernel(heads, tile, scale, piece, pieces, span_ids, *refs):
    query_ref, grad_ref, terms_ref, both_ref, _ = refs[:5]
    parts = (len(refs) - 9) // 2
    swapped, kept_ref = refs[5 : 5 + parts], refs[5 + parts]
    outs, (key_acc, value_acc, probs_ref) = refs[6 + parts : -3], refs[-3:]
    toks = both_ref.shape[0] // 2
    key_ref, value_ref = both_ref.at[pl.ds(0, toks)], both_ref.at[pl.ds(toks, toks)]
    group = (query_ref, grad_ref, key_ref, value_ref, terms_ref, tile)
    far_work(
        group, (key_acc, value_acc), scale, span_ids, kept_ref, probs_ref, heads, 2, piece, pieces
    )
    odd = lax.rem(lax.axis_index("ctx"), 2).astype(jnp.float32)

    def more(away, low, share):
        start = low * pieces + piece * share
        return swapped[away][start : start + share, :].astype(jnp.float32) * odd

    put_shares(outs, key_acc, value_acc, scale, more=more)


def far_work(group, accs, scale, span_ids, kept_ref, probs_ref, heads, step, piece, pieces):
    key_acc, value_acc = accs
    key_acc[...] = jnp.zeros_like(key_acc)
    value_acc[...] = jnp.zeros_like(value_acc)
    half = group[2].shape[0] // 2
    rows, length = half * heads, half // pieces
    halves = far_halves(span_ids, step)
    blocks = []
    for item in range(2):
        row_half, key_half = halves(item)
        row = pl.multiple_of(row_half * rows, rows)
        key = pl.multiple_of(key_half * half + piece * length, length)
        place = pl.multiple_of(key_half * length, length)
        blocks.append((row, key, length, kept_ref.at[item], probs_ref.at[item], place))
    block_grads(group, accs, scale, rows, blocks)


def join_kernel(*refs):
    count = len(refs) // 3
    even = 1.0 - lax.rem(lax.axis_index("ctx"), 2).astype(jnp.float32)
    for swapped, this, out in zip(refs, refs[count:], refs[2 * count :]):
        more = swapped[...].astype(jnp.float32) * even
        out[...] = (this[...].astype(jnp.float32) + more).astype(out.dtype)


def total_kernel(pieces, total_ref, swapped_ref, *refs):
    ins, (key_out, value_out) = refs[:-2], refs[-2:]
    share = key_out.shape[0]
    even = 1.0 - lax.rem(lax.axis_index("ctx"), 2).astype(jnp.float32)
    length = share // pieces
    whole = [ref for ref in ins if ref.shape[0] == 2 * share]
    cut = [ref for ref in ins if ref.shape[0] != 2 * share]
    for which, out in enumerate((key_out, value_out)):
        for piece in range(pieces):
            here = piece * length
            low = which * share + here
            part = total_ref[low : low + length, :]
            part = part + swapped_ref[low : low + length, :].astype(jnp.float32) * even
            for ref in whole:
                part = part + ref[low : low + length, :].astype(jnp.float32)
            for ref in cut[piece * len(cut) // pieces : (piece + 1) * len(cut) // pieces]:
                part = part + ref[which * length : (which + 1) * length, :].astype(jnp.float32)
            out[here : here + length, :] = part.astype(out.dtype)


def query_kernel(heads, tile, scale, pieces, span_ids, both_ref, own_ref, *refs):
    (key_1, both_2), kept_refs, (out_ref, acc, turned) = refs[:2], refs[2:-3], refs[-3:]
    toks = both_ref.shape[0] // 2
    half = toks // 2
    rows = half * heads
    per = tile // heads
    for index, key_ref in enumerate((both_ref, key_1, both_2)):
        for low in range(0, toks, half):
            turned[index, :, low : low + half] = key_ref[low : low + half, :].T

    @pl.loop(0, 2)
    def _(index):
        key = pl.multiple_of(index * half, half)
        for p in range(half // per):
            row = pl.multiple_of(index * rows + p * tile, tile)
            length = (p + 1) * per
            acc[:, pl.ds(row, tile)] = dot(
                turned[0, :, pl.ds(key, length)], own_ref[pl.ds(key, length), pl.ds(row, tile)], NN
            )

    first, second = span_pair(span_ids, lax.axis_index("ctx"))
    low = jnp.where(first > second, 1, 0)
    key = pl.multiple_of(low * half, half)
    for p in range(rows // tile):
        row = pl.multiple_of((1 - low) * rows + p * tile, tile)
        acc[:, pl.ds(row, tile)] += dot(
            turned[0, :, pl.ds(key, half)], own_ref[pl.ds(key, half), pl.ds(row, tile)], NN
        )
    for index, kept_ref in enumerate(kept_refs):
        step, piece = (1, 0) if index == 0 else (2, index - 1)
        length = kept_ref.shape[1]
        halves = far_halves(span_ids, step)

        @pl.loop(0, 2)
        def _(item):
            row_half, key_half = halves(item)
            key = pl.multiple_of(key_half * half + piece * length, length)
            for p in range(rows // tile):
                row = pl.multiple_of(row_half * rows + p * tile, tile)
                acc[:, pl.ds(row, tile)] += dot(
                    turned[step, :, pl.ds(key, length)],
                    kept_ref[item, :, p * tile : (p + 1) * tile],
                    NN,
                )

    for row in range(0, 2 * rows, tile):
        out_ref[row : row + tile, :] = (acc[:, row : row + tile] * scale).T.astype(out_ref.dtype)


VMEM = pl.BlockSpec(memory_space=pltpu.VMEM)
SMEM = pl.BlockSpec(memory_space=pltpu.SMEM)
HBM = pl.BlockSpec(memory_space=pltpu.HBM)
ANY = pl.BlockSpec(memory_space=pl.ANY)
MIB = 1024 * 1024


def call(kernel, ins, where, outs, scratch, blocks, limit, name, aliases=None):
    flops = blocks * 40 * 512 * 512 * 128
    return pl.pallas_call(
        kernel,
        out_shape=outs,
        in_specs=where,
        out_specs=[VMEM] * len(outs),
        scratch_shapes=scratch,
        input_output_aliases=aliases or {},
        compiler_params=pltpu.CompilerParams(vmem_limit_bytes=limit * MIB),
        name=name,
        cost_estimate=pl.CostEstimate(flops=int(flops), bytes_accessed=int(blocks * (1 << 20)), transcendentals=0),
    )(*ins)


def moved(block, back, away):
    holders, parts = lax.axis_size("ctx"), lax.axis_size("head")
    route = [
        (h * parts + x, ((h - back[h % 2]) % holders) * parts + (x + away) % parts)
        for h in range(holders)
        for x in range(parts)
    ]
    return lax.ppermute(block, ("ctx", "head"), route)


def local(queries, keys, values, outputs, out_grad, log_norm, span_ids):
    toks, heads, dim = queries.shape
    rows = toks * heads
    scale = dim ** (-0.5)
    parts = lax.axis_size("head")
    tile = 512
    q = queries.reshape(rows, dim)
    g = out_grad.reshape(rows, dim)
    o = outputs.reshape(rows, dim)
    share = 2 * toks // parts
    f32, bf16 = jnp.float32, jnp.bfloat16
    shape = jax.ShapeDtypeStruct
    grads = [shape((share, dim), bf16)] * parts
    accs = [pltpu.VMEM((toks, dim), f32)] * 2
    probs = pltpu.VMEM((toks // 2, rows // 2), bf16)

    key_1, value_1 = moved(keys, (-1, -1), 0), moved(values, (-1, -1), 0)
    inputs = tuple(
        pltpu.with_memory_space_constraint(a, pltpu.HBM)
        for a in (g, o, q, log_norm, keys, values, span_ids)
    )
    sums = [shape((toks, rows), bf16), shape((toks, dim), f32), shape((toks, dim), f32)]
    terms, both, kept, key_sum, value_sum = call(
        functools.partial(first_kernel, heads, tile, scale, parts),
        inputs,
        [HBM] * len(inputs),
        [shape((8, rows), f32), shape((2 * toks, dim), bf16)] + sums,
        [pltpu.VMEM(a.shape, a.dtype) for a in inputs[:4]]
        + [probs, pltpu.SMEM(span_ids.shape, span_ids.dtype), pltpu.SemaphoreType.DMA((4, 3))],
        1.625 * heads,
        20,
        "first",
    )
    (both_1,) = call(
        pack_kernel, (key_1, value_1), [VMEM] * 2, [shape((2 * toks, dim), bf16)], [], 0.01, 4, "pack"
    )
    both_2 = moved(both_1, (-1, -1), 0)

    block = (toks // 2, rows // 2)
    kept_1, *sent = call(
        functools.partial(near_kernel, heads, tile, scale, parts),
        (span_ids, q, g, terms, key_1, value_1, key_sum, value_sum, both_1),
        [SMEM] + [VMEM] * 7 + [ANY],
        [shape((2,) + block, bf16)] + grads + grads[1:],
        accs + [pltpu.VMEM((2,) + block, bf16)],
        2 * heads,
        18,
        "near",
    )
    swapped = [moved(part, (-1, 1), 0) for part in sent[:parts]]
    sent = call(
        join_kernel,
        (*swapped[1:], *sent[parts:]),
        [VMEM] * (2 * parts - 2),
        grads[1:],
        [],
        0.01,
        4,
        "join",
    )
    whole = [moved(part, (0, 0), away) for away, part in enumerate(sent, 1)]
    pieces = 1
    small = (2, toks // 2 // pieces, rows // 2)
    kept_2, cut, last = [], [], sent[0]
    for piece in range(pieces):
        kept_piece, *sent = call(
            functools.partial(far_kernel, heads, tile, scale, piece, pieces),
            (span_ids, q, g, terms, both_2, last, *swapped),
            [SMEM] + [VMEM] * 4 + [ANY] + [VMEM] * parts,
            [shape(small, bf16)] + [shape((share // pieces, dim), bf16)] * parts,
            [pltpu.VMEM((toks // pieces, dim), f32)] * 2 + [pltpu.VMEM(small, bf16)],
            2 * heads / pieces,
            18,
            "far",
        )
        kept_2.append(kept_piece)
        cut += [moved(part, (2, 2), away) for away, part in enumerate(sent)]
        last = sent[0]
    kept, _, _, total = call(
        functools.partial(last_kernel, heads, tile, scale, parts),
        (span_ids, q, g, terms, both, kept, key_sum, value_sum, last),
        [SMEM] + [VMEM] * 7 + [ANY],
        sums + [shape((share, dim), f32)],
        [probs],
        1.625 * heads,
        20,
        "last",
        {5: 0, 6: 1, 7: 2},
    )
    (query_grad,) = call(
        functools.partial(query_kernel, heads, tile, scale, pieces),
        (span_ids, both, kept, key_1, both_2, kept_1, *kept_2),
        [SMEM] + [VMEM] * (5 + pieces),
        [shape((rows, dim), bf16)],
        [pltpu.VMEM((dim, rows), f32), pltpu.VMEM((STEPS, dim, toks), bf16)],
        1.25 * heads,
        28,
        "queries",
    )
    key_grad, value_grad = call(
        functools.partial(total_kernel, pieces),
        (total, swapped[0], *whole, *cut),
        [VMEM] * (2 + len(whole) + len(cut)),
        [shape((share // 2, dim), bf16)] * 2,
        [],
        0.01,
        8,
        "total",
    )
    return query_grad.reshape(toks, heads, dim), key_grad, value_grad


def solution(mesh):
    in_specs = (
        P("ctx", "head", None),
        P("ctx", None),
        P("ctx", None),
        P("ctx", "head", None),
        P("ctx", "head", None),
        P("head", "ctx"),
        P(),
    )
    out_specs = (P("ctx", "head", None), P(("ctx", "head"), None), P(("ctx", "head"), None))
    return jax.shard_map(local, mesh=mesh, in_specs=in_specs, out_specs=out_specs, check_vma=False)
```

```python
import functools
import math

import jax
import jax.numpy as jnp
from jax import lax
from jax.experimental import pallas as pl
from jax.experimental.pallas import tpu as pltpu
from jax.sharding import PartitionSpec as P

STEPS = 3
NT = (((1,), (1,)), ((), ()))
NN = (((1,), (0,)), ((), ()))
TN = (((0,), (0,)), ((), ()))


def dot(a, b, dims):
    return lax.dot_general(a, b, dims, preferred_element_type=jnp.float32)


def three_terms(x):
    high = x.astype(jnp.bfloat16)
    rest = x - high.astype(jnp.float32)
    mid = rest.astype(jnp.bfloat16)
    low = (rest - mid.astype(jnp.float32)).astype(jnp.bfloat16)
    return high, mid, low


def row_terms(heads, tile, span, refs, out):
    grad_ref, outputs_ref, norm_ref = refs
    rows = grad_ref.shape[0] // 2
    toks = tile // heads
    spread = (
        lax.broadcasted_iota(jnp.int32, (toks, tile), 1) // heads
        == lax.broadcasted_iota(jnp.int32, (toks, tile), 0)
    ).astype(jnp.bfloat16)
    mine = (
        lax.broadcasted_iota(jnp.int32, (heads, tile), 1) % heads
        == lax.broadcasted_iota(jnp.int32, (heads, tile), 0)
    )
    ones = jnp.ones((8, grad_ref.shape[1]), jnp.bfloat16)
    for index in range(rows // tile):
        tok = pl.multiple_of(span * (rows // heads) + index * toks, toks)
        row = pl.multiple_of(span * rows + index * tile, tile)
        norm = norm_ref[:, pl.ds(tok, toks)] * math.log2(math.e)
        wide = sum(dot(part, spread, NN) for part in three_terms(norm))
        out[0:1, pl.ds(row, tile)] = jnp.sum(jnp.where(mine, wide, 0.0), axis=0, keepdims=True)
        prod = grad_ref[pl.ds(row, tile), :].astype(jnp.float32) * outputs_ref[
            pl.ds(row, tile), :
        ].astype(jnp.float32)
        high = prod.astype(jnp.bfloat16)
        low = (prod - high.astype(jnp.float32)).astype(jnp.bfloat16)
        out[1:2, pl.ds(row, tile)] = (dot(ones, high, NT) + dot(ones, low, NT))[0:1]


def opened(group, row, key, length):
    query_ref, grad_ref, key_ref, value_ref, _, tile = group
    k = key_ref[pl.ds(key, length), :]
    v = value_ref[pl.ds(key, length), :]
    scores = dot(k, query_ref[pl.ds(row, tile), :], NT)
    return scores, dot(v, grad_ref[pl.ds(row, tile), :], NT)


def closed(group, scale, row, triangle, scores, dprob):
    terms_ref, tile = group[4:]
    norm = terms_ref[0:1, pl.ds(row, tile)]
    delta = terms_ref[1:2, pl.ds(row, tile)]
    prob = jnp.exp2(scores * (scale * math.log2(math.e)) - norm)
    if triangle is not None:
        edge = prob.shape[0] - triangle.shape[0]
        last = jnp.where(triangle, prob[edge:], 0.0)
        prob = last if edge == 0 else jnp.concatenate([prob[:edge], last], axis=0)
    return prob.astype(jnp.bfloat16), (prob * (dprob - delta)).astype(jnp.bfloat16)


def triangle_grads(group, accs, scale, row, key, half, triangle, kept_ref):
    query_ref, grad_ref, tile = group[0], group[1], group[-1]
    key_acc, value_acc = accs
    per = triangle.shape[0]
    tiles = [(pl.multiple_of(row + p * tile, tile), (p + 1) * per) for p in range(half // per)]
    ahead = opened(group, tiles[0][0], key, tiles[0][1])
    for index, (row, length) in enumerate(tiles):
        now = ahead
        if index + 1 < len(tiles):
            ahead = opened(group, tiles[index + 1][0], key, tiles[index + 1][1])
        prob, dscore = closed(group, scale, row, triangle, *now)
        kept_ref[pl.ds(key, length), pl.ds(row, tile)] = dscore
        value_acc[pl.ds(key, length), :] += dot(prob, grad_ref[pl.ds(row, tile), :], NN)
        key_acc[pl.ds(key, length), :] += dot(dscore, query_ref[pl.ds(row, tile), :], NN)


def block_grads(group, accs, scale, rows, blocks):
    query_ref, grad_ref, tile = group[0], group[1], group[-1]
    key_acc, value_acc = accs
    count = rows // tile
    tiles = [(block, p) for block in blocks for p in range(count)]

    def start(block, p):
        row, key, length = block[:3]
        return opened(group, pl.multiple_of(row + p * tile, tile), key, length)

    ahead = start(*tiles[0])
    for index, (block, p) in enumerate(tiles):
        now = ahead
        if index + 1 < len(tiles):
            ahead = start(*tiles[index + 1])
        row, key, length, kept, probs = block
        prob, dscore = closed(group, scale, pl.multiple_of(row + p * tile, tile), None, *now)
        probs[:, p * tile : (p + 1) * tile] = prob
        kept[:, p * tile : (p + 1) * tile] = dscore
        if p == count - 1:
            value_acc[pl.ds(key, length), :] += dot(probs[...], grad_ref[pl.ds(row, rows), :], NN)
            key_acc[pl.ds(key, length), :] += dot(kept[...], query_ref[pl.ds(row, rows), :], NN)


def span_pair(span_ids, holder):
    return span_ids[2 * holder], span_ids[2 * holder + 1]


def far_halves(span_ids, step):
    me, holders = lax.axis_index("ctx"), lax.axis_size("ctx")
    mine = span_pair(span_ids, me)
    theirs = span_pair(span_ids, lax.rem(me + holders - step, holders))
    high_only = jnp.minimum(*mine) < jnp.minimum(*theirs)
    our_high = jnp.where(mine[0] > mine[1], 0, 1)
    their_low = jnp.where(theirs[0] > theirs[1], 1, 0)
    return lambda item: (
        jnp.where(high_only, our_high, item),
        jnp.where(high_only, item, their_low),
    )


def put_shares(outs, key_acc, value_acc, scale, first=0, parts=None, more=None):
    parts = parts or len(outs) + first
    share = key_acc.shape[0] // parts
    x = lax.axis_index("head")
    for away, out in enumerate(outs, first):
        start = pl.multiple_of(lax.rem(x + away, parts) * share, share)
        for low, part in (
            (0, key_acc[pl.ds(start, share), :] * scale),
            (share, value_acc[pl.ds(start, share), :]),
        ):
            if more is not None:
                part = part + more(away, low, share)
            out[low : low + share, :] = part.astype(out.dtype)


def own_work(group, accs, scale, span_ids, kept_ref, probs_ref, heads):
    tile = group[-1]
    toks, rows = kept_ref.shape
    half, span_rows, per = toks // 2, rows // 2, tile // heads
    first, second = span_pair(span_ids, lax.axis_index("ctx"))
    low = jnp.where(first > second, 1, 0)
    triangle = lax.broadcasted_iota(jnp.int32, (per, tile), 0) <= (
        lax.broadcasted_iota(jnp.int32, (per, tile), 1) // heads
    )

    def corner(which):
        key = pl.multiple_of(which * half, half)
        row = pl.multiple_of(which * span_rows, span_rows)
        triangle_grads(group, accs, scale, row, key, half, triangle, kept_ref)

    def square():
        key = pl.multiple_of(low * half, half)
        row = pl.multiple_of((1 - low) * span_rows, span_rows)
        kept = kept_ref.at[pl.ds(key, half), pl.ds(row, span_rows)]
        block_grads(group, accs, scale, span_rows, [(row, key, half, kept, probs_ref)])

    return low, corner, square


def first_kernel(heads, tile, scale, parts, *refs):
    inputs, refs = refs[:7], refs[7:]
    terms_ref, both_ref, kept_ref, key_acc, value_acc = refs[:5]
    held, (probs_ref, span_ids, sems) = refs[5:-3], refs[-3:]
    grad_ref, outputs_ref, query_ref, norm_ref = held
    toks = both_ref.shape[0] // 2
    key_ref, value_ref = both_ref.at[pl.ds(0, toks)], both_ref.at[pl.ds(toks, toks)]
    rows = toks * heads // 2
    whole = [
        pltpu.make_async_copy(a, b, sems.at[i, 2])
        for i, (a, b) in enumerate(zip(inputs[3:], (norm_ref, key_ref, value_ref, span_ids)))
    ]

    def halves(slot, index):
        part = pl.ds(pl.multiple_of(index * rows, rows), rows)
        return [
            pltpu.make_async_copy(inputs[i].at[part], held[i].at[part], sems.at[i, slot])
            for i in range(3)
        ]

    x = lax.axis_index("head")
    order = (1 - x, x) if parts == 2 else (0, 1)
    for copy in whole + halves(0, order[0]) + halves(1, order[1]):
        copy.start()
    key_acc[...] = jnp.zeros_like(key_acc)
    value_acc[...] = jnp.zeros_like(value_acc)
    for copy in whole:
        copy.wait()

    def arrive(slot):
        for copy in halves(slot, order[slot]):
            copy.wait()
        row_terms(heads, tile, order[slot], (grad_ref, outputs_ref, norm_ref), terms_ref)

    group = (query_ref, grad_ref, key_ref, value_ref, terms_ref, tile)
    accs = (key_acc, value_acc)
    low, corner, square = own_work(group, accs, scale, span_ids, kept_ref, probs_ref, heads)
    arrive(0)
    corner(order[0])
    arrive(1)
    if parts == 2:
        pl.when(low == order[0])(square)
        pl.when(low == order[1])(lambda: corner(order[1]))
    else:
        corner(order[1])
        square()


def last_kernel(heads, tile, scale, parts, span_ids, *refs):
    query_ref, grad_ref, terms_ref, both_ref = refs[:4]
    kept_ref, key_acc, value_acc, total_ref, probs_ref = refs[8:]
    if parts == 2:
        toks = both_ref.shape[0] // 2
        key_ref, value_ref = both_ref.at[pl.ds(0, toks)], both_ref.at[pl.ds(toks, toks)]
        group = (query_ref, grad_ref, key_ref, value_ref, terms_ref, tile)
        accs = (key_acc, value_acc)
        x = lax.axis_index("head")
        low, corner, square = own_work(group, accs, scale, span_ids, kept_ref, probs_ref, heads)
        pl.when(low == x)(square)
        pl.when(low != x)(lambda: corner(x))
    put_shares([total_ref], key_acc, value_acc, scale, 0, parts)


def near_kernel(heads, tile, scale, parts, span_ids, *refs):
    query_ref, grad_ref, terms_ref, key_ref, value_ref, own_keys, own_values, _, kept_ref = refs[:9]
    outs, own_outs, (key_acc, value_acc, probs_ref) = refs[9 : 9 + parts], refs[9 + parts : -3], refs[-3:]
    put_shares(own_outs, own_keys, own_values, scale, 1)
    group = (query_ref, grad_ref, key_ref, value_ref, terms_ref, tile)
    far_work(group, (key_acc, value_acc), scale, span_ids, kept_ref, probs_ref, heads, 1)
    put_shares(outs, key_acc, value_acc, scale)


def pack_kernel(key_ref, value_ref, out_ref):
    toks = key_ref.shape[0]
    out_ref[0:toks, :] = key_ref[...]
    out_ref[toks : 2 * toks, :] = value_ref[...]


def far_kernel(heads, tile, scale, span_ids, *refs):
    query_ref, grad_ref, terms_ref, over_ref, beside_ref, _ = refs[:6]
    parts = (len(refs) - 11) // 2
    swapped, both_ref, kept_ref = refs[6 : 6 + parts], refs[6 + parts], refs[7 + parts]
    outs, (key_acc, value_acc, probs_ref) = refs[8 + parts : -3], refs[-3:]
    toks = both_ref.shape[0] // 2
    is_odd = lax.rem(lax.axis_index("ctx"), 2) == 1

    @pl.when(is_odd)
    def _():
        both_ref[...] = beside_ref[...]

    @pl.when(jnp.logical_not(is_odd))
    def _():
        both_ref[...] = over_ref[...]

    key_ref, value_ref = both_ref.at[pl.ds(0, toks)], both_ref.at[pl.ds(toks, toks)]
    group = (query_ref, grad_ref, key_ref, value_ref, terms_ref, tile)
    far_work(group, (key_acc, value_acc), scale, span_ids, kept_ref, probs_ref, heads, 2)
    odd = is_odd.astype(jnp.float32)

    def more(away, low, share):
        return swapped[away][low : low + share, :].astype(jnp.float32) * odd

    put_shares(outs, key_acc, value_acc, scale, more=more)


def far_work(group, accs, scale, span_ids, kept_ref, probs_ref, heads, step):
    key_acc, value_acc = accs
    key_acc[...] = jnp.zeros_like(key_acc)
    value_acc[...] = jnp.zeros_like(value_acc)
    half = group[2].shape[0] // 2
    rows = half * heads
    halves = far_halves(span_ids, step)
    blocks = []
    for item in range(2):
        row_half, key_half = halves(item)
        row = pl.multiple_of(row_half * rows, rows)
        key = pl.multiple_of(key_half * half, half)
        blocks.append((row, key, half, kept_ref.at[item], probs_ref.at[item]))
    block_grads(group, accs, scale, rows, blocks)


def join_kernel(*refs):
    count = len(refs) // 3
    even = 1.0 - lax.rem(lax.axis_index("ctx"), 2).astype(jnp.float32)
    for swapped, this, out in zip(refs, refs[count:], refs[2 * count :]):
        more = swapped[...].astype(jnp.float32) * even
        out[...] = (this[...].astype(jnp.float32) + more).astype(out.dtype)


def total_kernel(total_ref, swapped_ref, *refs):
    ins, (key_out, value_out) = refs[:-2], refs[-2:]
    share = key_out.shape[0]
    even = 1.0 - lax.rem(lax.axis_index("ctx"), 2).astype(jnp.float32)
    for low, out in ((0, key_out), (share, value_out)):
        part = total_ref[low : low + share, :]
        part = part + swapped_ref[low : low + share, :].astype(jnp.float32) * even
        for ref in ins:
            part = part + ref[low : low + share, :].astype(jnp.float32)
        out[...] = part.astype(out.dtype)


def query_kernel(heads, tile, scale, span_ids, both_ref, own_ref, *refs):
    (key_1, both_2), kept_refs, (out_ref, acc, turned) = refs[:2], refs[2:-3], refs[-3:]
    toks = both_ref.shape[0] // 2
    half = toks // 2
    rows = half * heads
    per = tile // heads
    for index, key_ref in enumerate((both_ref, key_1, both_2)):
        for low in range(0, toks, half):
            turned[index, :, low : low + half] = key_ref[low : low + half, :].T

    @pl.loop(0, 2)
    def _(index):
        key = pl.multiple_of(index * half, half)
        for p in range(half // per):
            row = pl.multiple_of(index * rows + p * tile, tile)
            length = (p + 1) * per
            acc[:, pl.ds(row, tile)] = dot(
                turned[0, :, pl.ds(key, length)], own_ref[pl.ds(key, length), pl.ds(row, tile)], NN
            )

    first, second = span_pair(span_ids, lax.axis_index("ctx"))
    low = jnp.where(first > second, 1, 0)
    key = pl.multiple_of(low * half, half)
    for p in range(rows // tile):
        row = pl.multiple_of((1 - low) * rows + p * tile, tile)
        acc[:, pl.ds(row, tile)] += dot(
            turned[0, :, pl.ds(key, half)], own_ref[pl.ds(key, half), pl.ds(row, tile)], NN
        )
    for step, kept_ref in enumerate(kept_refs, 1):
        halves = far_halves(span_ids, step)

        @pl.loop(0, 2)
        def _(item):
            row_half, key_half = halves(item)
            key = pl.multiple_of(key_half * half, half)
            for p in range(rows // tile):
                row = pl.multiple_of(row_half * rows + p * tile, tile)
                acc[:, pl.ds(row, tile)] += dot(
                    turned[step, :, pl.ds(key, half)],
                    kept_ref[item, :, p * tile : (p + 1) * tile],
                    NN,
                )

    for row in range(0, 2 * rows, tile):
        out_ref[row : row + tile, :] = (acc[:, row : row + tile] * scale).astype(out_ref.dtype).T


VMEM = pl.BlockSpec(memory_space=pltpu.VMEM)
SMEM = pl.BlockSpec(memory_space=pltpu.SMEM)
HBM = pl.BlockSpec(memory_space=pltpu.HBM)
ANY = pl.BlockSpec(memory_space=pl.ANY)
MIB = 1024 * 1024


def call(kernel, ins, where, outs, scratch, blocks, limit, name, aliases=None):
    flops = blocks * 40 * 512 * 512 * 128
    return pl.pallas_call(
        kernel,
        out_shape=outs,
        in_specs=where,
        out_specs=[VMEM] * len(outs),
        scratch_shapes=scratch,
        input_output_aliases=aliases or {},
        compiler_params=pltpu.CompilerParams(vmem_limit_bytes=limit * MIB),
        name=name,
        cost_estimate=pl.CostEstimate(flops=int(flops), bytes_accessed=int(blocks * (1 << 20)), transcendentals=0),
    )(*ins)


def moved(block, back, away):
    holders, parts = lax.axis_size("ctx"), lax.axis_size("head")
    route = [
        (h * parts + x, ((h - back[h % 2]) % holders) * parts + (x + away) % parts)
        for h in range(holders)
        for x in range(parts)
    ]
    return lax.ppermute(block, ("ctx", "head"), route)


def local(queries, keys, values, outputs, out_grad, log_norm, span_ids):
    toks, heads, dim = queries.shape
    rows = toks * heads
    scale = dim ** (-0.5)
    parts = lax.axis_size("head")
    tile = 512
    q = queries.reshape(rows, dim)
    g = out_grad.reshape(rows, dim)
    o = outputs.reshape(rows, dim)
    share = 2 * toks // parts
    f32, bf16 = jnp.float32, jnp.bfloat16
    shape = jax.ShapeDtypeStruct
    grads = [shape((share, dim), bf16)] * parts
    accs = [pltpu.VMEM((toks, dim), f32)] * 2
    probs = pltpu.VMEM((toks // 2, rows // 2), bf16)

    key_1, value_1 = moved(keys, (-1, -1), 0), moved(values, (-1, -1), 0)
    inputs = tuple(
        pltpu.with_memory_space_constraint(a, pltpu.HBM)
        for a in (g, o, q, log_norm, keys, values, span_ids)
    )
    sums = [shape((toks, rows), bf16), shape((toks, dim), f32), shape((toks, dim), f32)]
    terms, both, kept, key_sum, value_sum = call(
        functools.partial(first_kernel, heads, tile, scale, parts),
        inputs,
        [HBM] * len(inputs),
        [shape((8, rows), f32), shape((2 * toks, dim), bf16)] + sums,
        [pltpu.VMEM(a.shape, a.dtype) for a in inputs[:4]]
        + [probs, pltpu.SMEM(span_ids.shape, span_ids.dtype), pltpu.SemaphoreType.DMA((4, 3))],
        1.625 * heads,
        20,
        "first",
    )
    (both_1,) = call(
        pack_kernel, (key_1, value_1), [VMEM] * 2, [shape((2 * toks, dim), bf16)], [], 0.01, 4, "pack"
    )
    over, beside = moved(both, (-2, 0), 0), moved(both_1, (-1, 1), 0)

    block = (toks // 2, rows // 2)
    kept_1, *sent = call(
        functools.partial(near_kernel, heads, tile, scale, parts),
        (span_ids, q, g, terms, key_1, value_1, key_sum, value_sum, both_1),
        [SMEM] + [VMEM] * 7 + [ANY],
        [shape((2,) + block, bf16)] + grads + grads[1:],
        accs + [pltpu.VMEM((2,) + block, bf16)],
        2 * heads,
        18,
        "near",
    )
    swapped = [moved(part, (-1, 1), 0) for part in sent[:parts]]
    sent = call(
        join_kernel,
        (*swapped[1:], *sent[parts:]),
        [VMEM] * (2 * parts - 2),
        grads[1:],
        [],
        0.01,
        4,
        "join",
    )
    whole = [moved(part, (0, 0), away) for away, part in enumerate(sent, 1)]
    both_2, kept_2, *sent = call(
        functools.partial(far_kernel, heads, tile, scale),
        (span_ids, q, g, terms, over, beside, sent[0], *swapped),
        [SMEM] + [VMEM] * 5 + [ANY] + [VMEM] * parts,
        [shape((2 * toks, dim), bf16), shape((2,) + block, bf16)] + grads,
        accs + [pltpu.VMEM((2,) + block, bf16)],
        2 * heads,
        18,
        "far",
    )
    landed = whole + [moved(part, (2, 2), away) for away, part in enumerate(sent)]
    kept, _, _, total = call(
        functools.partial(last_kernel, heads, tile, scale, parts),
        (span_ids, q, g, terms, both, kept, key_sum, value_sum, sent[0]),
        [SMEM] + [VMEM] * 7 + [ANY],
        sums + [shape((share, dim), f32)],
        [probs],
        1.625 * heads,
        20,
        "last",
        {5: 0, 6: 1, 7: 2},
    )
    (query_grad,) = call(
        functools.partial(query_kernel, heads, tile, scale),
        (span_ids, both, kept, key_1, both_2, kept_1, kept_2),
        [SMEM] + [VMEM] * 6,
        [shape((rows, dim), bf16)],
        [pltpu.VMEM((dim, rows), f32), pltpu.VMEM((STEPS, dim, toks), bf16)],
        1.25 * heads,
        28,
        "queries",
    )
    key_grad, value_grad = call(
        total_kernel,
        (total, swapped[0], *landed),
        [VMEM] * (2 + len(landed)),
        [shape((share // 2, dim), bf16)] * 2,
        [],
        0.01,
        8,
        "total",
    )
    return query_grad.reshape(toks, heads, dim), key_grad, value_grad


def solution(mesh):
    in_specs = (
        P("ctx", "head", None),
        P("ctx", None),
        P("ctx", None),
        P("ctx", "head", None),
        P("ctx", "head", None),
        P("head", "ctx"),
        P(),
    )
    out_specs = (P("ctx", "head", None), P(("ctx", "head"), None), P(("ctx", "head"), None))
    return jax.shard_map(local, mesh=mesh, in_specs=in_specs, out_specs=out_specs, check_vma=False)
```

```python
import functools
import math

import jax
import jax.numpy as jnp
from jax import lax
from jax.experimental import pallas as pl
from jax.experimental.pallas import tpu as pltpu
from jax.sharding import PartitionSpec as P

STEPS = 3
NT = (((1,), (1,)), ((), ()))
NN = (((1,), (0,)), ((), ()))
TN = (((0,), (0,)), ((), ()))


def dot(a, b, dims):
    return lax.dot_general(a, b, dims, preferred_element_type=jnp.float32)


def three_terms(x):
    high = x.astype(jnp.bfloat16)
    rest = x - high.astype(jnp.float32)
    mid = rest.astype(jnp.bfloat16)
    low = (rest - mid.astype(jnp.float32)).astype(jnp.bfloat16)
    return high, mid, low


def row_terms(heads, tile, span, refs, out):
    grad_ref, outputs_ref, norm_ref = refs
    rows = grad_ref.shape[0] // 2
    toks = tile // heads
    spread = (
        lax.broadcasted_iota(jnp.int32, (toks, tile), 1) // heads
        == lax.broadcasted_iota(jnp.int32, (toks, tile), 0)
    ).astype(jnp.bfloat16)
    mine = (
        lax.broadcasted_iota(jnp.int32, (heads, tile), 1) % heads
        == lax.broadcasted_iota(jnp.int32, (heads, tile), 0)
    )
    ones = jnp.ones((8, grad_ref.shape[1]), jnp.bfloat16)
    for index in range(rows // tile):
        tok = pl.multiple_of(span * (rows // heads) + index * toks, toks)
        row = pl.multiple_of(span * rows + index * tile, tile)
        norm = norm_ref[:, pl.ds(tok, toks)] * math.log2(math.e)
        wide = sum(dot(part, spread, NN) for part in three_terms(norm))
        out[0:1, pl.ds(row, tile)] = jnp.sum(jnp.where(mine, wide, 0.0), axis=0, keepdims=True)
        prod = grad_ref[pl.ds(row, tile), :].astype(jnp.float32) * outputs_ref[
            pl.ds(row, tile), :
        ].astype(jnp.float32)
        high = prod.astype(jnp.bfloat16)
        low = (prod - high.astype(jnp.float32)).astype(jnp.bfloat16)
        out[1:2, pl.ds(row, tile)] = (dot(ones, high, NT) + dot(ones, low, NT))[0:1]


def opened(group, row, key, length):
    query_ref, grad_ref, key_ref, value_ref, _, tile = group
    k = key_ref[pl.ds(key, length), :]
    v = value_ref[pl.ds(key, length), :]
    scores = dot(k, query_ref[pl.ds(row, tile), :], NT)
    return scores, dot(v, grad_ref[pl.ds(row, tile), :], NT)


def closed(group, scale, row, triangle, scores, dprob):
    terms_ref, tile = group[4:]
    norm = terms_ref[0:1, pl.ds(row, tile)]
    delta = terms_ref[1:2, pl.ds(row, tile)]
    prob = jnp.exp2(scores * (scale * math.log2(math.e)) - norm)
    if triangle is not None:
        edge = prob.shape[0] - triangle.shape[0]
        last = jnp.where(triangle, prob[edge:], 0.0)
        prob = last if edge == 0 else jnp.concatenate([prob[:edge], last], axis=0)
    return prob.astype(jnp.bfloat16), (prob * (dprob - delta)).astype(jnp.bfloat16)


def triangle_grads(group, accs, scale, row, key, half, triangle, kept_ref):
    query_ref, grad_ref, tile = group[0], group[1], group[-1]
    key_acc, value_acc = accs
    per = triangle.shape[0]
    tiles = [(pl.multiple_of(row + p * tile, tile), (p + 1) * per) for p in range(half // per)]
    ahead = opened(group, tiles[0][0], key, tiles[0][1])
    for index, (row, length) in enumerate(tiles):
        now = ahead
        if index + 1 < len(tiles):
            ahead = opened(group, tiles[index + 1][0], key, tiles[index + 1][1])
        prob, dscore = closed(group, scale, row, triangle, *now)
        kept_ref[pl.ds(key, length), pl.ds(row, tile)] = dscore
        value_acc[pl.ds(key, length), :] += dot(prob, grad_ref[pl.ds(row, tile), :], NN)
        key_acc[pl.ds(key, length), :] += dot(dscore, query_ref[pl.ds(row, tile), :], NN)


def block_grads(group, accs, scale, rows, blocks):
    query_ref, grad_ref, tile = group[0], group[1], group[-1]
    key_acc, value_acc = accs
    count = rows // tile
    tiles = [(block, p) for block in blocks for p in range(count)]

    def start(block, p):
        row, key, length = block[:3]
        return opened(group, pl.multiple_of(row + p * tile, tile), key, length)

    ahead = start(*tiles[0])
    for index, (block, p) in enumerate(tiles):
        now = ahead
        if index + 1 < len(tiles):
            ahead = start(*tiles[index + 1])
        row, key, length, kept, probs = block
        prob, dscore = closed(group, scale, pl.multiple_of(row + p * tile, tile), None, *now)
        probs[:, p * tile : (p + 1) * tile] = prob
        kept[:, p * tile : (p + 1) * tile] = dscore
        if p == count - 1:
            value_acc[pl.ds(key, length), :] += dot(probs[...], grad_ref[pl.ds(row, rows), :], NN)
            key_acc[pl.ds(key, length), :] += dot(kept[...], query_ref[pl.ds(row, rows), :], NN)


def span_pair(span_ids, holder):
    return span_ids[2 * holder], span_ids[2 * holder + 1]


def far_halves(span_ids, step):
    me, holders = lax.axis_index("ctx"), lax.axis_size("ctx")
    mine = span_pair(span_ids, me)
    theirs = span_pair(span_ids, lax.rem(me + holders - step, holders))
    high_only = jnp.minimum(*mine) < jnp.minimum(*theirs)
    our_high = jnp.where(mine[0] > mine[1], 0, 1)
    their_low = jnp.where(theirs[0] > theirs[1], 1, 0)
    return lambda item: (
        jnp.where(high_only, our_high, item),
        jnp.where(high_only, item, their_low),
    )


def put_shares(outs, key_acc, value_acc, scale, first=0, parts=None, more=None):
    parts = parts or len(outs) + first
    share = key_acc.shape[0] // parts
    x = lax.axis_index("head")
    for away, out in enumerate(outs, first):
        start = pl.multiple_of(lax.rem(x + away, parts) * share, share)
        for low, part in (
            (0, key_acc[pl.ds(start, share), :] * scale),
            (share, value_acc[pl.ds(start, share), :]),
        ):
            if more is not None:
                part = part + more(away, low, share)
            out[low : low + share, :] = part.astype(out.dtype)


def own_work(group, accs, scale, span_ids, kept_ref, probs_ref, heads):
    tile = group[-1]
    toks, rows = kept_ref.shape
    half, span_rows, per = toks // 2, rows // 2, tile // heads
    first, second = span_pair(span_ids, lax.axis_index("ctx"))
    low = jnp.where(first > second, 1, 0)
    triangle = lax.broadcasted_iota(jnp.int32, (per, tile), 0) <= (
        lax.broadcasted_iota(jnp.int32, (per, tile), 1) // heads
    )

    def corner(which):
        key = pl.multiple_of(which * half, half)
        row = pl.multiple_of(which * span_rows, span_rows)
        triangle_grads(group, accs, scale, row, key, half, triangle, kept_ref)

    def square():
        key = pl.multiple_of(low * half, half)
        row = pl.multiple_of((1 - low) * span_rows, span_rows)
        kept = kept_ref.at[pl.ds(key, half), pl.ds(row, span_rows)]
        block_grads(group, accs, scale, span_rows, [(row, key, half, kept, probs_ref)])

    return low, corner, square


def first_kernel(heads, tile, scale, parts, *refs):
    inputs, refs = refs[:7], refs[7:]
    terms_ref, both_ref, kept_ref, key_acc, value_acc = refs[:5]
    held, (probs_ref, span_ids, sems) = refs[5:-3], refs[-3:]
    grad_ref, outputs_ref, query_ref, norm_ref = held
    toks = both_ref.shape[0] // 2
    key_ref, value_ref = both_ref.at[pl.ds(0, toks)], both_ref.at[pl.ds(toks, toks)]
    rows = toks * heads // 2
    whole = [
        pltpu.make_async_copy(a, b, sems.at[i, 2])
        for i, (a, b) in enumerate(zip(inputs[3:], (norm_ref, key_ref, value_ref, span_ids)))
    ]

    def halves(slot, index):
        part = pl.ds(pl.multiple_of(index * rows, rows), rows)
        return [
            pltpu.make_async_copy(inputs[i].at[part], held[i].at[part], sems.at[i, slot])
            for i in range(3)
        ]

    x = lax.axis_index("head")
    order = (1 - x, x) if parts == 2 else (0, 1)
    for copy in whole + halves(0, order[0]) + halves(1, order[1]):
        copy.start()
    key_acc[...] = jnp.zeros_like(key_acc)
    value_acc[...] = jnp.zeros_like(value_acc)
    for copy in whole:
        copy.wait()

    def arrive(slot):
        for copy in halves(slot, order[slot]):
            copy.wait()
        row_terms(heads, tile, order[slot], (grad_ref, outputs_ref, norm_ref), terms_ref)

    group = (query_ref, grad_ref, key_ref, value_ref, terms_ref, tile)
    accs = (key_acc, value_acc)
    low, corner, square = own_work(group, accs, scale, span_ids, kept_ref, probs_ref, heads)
    arrive(0)
    corner(order[0])
    arrive(1)
    if parts == 2:
        pl.when(low == order[0])(square)
        pl.when(low == order[1])(lambda: corner(order[1]))
    else:
        corner(order[1])
        square()


def last_kernel(heads, tile, scale, parts, span_ids, *refs):
    query_ref, grad_ref, terms_ref, both_ref = refs[:4]
    kept_ref, key_acc, value_acc, total_ref, probs_ref = refs[8:]
    if parts == 2:
        toks = both_ref.shape[0] // 2
        key_ref, value_ref = both_ref.at[pl.ds(0, toks)], both_ref.at[pl.ds(toks, toks)]
        group = (query_ref, grad_ref, key_ref, value_ref, terms_ref, tile)
        accs = (key_acc, value_acc)
        x = lax.axis_index("head")
        low, corner, square = own_work(group, accs, scale, span_ids, kept_ref, probs_ref, heads)
        pl.when(low == x)(square)
        pl.when(low != x)(lambda: corner(x))
    put_shares([total_ref], key_acc, value_acc, scale, 0, parts)


def near_kernel(heads, tile, scale, parts, span_ids, *refs):
    query_ref, grad_ref, terms_ref, key_ref, value_ref, own_keys, own_values, _, kept_ref = refs[:9]
    outs, own_outs, (key_acc, value_acc, probs_ref) = refs[9 : 9 + parts], refs[9 + parts : -3], refs[-3:]
    put_shares(own_outs, own_keys, own_values, scale, 1)
    group = (query_ref, grad_ref, key_ref, value_ref, terms_ref, tile)
    far_work(group, (key_acc, value_acc), scale, span_ids, kept_ref, probs_ref, heads, 1)
    put_shares(outs, key_acc, value_acc, scale)


def pack_kernel(key_ref, value_ref, both_ref, out_ref, copy_ref):
    toks = key_ref.shape[0]
    copy_ref[...] = both_ref[...]
    out_ref[0:toks, :] = key_ref[...]
    out_ref[toks : 2 * toks, :] = value_ref[...]


def far_kernel(heads, tile, scale, span_ids, *refs):
    query_ref, grad_ref, terms_ref, over_ref, beside_ref, _ = refs[:6]
    parts = (len(refs) - 11) // 2
    swapped, both_ref, kept_ref = refs[6 : 6 + parts], refs[6 + parts], refs[7 + parts]
    outs, (key_acc, value_acc, probs_ref) = refs[8 + parts : -3], refs[-3:]
    toks = both_ref.shape[0] // 2
    is_odd = lax.rem(lax.axis_index("ctx"), 2) == 1

    @pl.when(is_odd)
    def _():
        both_ref[...] = beside_ref[...]

    @pl.when(jnp.logical_not(is_odd))
    def _():
        both_ref[...] = over_ref[...]

    key_ref, value_ref = both_ref.at[pl.ds(0, toks)], both_ref.at[pl.ds(toks, toks)]
    group = (query_ref, grad_ref, key_ref, value_ref, terms_ref, tile)
    far_work(group, (key_acc, value_acc), scale, span_ids, kept_ref, probs_ref, heads, 2)
    odd = is_odd.astype(jnp.float32)

    def more(away, low, share):
        return swapped[away][low : low + share, :].astype(jnp.float32) * odd

    put_shares(outs, key_acc, value_acc, scale, more=more)


def far_work(group, accs, scale, span_ids, kept_ref, probs_ref, heads, step):
    key_acc, value_acc = accs
    key_acc[...] = jnp.zeros_like(key_acc)
    value_acc[...] = jnp.zeros_like(value_acc)
    half = group[2].shape[0] // 2
    rows = half * heads
    halves = far_halves(span_ids, step)
    blocks = []
    for item in range(2):
        row_half, key_half = halves(item)
        row = pl.multiple_of(row_half * rows, rows)
        key = pl.multiple_of(key_half * half, half)
        blocks.append((row, key, half, kept_ref.at[item], probs_ref.at[item]))
    block_grads(group, accs, scale, rows, blocks)


def join_kernel(*refs):
    count = len(refs) // 3
    even = 1.0 - lax.rem(lax.axis_index("ctx"), 2).astype(jnp.float32)
    for swapped, this, out in zip(refs, refs[count:], refs[2 * count :]):
        more = swapped[...].astype(jnp.float32) * even
        out[...] = (this[...].astype(jnp.float32) + more).astype(out.dtype)


def total_kernel(total_ref, swapped_ref, *refs):
    ins, (key_out, value_out) = refs[:-2], refs[-2:]
    share = key_out.shape[0]
    even = 1.0 - lax.rem(lax.axis_index("ctx"), 2).astype(jnp.float32)
    for low, out in ((0, key_out), (share, value_out)):
        part = total_ref[low : low + share, :]
        part = part + swapped_ref[low : low + share, :].astype(jnp.float32) * even
        for ref in ins:
            part = part + ref[low : low + share, :].astype(jnp.float32)
        out[...] = part.astype(out.dtype)


def query_kernel(heads, tile, scale, span_ids, both_ref, own_ref, *refs):
    (key_1, both_2), kept_refs, (out_ref, acc, turned) = refs[:2], refs[2:-3], refs[-3:]
    toks = both_ref.shape[0] // 2
    half = toks // 2
    rows = half * heads
    per = tile // heads
    for index, key_ref in enumerate((both_ref, key_1, both_2)):
        for low in range(0, toks, half):
            turned[index, :, low : low + half] = key_ref[low : low + half, :].T

    @pl.loop(0, 2)
    def _(index):
        key = pl.multiple_of(index * half, half)
        for p in range(half // per):
            row = pl.multiple_of(index * rows + p * tile, tile)
            length = (p + 1) * per
            acc[:, pl.ds(row, tile)] = dot(
                turned[0, :, pl.ds(key, length)], own_ref[pl.ds(key, length), pl.ds(row, tile)], NN
            )

    first, second = span_pair(span_ids, lax.axis_index("ctx"))
    low = jnp.where(first > second, 1, 0)
    key = pl.multiple_of(low * half, half)
    for p in range(rows // tile):
        row = pl.multiple_of((1 - low) * rows + p * tile, tile)
        acc[:, pl.ds(row, tile)] += dot(
            turned[0, :, pl.ds(key, half)], own_ref[pl.ds(key, half), pl.ds(row, tile)], NN
        )
    for step, kept_ref in enumerate(kept_refs, 1):
        halves = far_halves(span_ids, step)

        @pl.loop(0, 2)
        def _(item):
            row_half, key_half = halves(item)
            key = pl.multiple_of(key_half * half, half)
            for p in range(rows // tile):
                row = pl.multiple_of(row_half * rows + p * tile, tile)
                acc[:, pl.ds(row, tile)] += dot(
                    turned[step, :, pl.ds(key, half)],
                    kept_ref[item, :, p * tile : (p + 1) * tile],
                    NN,
                )

    for row in range(0, 2 * rows, tile):
        out_ref[row : row + tile, :] = (acc[:, row : row + tile] * scale).astype(out_ref.dtype).T


VMEM = pl.BlockSpec(memory_space=pltpu.VMEM)
SMEM = pl.BlockSpec(memory_space=pltpu.SMEM)
HBM = pl.BlockSpec(memory_space=pltpu.HBM)
ANY = pl.BlockSpec(memory_space=pl.ANY)
MIB = 1024 * 1024


def call(kernel, ins, where, outs, scratch, blocks, limit, name, aliases=None):
    flops = blocks * 40 * 512 * 512 * 128
    return pl.pallas_call(
        kernel,
        out_shape=outs,
        in_specs=where,
        out_specs=[VMEM] * len(outs),
        scratch_shapes=scratch,
        input_output_aliases=aliases or {},
        compiler_params=pltpu.CompilerParams(vmem_limit_bytes=limit * MIB),
        name=name,
        cost_estimate=pl.CostEstimate(flops=int(flops), bytes_accessed=int(blocks * (1 << 20)), transcendentals=0),
    )(*ins)


def moved(block, back, away):
    holders, parts = lax.axis_size("ctx"), lax.axis_size("head")
    route = [
        (h * parts + x, ((h - back[h % 2]) % holders) * parts + (x + away) % parts)
        for h in range(holders)
        for x in range(parts)
    ]
    return lax.ppermute(block, ("ctx", "head"), route)


def local(queries, keys, values, outputs, out_grad, log_norm, span_ids):
    toks, heads, dim = queries.shape
    rows = toks * heads
    scale = dim ** (-0.5)
    parts = lax.axis_size("head")
    tile = 512
    q = queries.reshape(rows, dim)
    g = out_grad.reshape(rows, dim)
    o = outputs.reshape(rows, dim)
    share = 2 * toks // parts
    f32, bf16 = jnp.float32, jnp.bfloat16
    shape = jax.ShapeDtypeStruct
    grads = [shape((share, dim), bf16)] * parts
    accs = [pltpu.VMEM((toks, dim), f32)] * 2
    probs = pltpu.VMEM((toks // 2, rows // 2), bf16)

    key_1, value_1 = moved(keys, (-1, -1), 0), moved(values, (-1, -1), 0)
    inputs = tuple(
        pltpu.with_memory_space_constraint(a, pltpu.HBM)
        for a in (g, o, q, log_norm, keys, values, span_ids)
    )
    sums = [shape((toks, rows), bf16), shape((toks, dim), f32), shape((toks, dim), f32)]
    terms, both, kept, key_sum, value_sum = call(
        functools.partial(first_kernel, heads, tile, scale, parts),
        inputs,
        [HBM] * len(inputs),
        [shape((8, rows), f32), shape((2 * toks, dim), bf16)] + sums,
        [pltpu.VMEM(a.shape, a.dtype) for a in inputs[:4]]
        + [probs, pltpu.SMEM(span_ids.shape, span_ids.dtype), pltpu.SemaphoreType.DMA((4, 3))],
        1.625 * heads,
        20,
        "first",
    )
    packed = [shape((2 * toks, dim), bf16)] * 2
    both_1, copied = call(
        pack_kernel, (key_1, value_1, both), [VMEM] * 3, packed, [], 0.01, 4, "pack"
    )
    beside, over = moved(both_1, (-1, 1), 0), moved(copied, (-2, 0), 0)

    block = (toks // 2, rows // 2)
    kept_1, *sent = call(
        functools.partial(near_kernel, heads, tile, scale, parts),
        (span_ids, q, g, terms, key_1, value_1, key_sum, value_sum, both_1),
        [SMEM] + [VMEM] * 7 + [ANY],
        [shape((2,) + block, bf16)] + grads + grads[1:],
        accs + [pltpu.VMEM((2,) + block, bf16)],
        2 * heads,
        18,
        "near",
    )
    swapped = [moved(part, (-1, 1), 0) for part in sent[:parts]]
    sent = call(
        join_kernel,
        (*swapped[1:], *sent[parts:]),
        [VMEM] * (2 * parts - 2),
        grads[1:],
        [],
        0.01,
        4,
        "join",
    )
    whole = [moved(part, (0, 0), away) for away, part in enumerate(sent, 1)]
    both_2, kept_2, *sent = call(
        functools.partial(far_kernel, heads, tile, scale),
        (span_ids, q, g, terms, over, beside, sent[0], *swapped),
        [SMEM] + [VMEM] * 5 + [ANY] + [VMEM] * parts,
        [shape((2 * toks, dim), bf16), shape((2,) + block, bf16)] + grads,
        accs + [pltpu.VMEM((2,) + block, bf16)],
        2 * heads,
        18,
        "far",
    )
    landed = whole + [moved(part, (2, 2), away) for away, part in enumerate(sent)]
    kept, _, _, total = call(
        functools.partial(last_kernel, heads, tile, scale, parts),
        (span_ids, q, g, terms, both, kept, key_sum, value_sum, sent[0]),
        [SMEM] + [VMEM] * 7 + [ANY],
        sums + [shape((share, dim), f32)],
        [probs],
        1.625 * heads,
        20,
        "last",
        {5: 0, 6: 1, 7: 2},
    )
    (query_grad,) = call(
        functools.partial(query_kernel, heads, tile, scale),
        (span_ids, both, kept, key_1, both_2, kept_1, kept_2),
        [SMEM] + [VMEM] * 6,
        [shape((rows, dim), bf16)],
        [pltpu.VMEM((dim, rows), f32), pltpu.VMEM((STEPS, dim, toks), bf16)],
        1.25 * heads,
        28,
        "queries",
    )
    key_grad, value_grad = call(
        total_kernel,
        (total, swapped[0], *landed),
        [VMEM] * (2 + len(landed)),
        [shape((share // 2, dim), bf16)] * 2,
        [],
        0.01,
        8,
        "total",
    )
    return query_grad.reshape(toks, heads, dim), key_grad, value_grad


def solution(mesh):
    in_specs = (
        P("ctx", "head", None),
        P("ctx", None),
        P("ctx", None),
        P("ctx", "head", None),
        P("ctx", "head", None),
        P("head", "ctx"),
        P(),
    )
    out_specs = (P("ctx", "head", None), P(("ctx", "head"), None), P(("ctx", "head"), None))
    return jax.shard_map(local, mesh=mesh, in_specs=in_specs, out_specs=out_specs, check_vma=False)
```

```python
import functools
import math

import jax
import jax.numpy as jnp
from jax import lax
from jax.experimental import pallas as pl
from jax.experimental.pallas import tpu as pltpu
from jax.sharding import PartitionSpec as P

STEPS = 3
NT = (((1,), (1,)), ((), ()))
NN = (((1,), (0,)), ((), ()))
TN = (((0,), (0,)), ((), ()))


def dot(a, b, dims):
    return lax.dot_general(a, b, dims, preferred_element_type=jnp.float32)


def three_terms(x):
    high = x.astype(jnp.bfloat16)
    rest = x - high.astype(jnp.float32)
    mid = rest.astype(jnp.bfloat16)
    low = (rest - mid.astype(jnp.float32)).astype(jnp.bfloat16)
    return high, mid, low


def row_terms(heads, tile, span, refs, out):
    grad_ref, outputs_ref, norm_ref = refs
    rows = grad_ref.shape[0] // 2
    toks = tile // heads
    spread = (
        lax.broadcasted_iota(jnp.int32, (toks, tile), 1) // heads
        == lax.broadcasted_iota(jnp.int32, (toks, tile), 0)
    ).astype(jnp.bfloat16)
    mine = (
        lax.broadcasted_iota(jnp.int32, (heads, tile), 1) % heads
        == lax.broadcasted_iota(jnp.int32, (heads, tile), 0)
    )
    ones = jnp.ones((8, grad_ref.shape[1]), jnp.bfloat16)
    for index in range(rows // tile):
        tok = pl.multiple_of(span * (rows // heads) + index * toks, toks)
        row = pl.multiple_of(span * rows + index * tile, tile)
        norm = norm_ref[:, pl.ds(tok, toks)] * math.log2(math.e)
        wide = sum(dot(part, spread, NN) for part in three_terms(norm))
        out[0:1, pl.ds(row, tile)] = jnp.sum(jnp.where(mine, wide, 0.0), axis=0, keepdims=True)
        prod = grad_ref[pl.ds(row, tile), :].astype(jnp.float32) * outputs_ref[
            pl.ds(row, tile), :
        ].astype(jnp.float32)
        high = prod.astype(jnp.bfloat16)
        low = (prod - high.astype(jnp.float32)).astype(jnp.bfloat16)
        out[1:2, pl.ds(row, tile)] = (dot(ones, high, NT) + dot(ones, low, NT))[0:1]


def opened(group, row, key, length):
    query_ref, grad_ref, key_ref, value_ref, _, tile = group
    k = key_ref[pl.ds(key, length), :]
    v = value_ref[pl.ds(key, length), :]
    scores = dot(k, query_ref[pl.ds(row, tile), :], NT)
    return scores, dot(v, grad_ref[pl.ds(row, tile), :], NT)


def closed(group, scale, row, triangle, scores, dprob):
    terms_ref, tile = group[4:]
    norm = terms_ref[0:1, pl.ds(row, tile)]
    delta = terms_ref[1:2, pl.ds(row, tile)]
    prob = jnp.exp2(scores * (scale * math.log2(math.e)) - norm)
    if triangle is not None:
        edge = prob.shape[0] - triangle.shape[0]
        last = jnp.where(triangle, prob[edge:], 0.0)
        prob = last if edge == 0 else jnp.concatenate([prob[:edge], last], axis=0)
    return prob.astype(jnp.bfloat16), (prob * (dprob - delta)).astype(jnp.bfloat16)


def triangle_grads(group, accs, scale, row, key, half, triangle, kept_ref):
    query_ref, grad_ref, tile = group[0], group[1], group[-1]
    key_acc, value_acc = accs
    per = triangle.shape[0]
    tiles = [(pl.multiple_of(row + p * tile, tile), (p + 1) * per) for p in range(half // per)]
    ahead = opened(group, tiles[0][0], key, tiles[0][1])
    for index, (row, length) in enumerate(tiles):
        now = ahead
        if index + 1 < len(tiles):
            ahead = opened(group, tiles[index + 1][0], key, tiles[index + 1][1])
        prob, dscore = closed(group, scale, row, triangle, *now)
        kept_ref[pl.ds(key, length), pl.ds(row, tile)] = dscore
        value_acc[pl.ds(key, length), :] += dot(prob, grad_ref[pl.ds(row, tile), :], NN)
        key_acc[pl.ds(key, length), :] += dot(dscore, query_ref[pl.ds(row, tile), :], NN)


def block_grads(group, accs, scale, rows, blocks):
    query_ref, grad_ref, tile = group[0], group[1], 256
    group = group[:-1] + (tile,)
    key_acc, value_acc = accs
    count = rows // tile
    tiles = [(block, p) for block in blocks for p in range(count)]

    def start(block, p):
        row, key, length = block[:3]
        return opened(group, pl.multiple_of(row + p * tile, tile), key, length)

    ahead = start(*tiles[0])
    for index, (block, p) in enumerate(tiles):
        now = ahead
        if index + 1 < len(tiles):
            ahead = start(*tiles[index + 1])
        row, key, length, kept, probs = block
        prob, dscore = closed(group, scale, pl.multiple_of(row + p * tile, tile), None, *now)
        probs[:, p * tile : (p + 1) * tile] = prob
        kept[:, p * tile : (p + 1) * tile] = dscore
        if p == count - 1:
            value_acc[pl.ds(key, length), :] += dot(probs[...], grad_ref[pl.ds(row, rows), :], NN)
            key_acc[pl.ds(key, length), :] += dot(kept[...], query_ref[pl.ds(row, rows), :], NN)


def span_pair(span_ids, holder):
    return span_ids[2 * holder], span_ids[2 * holder + 1]


def far_halves(span_ids, step):
    me, holders = lax.axis_index("ctx"), lax.axis_size("ctx")
    mine = span_pair(span_ids, me)
    theirs = span_pair(span_ids, lax.rem(me + holders - step, holders))
    high_only = jnp.minimum(*mine) < jnp.minimum(*theirs)
    our_high = jnp.where(mine[0] > mine[1], 0, 1)
    their_low = jnp.where(theirs[0] > theirs[1], 1, 0)
    return lambda item: (
        jnp.where(high_only, our_high, item),
        jnp.where(high_only, item, their_low),
    )


def put_shares(outs, key_acc, value_acc, scale, first=0, parts=None, more=None):
    parts = parts or len(outs) + first
    share = key_acc.shape[0] // parts
    x = lax.axis_index("head")
    for away, out in enumerate(outs, first):
        start = pl.multiple_of(lax.rem(x + away, parts) * share, share)
        for low, part in (
            (0, key_acc[pl.ds(start, share), :] * scale),
            (share, value_acc[pl.ds(start, share), :]),
        ):
            if more is not None:
                part = part + more(away, low, share)
            out[low : low + share, :] = part.astype(out.dtype)


def own_work(group, accs, scale, span_ids, kept_ref, probs_ref, heads):
    tile = group[-1]
    toks, rows = kept_ref.shape
    half, span_rows, per = toks // 2, rows // 2, tile // heads
    first, second = span_pair(span_ids, lax.axis_index("ctx"))
    low = jnp.where(first > second, 1, 0)
    triangle = lax.broadcasted_iota(jnp.int32, (per, tile), 0) <= (
        lax.broadcasted_iota(jnp.int32, (per, tile), 1) // heads
    )

    def corner(which):
        key = pl.multiple_of(which * half, half)
        row = pl.multiple_of(which * span_rows, span_rows)
        triangle_grads(group, accs, scale, row, key, half, triangle, kept_ref)

    def square():
        key = pl.multiple_of(low * half, half)
        row = pl.multiple_of((1 - low) * span_rows, span_rows)
        kept = kept_ref.at[pl.ds(key, half), pl.ds(row, span_rows)]
        block_grads(group, accs, scale, span_rows, [(row, key, half, kept, probs_ref)])

    return low, corner, square


def first_kernel(heads, tile, scale, parts, *refs):
    inputs, refs = refs[:7], refs[7:]
    terms_ref, both_ref, kept_ref, key_acc, value_acc = refs[:5]
    held, (probs_ref, span_ids, sems) = refs[5:-3], refs[-3:]
    grad_ref, outputs_ref, query_ref, norm_ref = held
    toks = both_ref.shape[0] // 2
    key_ref, value_ref = both_ref.at[pl.ds(0, toks)], both_ref.at[pl.ds(toks, toks)]
    rows = toks * heads // 2
    whole = [
        pltpu.make_async_copy(a, b, sems.at[i, 2])
        for i, (a, b) in enumerate(zip(inputs[3:], (norm_ref, key_ref, value_ref, span_ids)))
    ]

    def halves(slot, index):
        part = pl.ds(pl.multiple_of(index * rows, rows), rows)
        return [
            pltpu.make_async_copy(inputs[i].at[part], held[i].at[part], sems.at[i, slot])
            for i in range(3)
        ]

    x = lax.axis_index("head")
    order = (1 - x, x) if parts == 2 else (0, 1)
    for copy in whole + halves(0, order[0]) + halves(1, order[1]):
        copy.start()
    key_acc[...] = jnp.zeros_like(key_acc)
    value_acc[...] = jnp.zeros_like(value_acc)
    for copy in whole:
        copy.wait()

    def arrive(slot):
        for copy in halves(slot, order[slot]):
            copy.wait()
        row_terms(heads, tile, order[slot], (grad_ref, outputs_ref, norm_ref), terms_ref)

    group = (query_ref, grad_ref, key_ref, value_ref, terms_ref, tile)
    accs = (key_acc, value_acc)
    low, corner, square = own_work(group, accs, scale, span_ids, kept_ref, probs_ref, heads)
    arrive(0)
    corner(order[0])
    arrive(1)
    if parts == 2:
        pl.when(low == order[0])(square)
        pl.when(low == order[1])(lambda: corner(order[1]))
    else:
        corner(order[1])
        square()


def last_kernel(heads, tile, scale, parts, span_ids, *refs):
    query_ref, grad_ref, terms_ref, both_ref = refs[:4]
    kept_ref, key_acc, value_acc, total_ref, probs_ref = refs[8:]
    if parts == 2:
        toks = both_ref.shape[0] // 2
        key_ref, value_ref = both_ref.at[pl.ds(0, toks)], both_ref.at[pl.ds(toks, toks)]
        group = (query_ref, grad_ref, key_ref, value_ref, terms_ref, tile)
        accs = (key_acc, value_acc)
        x = lax.axis_index("head")
        low, corner, square = own_work(group, accs, scale, span_ids, kept_ref, probs_ref, heads)
        pl.when(low == x)(square)
        pl.when(low != x)(lambda: corner(x))
    put_shares([total_ref], key_acc, value_acc, scale, 0, parts)


def near_kernel(heads, tile, scale, parts, span_ids, *refs):
    query_ref, grad_ref, terms_ref, key_ref, value_ref, own_keys, own_values, _, kept_ref = refs[:9]
    outs, own_outs, (key_acc, value_acc, probs_ref) = refs[9 : 9 + parts], refs[9 + parts : -3], refs[-3:]
    put_shares(own_outs, own_keys, own_values, scale, 1)
    group = (query_ref, grad_ref, key_ref, value_ref, terms_ref, tile)
    far_work(group, (key_acc, value_acc), scale, span_ids, kept_ref, probs_ref, heads, 1)
    put_shares(outs, key_acc, value_acc, scale)


def pack_kernel(key_ref, value_ref, out_ref):
    toks = key_ref.shape[0]
    out_ref[0:toks, :] = key_ref[...]
    out_ref[toks : 2 * toks, :] = value_ref[...]


def far_kernel(heads, tile, scale, span_ids, *refs):
    query_ref, grad_ref, terms_ref, over_ref, beside_ref, _ = refs[:6]
    parts = (len(refs) - 11) // 2
    swapped, both_ref, kept_ref = refs[6 : 6 + parts], refs[6 + parts], refs[7 + parts]
    outs, (key_acc, value_acc, probs_ref) = refs[8 + parts : -3], refs[-3:]
    toks = both_ref.shape[0] // 2
    is_odd = lax.rem(lax.axis_index("ctx"), 2) == 1

    @pl.when(is_odd)
    def _():
        both_ref[...] = beside_ref[...]

    @pl.when(jnp.logical_not(is_odd))
    def _():
        both_ref[...] = over_ref[...]

    key_ref, value_ref = both_ref.at[pl.ds(0, toks)], both_ref.at[pl.ds(toks, toks)]
    group = (query_ref, grad_ref, key_ref, value_ref, terms_ref, tile)
    far_work(group, (key_acc, value_acc), scale, span_ids, kept_ref, probs_ref, heads, 2)
    odd = is_odd.astype(jnp.float32)

    def more(away, low, share):
        return swapped[away][low : low + share, :].astype(jnp.float32) * odd

    put_shares(outs, key_acc, value_acc, scale, more=more)


def far_work(group, accs, scale, span_ids, kept_ref, probs_ref, heads, step):
    key_acc, value_acc = accs
    key_acc[...] = jnp.zeros_like(key_acc)
    value_acc[...] = jnp.zeros_like(value_acc)
    half = group[2].shape[0] // 2
    rows = half * heads
    halves = far_halves(span_ids, step)
    blocks = []
    for item in range(2):
        row_half, key_half = halves(item)
        row = pl.multiple_of(row_half * rows, rows)
        key = pl.multiple_of(key_half * half, half)
        blocks.append((row, key, half, kept_ref.at[item], probs_ref.at[item]))
    block_grads(group, accs, scale, rows, blocks)


def join_kernel(*refs):
    count = len(refs) // 3
    even = 1.0 - lax.rem(lax.axis_index("ctx"), 2).astype(jnp.float32)
    for swapped, this, out in zip(refs, refs[count:], refs[2 * count :]):
        more = swapped[...].astype(jnp.float32) * even
        out[...] = (this[...].astype(jnp.float32) + more).astype(out.dtype)


def total_kernel(total_ref, swapped_ref, *refs):
    ins, (key_out, value_out) = refs[:-2], refs[-2:]
    share = key_out.shape[0]
    even = 1.0 - lax.rem(lax.axis_index("ctx"), 2).astype(jnp.float32)
    for low, out in ((0, key_out), (share, value_out)):
        part = total_ref[low : low + share, :]
        part = part + swapped_ref[low : low + share, :].astype(jnp.float32) * even
        for ref in ins:
            part = part + ref[low : low + share, :].astype(jnp.float32)
        out[...] = part.astype(out.dtype)


def query_kernel(heads, tile, scale, span_ids, both_ref, own_ref, *refs):
    (key_1, both_2), kept_refs, (out_ref, acc, turned) = refs[:2], refs[2:-3], refs[-3:]
    toks = both_ref.shape[0] // 2
    half = toks // 2
    rows = half * heads
    per = tile // heads
    for index, key_ref in enumerate((both_ref, key_1, both_2)):
        for low in range(0, toks, half):
            turned[index, :, low : low + half] = key_ref[low : low + half, :].T

    @pl.loop(0, 2)
    def _(index):
        key = pl.multiple_of(index * half, half)
        for p in range(half // per):
            row = pl.multiple_of(index * rows + p * tile, tile)
            length = (p + 1) * per
            acc[:, pl.ds(row, tile)] = dot(
                turned[0, :, pl.ds(key, length)], own_ref[pl.ds(key, length), pl.ds(row, tile)], NN
            )

    first, second = span_pair(span_ids, lax.axis_index("ctx"))
    low = jnp.where(first > second, 1, 0)
    key = pl.multiple_of(low * half, half)
    for p in range(rows // tile):
        row = pl.multiple_of((1 - low) * rows + p * tile, tile)
        acc[:, pl.ds(row, tile)] += dot(
            turned[0, :, pl.ds(key, half)], own_ref[pl.ds(key, half), pl.ds(row, tile)], NN
        )
    for step, kept_ref in enumerate(kept_refs, 1):
        halves = far_halves(span_ids, step)

        @pl.loop(0, 2)
        def _(item):
            row_half, key_half = halves(item)
            key = pl.multiple_of(key_half * half, half)
            for p in range(rows // tile):
                row = pl.multiple_of(row_half * rows + p * tile, tile)
                acc[:, pl.ds(row, tile)] += dot(
                    turned[step, :, pl.ds(key, half)],
                    kept_ref[item, :, p * tile : (p + 1) * tile],
                    NN,
                )

    for row in range(0, 2 * rows, tile):
        out_ref[row : row + tile, :] = (acc[:, row : row + tile] * scale).astype(out_ref.dtype).T


VMEM = pl.BlockSpec(memory_space=pltpu.VMEM)
SMEM = pl.BlockSpec(memory_space=pltpu.SMEM)
HBM = pl.BlockSpec(memory_space=pltpu.HBM)
ANY = pl.BlockSpec(memory_space=pl.ANY)
MIB = 1024 * 1024


def call(kernel, ins, where, outs, scratch, blocks, limit, name, aliases=None):
    flops = blocks * 40 * 512 * 512 * 128
    return pl.pallas_call(
        kernel,
        out_shape=outs,
        in_specs=where,
        out_specs=[VMEM] * len(outs),
        scratch_shapes=scratch,
        input_output_aliases=aliases or {},
        compiler_params=pltpu.CompilerParams(vmem_limit_bytes=limit * MIB),
        name=name,
        cost_estimate=pl.CostEstimate(flops=int(flops), bytes_accessed=int(blocks * (1 << 20)), transcendentals=0),
    )(*ins)


def moved(block, back, away):
    holders, parts = lax.axis_size("ctx"), lax.axis_size("head")
    route = [
        (h * parts + x, ((h - back[h % 2]) % holders) * parts + (x + away) % parts)
        for h in range(holders)
        for x in range(parts)
    ]
    return lax.ppermute(block, ("ctx", "head"), route)


def local(queries, keys, values, outputs, out_grad, log_norm, span_ids):
    toks, heads, dim = queries.shape
    rows = toks * heads
    scale = dim ** (-0.5)
    parts = lax.axis_size("head")
    tile = 512
    q = queries.reshape(rows, dim)
    g = out_grad.reshape(rows, dim)
    o = outputs.reshape(rows, dim)
    share = 2 * toks // parts
    f32, bf16 = jnp.float32, jnp.bfloat16
    shape = jax.ShapeDtypeStruct
    grads = [shape((share, dim), bf16)] * parts
    accs = [pltpu.VMEM((toks, dim), f32)] * 2
    probs = pltpu.VMEM((toks // 2, rows // 2), bf16)

    key_1, value_1 = moved(keys, (-1, -1), 0), moved(values, (-1, -1), 0)
    inputs = tuple(
        pltpu.with_memory_space_constraint(a, pltpu.HBM)
        for a in (g, o, q, log_norm, keys, values, span_ids)
    )
    sums = [shape((toks, rows), bf16), shape((toks, dim), f32), shape((toks, dim), f32)]
    terms, both, kept, key_sum, value_sum = call(
        functools.partial(first_kernel, heads, tile, scale, parts),
        inputs,
        [HBM] * len(inputs),
        [shape((8, rows), f32), shape((2 * toks, dim), bf16)] + sums,
        [pltpu.VMEM(a.shape, a.dtype) for a in inputs[:4]]
        + [probs, pltpu.SMEM(span_ids.shape, span_ids.dtype), pltpu.SemaphoreType.DMA((4, 3))],
        1.625 * heads,
        20,
        "first",
    )
    (both_1,) = call(
        pack_kernel, (key_1, value_1), [VMEM] * 2, [shape((2 * toks, dim), bf16)], [], 0.01, 4, "pack"
    )
    over, beside = moved(both, (-2, 0), 0), moved(both_1, (-1, 1), 0)

    block = (toks // 2, rows // 2)
    kept_1, *sent = call(
        functools.partial(near_kernel, heads, tile, scale, parts),
        (span_ids, q, g, terms, key_1, value_1, key_sum, value_sum, both_1),
        [SMEM] + [VMEM] * 7 + [ANY],
        [shape((2,) + block, bf16)] + grads + grads[1:],
        accs + [pltpu.VMEM((2,) + block, bf16)],
        2 * heads,
        18,
        "near",
    )
    swapped = [moved(part, (-1, 1), 0) for part in sent[:parts]]
    sent = call(
        join_kernel,
        (*swapped[1:], *sent[parts:]),
        [VMEM] * (2 * parts - 2),
        grads[1:],
        [],
        0.01,
        4,
        "join",
    )
    whole = [moved(part, (0, 0), away) for away, part in enumerate(sent, 1)]
    both_2, kept_2, *sent = call(
        functools.partial(far_kernel, heads, tile, scale),
        (span_ids, q, g, terms, over, beside, sent[0], *swapped),
        [SMEM] + [VMEM] * 5 + [ANY] + [VMEM] * parts,
        [shape((2 * toks, dim), bf16), shape((2,) + block, bf16)] + grads,
        accs + [pltpu.VMEM((2,) + block, bf16)],
        2 * heads,
        18,
        "far",
    )
    landed = whole + [moved(part, (2, 2), away) for away, part in enumerate(sent)]
    kept, _, _, total = call(
        functools.partial(last_kernel, heads, tile, scale, parts),
        (span_ids, q, g, terms, both, kept, key_sum, value_sum, sent[0]),
        [SMEM] + [VMEM] * 7 + [ANY],
        sums + [shape((share, dim), f32)],
        [probs],
        1.625 * heads,
        20,
        "last",
        {5: 0, 6: 1, 7: 2},
    )
    (query_grad,) = call(
        functools.partial(query_kernel, heads, tile, scale),
        (span_ids, both, kept, key_1, both_2, kept_1, kept_2),
        [SMEM] + [VMEM] * 6,
        [shape((rows, dim), bf16)],
        [pltpu.VMEM((dim, rows), f32), pltpu.VMEM((STEPS, dim, toks), bf16)],
        0.02 * heads,
        28,
        "queries",
    )
    key_grad, value_grad = call(
        total_kernel,
        (total, swapped[0], *landed),
        [VMEM] * (2 + len(landed)),
        [shape((share // 2, dim), bf16)] * 2,
        [],
        0.01,
        8,
        "total",
    )
    return query_grad.reshape(toks, heads, dim), key_grad, value_grad


def solution(mesh):
    in_specs = (
        P("ctx", "head", None),
        P("ctx", None),
        P("ctx", None),
        P("ctx", "head", None),
        P("ctx", "head", None),
        P("head", "ctx"),
        P(),
    )
    out_specs = (P("ctx", "head", None), P(("ctx", "head"), None), P(("ctx", "head"), None))
    return jax.shard_map(local, mesh=mesh, in_specs=in_specs, out_specs=out_specs, check_vma=False)
```

```python
import functools
import math

import jax
import jax.numpy as jnp
from jax import lax
from jax.experimental import pallas as pl
from jax.experimental.pallas import tpu as pltpu
from jax.sharding import PartitionSpec as P

STEPS = 3
NT = (((1,), (1,)), ((), ()))
NN = (((1,), (0,)), ((), ()))
TN = (((0,), (0,)), ((), ()))


def dot(a, b, dims):
    return lax.dot_general(a, b, dims, preferred_element_type=jnp.float32)


def three_terms(x):
    high = x.astype(jnp.bfloat16)
    rest = x - high.astype(jnp.float32)
    mid = rest.astype(jnp.bfloat16)
    low = (rest - mid.astype(jnp.float32)).astype(jnp.bfloat16)
    return high, mid, low


def row_terms(heads, tile, span, refs, out):
    grad_ref, outputs_ref, norm_ref = refs
    rows = grad_ref.shape[0] // 2
    toks = tile // heads
    spread = (
        lax.broadcasted_iota(jnp.int32, (toks, tile), 1) // heads
        == lax.broadcasted_iota(jnp.int32, (toks, tile), 0)
    ).astype(jnp.bfloat16)
    mine = (
        lax.broadcasted_iota(jnp.int32, (heads, tile), 1) % heads
        == lax.broadcasted_iota(jnp.int32, (heads, tile), 0)
    )
    ones = jnp.ones((8, grad_ref.shape[1]), jnp.bfloat16)
    for index in range(rows // tile):
        tok = pl.multiple_of(span * (rows // heads) + index * toks, toks)
        row = pl.multiple_of(span * rows + index * tile, tile)
        norm = norm_ref[:, pl.ds(tok, toks)] * math.log2(math.e)
        wide = sum(dot(part, spread, NN) for part in three_terms(norm))
        out[0:1, pl.ds(row, tile)] = jnp.sum(jnp.where(mine, wide, 0.0), axis=0, keepdims=True)
        prod = grad_ref[pl.ds(row, tile), :].astype(jnp.float32) * outputs_ref[
            pl.ds(row, tile), :
        ].astype(jnp.float32)
        high = prod.astype(jnp.bfloat16)
        low = (prod - high.astype(jnp.float32)).astype(jnp.bfloat16)
        out[1:2, pl.ds(row, tile)] = (dot(ones, high, NT) + dot(ones, low, NT))[0:1]


def opened(group, row, key, length):
    query_ref, grad_ref, key_ref, value_ref, _, tile = group
    k = key_ref[pl.ds(key, length), :]
    v = value_ref[pl.ds(key, length), :]
    scores = dot(k, query_ref[pl.ds(row, tile), :], NT)
    return scores, dot(v, grad_ref[pl.ds(row, tile), :], NT)


def closed(group, scale, row, triangle, scores, dprob):
    terms_ref, tile = group[4:]
    norm = terms_ref[0:1, pl.ds(row, tile)]
    delta = terms_ref[1:2, pl.ds(row, tile)]
    prob = jnp.exp2(scores * (scale * math.log2(math.e)) - norm)
    if triangle is not None:
        edge = prob.shape[0] - triangle.shape[0]
        last = jnp.where(triangle, prob[edge:], 0.0)
        prob = last if edge == 0 else jnp.concatenate([prob[:edge], last], axis=0)
    return prob.astype(jnp.bfloat16), (prob * (dprob - delta)).astype(jnp.bfloat16)


def triangle_grads(group, accs, scale, row, key, half, triangle, kept_ref):
    query_ref, grad_ref, tile = group[0], group[1], group[-1]
    key_acc, value_acc = accs
    per = triangle.shape[0]
    tiles = [(pl.multiple_of(row + p * tile, tile), (p + 1) * per) for p in range(half // per)]
    ahead = opened(group, tiles[0][0], key, tiles[0][1])
    for index, (row, length) in enumerate(tiles):
        now = ahead
        if index + 1 < len(tiles):
            ahead = opened(group, tiles[index + 1][0], key, tiles[index + 1][1])
        prob, dscore = closed(group, scale, row, triangle, *now)
        kept_ref[pl.ds(key, length), pl.ds(row, tile)] = dscore
        value_acc[pl.ds(key, length), :] += dot(prob, grad_ref[pl.ds(row, tile), :], NN)
        key_acc[pl.ds(key, length), :] += dot(dscore, query_ref[pl.ds(row, tile), :], NN)


def block_grads(group, accs, scale, rows, blocks):
    query_ref, grad_ref, tile = group[0], group[1], 256
    group = group[:-1] + (tile,)
    key_acc, value_acc = accs
    count = rows // tile
    tiles = [(block, p) for block in blocks for p in range(count)]

    def start(block, p):
        row, key, length = block[:3]
        return opened(group, pl.multiple_of(row + p * tile, tile), key, length)

    ahead = start(*tiles[0])
    for index, (block, p) in enumerate(tiles):
        now = ahead
        if index + 1 < len(tiles):
            ahead = start(*tiles[index + 1])
        row, key, length, kept, probs = block
        prob, dscore = closed(group, scale, pl.multiple_of(row + p * tile, tile), None, *now)
        probs[:, p * tile : (p + 1) * tile] = prob
        kept[:, p * tile : (p + 1) * tile] = dscore
        if p == count - 1:
            value_acc[pl.ds(key, length), :] += dot(probs[...], grad_ref[pl.ds(row, rows), :], NN)
            key_acc[pl.ds(key, length), :] += dot(kept[...], query_ref[pl.ds(row, rows), :], NN)


def span_pair(span_ids, holder):
    return span_ids[2 * holder], span_ids[2 * holder + 1]


def far_halves(span_ids, step):
    me, holders = lax.axis_index("ctx"), lax.axis_size("ctx")
    mine = span_pair(span_ids, me)
    theirs = span_pair(span_ids, lax.rem(me + holders - step, holders))
    high_only = jnp.minimum(*mine) < jnp.minimum(*theirs)
    our_high = jnp.where(mine[0] > mine[1], 0, 1)
    their_low = jnp.where(theirs[0] > theirs[1], 1, 0)
    return lambda item: (
        jnp.where(high_only, our_high, item),
        jnp.where(high_only, item, their_low),
    )


def put_shares(outs, key_acc, value_acc, scale, first=0, parts=None, more=None):
    parts = parts or len(outs) + first
    share = key_acc.shape[0] // parts
    x = lax.axis_index("head")
    for away, out in enumerate(outs, first):
        start = pl.multiple_of(lax.rem(x + away, parts) * share, share)
        for low, part in (
            (0, key_acc[pl.ds(start, share), :] * scale),
            (share, value_acc[pl.ds(start, share), :]),
        ):
            if more is not None:
                part = part + more(away, low, share)
            out[low : low + share, :] = part.astype(out.dtype)


def own_work(group, accs, scale, span_ids, kept_ref, probs_ref, heads):
    tile = group[-1]
    toks, rows = kept_ref.shape
    half, span_rows, per = toks // 2, rows // 2, tile // heads
    first, second = span_pair(span_ids, lax.axis_index("ctx"))
    low = jnp.where(first > second, 1, 0)
    triangle = lax.broadcasted_iota(jnp.int32, (per, tile), 0) <= (
        lax.broadcasted_iota(jnp.int32, (per, tile), 1) // heads
    )

    def corner(which):
        key = pl.multiple_of(which * half, half)
        row = pl.multiple_of(which * span_rows, span_rows)
        triangle_grads(group, accs, scale, row, key, half, triangle, kept_ref)

    def square():
        key = pl.multiple_of(low * half, half)
        row = pl.multiple_of((1 - low) * span_rows, span_rows)
        kept = kept_ref.at[pl.ds(key, half), pl.ds(row, span_rows)]
        block_grads(group, accs, scale, span_rows, [(row, key, half, kept, probs_ref)])

    return low, corner, square


def first_kernel(heads, tile, scale, parts, *refs):
    inputs, refs = refs[:7], refs[7:]
    terms_ref, both_ref, kept_ref, key_acc, value_acc = refs[:5]
    held, (probs_ref, span_ids, sems) = refs[5:-3], refs[-3:]
    grad_ref, outputs_ref, query_ref, norm_ref = held
    toks = both_ref.shape[0] // 2
    key_ref, value_ref = both_ref.at[pl.ds(0, toks)], both_ref.at[pl.ds(toks, toks)]
    rows = toks * heads // 2
    whole = [
        pltpu.make_async_copy(a, b, sems.at[i, 2])
        for i, (a, b) in enumerate(zip(inputs[3:], (norm_ref, key_ref, value_ref, span_ids)))
    ]

    def halves(slot, index):
        part = pl.ds(pl.multiple_of(index * rows, rows), rows)
        return [
            pltpu.make_async_copy(inputs[i].at[part], held[i].at[part], sems.at[i, slot])
            for i in range(3)
        ]

    x = lax.axis_index("head")
    order = (1 - x, x) if parts == 2 else (0, 1)
    for copy in whole + halves(0, order[0]) + halves(1, order[1]):
        copy.start()
    key_acc[...] = jnp.zeros_like(key_acc)
    value_acc[...] = jnp.zeros_like(value_acc)
    for copy in whole:
        copy.wait()

    def arrive(slot):
        for copy in halves(slot, order[slot]):
            copy.wait()
        row_terms(heads, tile, order[slot], (grad_ref, outputs_ref, norm_ref), terms_ref)

    group = (query_ref, grad_ref, key_ref, value_ref, terms_ref, tile)
    accs = (key_acc, value_acc)
    low, corner, square = own_work(group, accs, scale, span_ids, kept_ref, probs_ref, heads)
    arrive(0)
    corner(order[0])
    arrive(1)
    if parts != 2:
        corner(order[1])
        square()


def more_kernel(heads, tile, scale, span_ids, *refs):
    kept_ref, key_acc, value_acc, probs_ref = refs[7:]
    x = lax.axis_index("head")
    _, low, corner, square = split_work(
        heads, tile, scale, span_ids, refs[:4], kept_ref, key_acc, value_acc, probs_ref
    )
    pl.when(low != x)(square)
    pl.when(low == x)(lambda: corner(x))


def split_work(heads, tile, scale, span_ids, ins, kept_ref, key_acc, value_acc, probs_ref):
    query_ref, grad_ref, terms_ref, both_ref = ins
    toks = both_ref.shape[0] // 2
    key_ref, value_ref = both_ref.at[pl.ds(0, toks)], both_ref.at[pl.ds(toks, toks)]
    group = (query_ref, grad_ref, key_ref, value_ref, terms_ref, tile)
    accs = (key_acc, value_acc)
    return accs, *own_work(group, accs, scale, span_ids, kept_ref, probs_ref, heads)


def last_kernel(heads, tile, scale, parts, span_ids, *refs):
    kept_ref, key_acc, value_acc, total_ref, probs_ref = refs[8:]
    if parts == 2:
        x = lax.axis_index("head")
        _, low, corner, square = split_work(
            heads, tile, scale, span_ids, refs[:4], kept_ref, key_acc, value_acc, probs_ref
        )
        pl.when(low == x)(square)
        pl.when(low != x)(lambda: corner(x))
    put_shares([total_ref], key_acc, value_acc, scale, 0, parts)


def near_kernel(heads, tile, scale, parts, span_ids, *refs):
    query_ref, grad_ref, terms_ref, key_ref, value_ref, own_keys, own_values, _, kept_ref = refs[:9]
    outs, own_outs, (key_acc, value_acc, probs_ref) = refs[9 : 9 + parts], refs[9 + parts : -3], refs[-3:]
    put_shares(own_outs, own_keys, own_values, scale, 1)
    group = (query_ref, grad_ref, key_ref, value_ref, terms_ref, tile)
    far_work(group, (key_acc, value_acc), scale, span_ids, kept_ref, probs_ref, heads, 1)
    put_shares(outs, key_acc, value_acc, scale)


def pack_kernel(key_ref, value_ref, out_ref):
    toks = key_ref.shape[0]
    out_ref[0:toks, :] = key_ref[...]
    out_ref[toks : 2 * toks, :] = value_ref[...]


def far_kernel(heads, tile, scale, span_ids, *refs):
    query_ref, grad_ref, terms_ref, over_ref, beside_ref, _ = refs[:6]
    parts = (len(refs) - 11) // 2
    swapped, both_ref, kept_ref = refs[6 : 6 + parts], refs[6 + parts], refs[7 + parts]
    outs, (key_acc, value_acc, probs_ref) = refs[8 + parts : -3], refs[-3:]
    toks = both_ref.shape[0] // 2
    is_odd = lax.rem(lax.axis_index("ctx"), 2) == 1

    @pl.when(is_odd)
    def _():
        both_ref[...] = beside_ref[...]

    @pl.when(jnp.logical_not(is_odd))
    def _():
        both_ref[...] = over_ref[...]

    key_ref, value_ref = both_ref.at[pl.ds(0, toks)], both_ref.at[pl.ds(toks, toks)]
    group = (query_ref, grad_ref, key_ref, value_ref, terms_ref, tile)
    far_work(group, (key_acc, value_acc), scale, span_ids, kept_ref, probs_ref, heads, 2)
    odd = is_odd.astype(jnp.float32)

    def more(away, low, share):
        return swapped[away][low : low + share, :].astype(jnp.float32) * odd

    put_shares(outs, key_acc, value_acc, scale, more=more)


def far_work(group, accs, scale, span_ids, kept_ref, probs_ref, heads, step):
    key_acc, value_acc = accs
    key_acc[...] = jnp.zeros_like(key_acc)
    value_acc[...] = jnp.zeros_like(value_acc)
    half = group[2].shape[0] // 2
    rows = half * heads
    halves = far_halves(span_ids, step)
    blocks = []
    for item in range(2):
        row_half, key_half = halves(item)
        row = pl.multiple_of(row_half * rows, rows)
        key = pl.multiple_of(key_half * half, half)
        blocks.append((row, key, half, kept_ref.at[item], probs_ref.at[item]))
    block_grads(group, accs, scale, rows, blocks)


def join_kernel(*refs):
    count = len(refs) // 3
    even = 1.0 - lax.rem(lax.axis_index("ctx"), 2).astype(jnp.float32)
    for swapped, this, out in zip(refs, refs[count:], refs[2 * count :]):
        more = swapped[...].astype(jnp.float32) * even
        out[...] = (this[...].astype(jnp.float32) + more).astype(out.dtype)


def total_kernel(total_ref, swapped_ref, *refs):
    ins, (key_out, value_out) = refs[:-2], refs[-2:]
    share = key_out.shape[0]
    even = 1.0 - lax.rem(lax.axis_index("ctx"), 2).astype(jnp.float32)
    for low, out in ((0, key_out), (share, value_out)):
        part = total_ref[low : low + share, :]
        part = part + swapped_ref[low : low + share, :].astype(jnp.float32) * even
        for ref in ins:
            part = part + ref[low : low + share, :].astype(jnp.float32)
        out[...] = part.astype(out.dtype)


def query_kernel(heads, tile, scale, span_ids, both_ref, own_ref, *refs):
    (key_1, both_2), kept_refs, (out_ref, acc, turned) = refs[:2], refs[2:-3], refs[-3:]
    toks = both_ref.shape[0] // 2
    half = toks // 2
    rows = half * heads
    per = tile // heads
    for index, key_ref in enumerate((both_ref, key_1, both_2)):
        for low in range(0, toks, half):
            turned[index, :, low : low + half] = key_ref[low : low + half, :].T

    @pl.loop(0, 2)
    def _(index):
        key = pl.multiple_of(index * half, half)
        for p in range(half // per):
            row = pl.multiple_of(index * rows + p * tile, tile)
            length = (p + 1) * per
            acc[:, pl.ds(row, tile)] = dot(
                turned[0, :, pl.ds(key, length)], own_ref[pl.ds(key, length), pl.ds(row, tile)], NN
            )

    first, second = span_pair(span_ids, lax.axis_index("ctx"))
    low = jnp.where(first > second, 1, 0)
    key = pl.multiple_of(low * half, half)
    for p in range(rows // tile):
        row = pl.multiple_of((1 - low) * rows + p * tile, tile)
        acc[:, pl.ds(row, tile)] += dot(
            turned[0, :, pl.ds(key, half)], own_ref[pl.ds(key, half), pl.ds(row, tile)], NN
        )
    for step, kept_ref in enumerate(kept_refs, 1):
        halves = far_halves(span_ids, step)

        @pl.loop(0, 2)
        def _(item):
            row_half, key_half = halves(item)
            key = pl.multiple_of(key_half * half, half)
            for p in range(rows // tile):
                row = pl.multiple_of(row_half * rows + p * tile, tile)
                acc[:, pl.ds(row, tile)] += dot(
                    turned[step, :, pl.ds(key, half)],
                    kept_ref[item, :, p * tile : (p + 1) * tile],
                    NN,
                )

    for row in range(0, 2 * rows, tile):
        out_ref[row : row + tile, :] = (acc[:, row : row + tile] * scale).astype(out_ref.dtype).T


VMEM = pl.BlockSpec(memory_space=pltpu.VMEM)
SMEM = pl.BlockSpec(memory_space=pltpu.SMEM)
HBM = pl.BlockSpec(memory_space=pltpu.HBM)
ANY = pl.BlockSpec(memory_space=pl.ANY)
MIB = 1024 * 1024


def call(kernel, ins, where, outs, scratch, blocks, limit, name, aliases=None):
    flops = blocks * 40 * 512 * 512 * 128
    return pl.pallas_call(
        kernel,
        out_shape=outs,
        in_specs=where,
        out_specs=[VMEM] * len(outs),
        scratch_shapes=scratch,
        input_output_aliases=aliases or {},
        compiler_params=pltpu.CompilerParams(vmem_limit_bytes=limit * MIB),
        name=name,
        cost_estimate=pl.CostEstimate(flops=int(flops), bytes_accessed=int(blocks * (1 << 20)), transcendentals=0),
    )(*ins)


def moved(block, back, away):
    holders, parts = lax.axis_size("ctx"), lax.axis_size("head")
    route = [
        (h * parts + x, ((h - back[h % 2]) % holders) * parts + (x + away) % parts)
        for h in range(holders)
        for x in range(parts)
    ]
    return lax.ppermute(block, ("ctx", "head"), route)


def local(queries, keys, values, outputs, out_grad, log_norm, span_ids):
    toks, heads, dim = queries.shape
    rows = toks * heads
    scale = dim ** (-0.5)
    parts = lax.axis_size("head")
    tile = 512
    q = queries.reshape(rows, dim)
    g = out_grad.reshape(rows, dim)
    o = outputs.reshape(rows, dim)
    share = 2 * toks // parts
    f32, bf16 = jnp.float32, jnp.bfloat16
    shape = jax.ShapeDtypeStruct
    grads = [shape((share, dim), bf16)] * parts
    accs = [pltpu.VMEM((toks, dim), f32)] * 2
    probs = pltpu.VMEM((toks // 2, rows // 2), bf16)

    key_1, value_1 = moved(keys, (-1, -1), 0), moved(values, (-1, -1), 0)
    inputs = tuple(
        pltpu.with_memory_space_constraint(a, pltpu.HBM)
        for a in (g, o, q, log_norm, keys, values, span_ids)
    )
    sums = [shape((toks, rows), bf16), shape((toks, dim), f32), shape((toks, dim), f32)]
    terms, both, kept, key_sum, value_sum = call(
        functools.partial(first_kernel, heads, tile, scale, parts),
        inputs,
        [HBM] * len(inputs),
        [shape((8, rows), f32), shape((2 * toks, dim), bf16)] + sums,
        [pltpu.VMEM(a.shape, a.dtype) for a in inputs[:4]]
        + [probs, pltpu.SMEM(span_ids.shape, span_ids.dtype), pltpu.SemaphoreType.DMA((4, 3))],
        1.625 * heads,
        20,
        "first",
    )
    if parts == 2:
        kept, key_sum, value_sum = call(
            functools.partial(more_kernel, heads, tile, scale),
            (span_ids, q, g, terms, both, kept, key_sum, value_sum),
            [SMEM] + [VMEM] * 7,
            sums,
            [probs],
            0.8 * heads,
            20,
            "more",
            {5: 0, 6: 1, 7: 2},
        )
    (both_1,) = call(
        pack_kernel, (key_1, value_1), [VMEM] * 2, [shape((2 * toks, dim), bf16)], [], 0.01, 4, "pack"
    )
    over, beside = moved(both, (-2, 0), 0), moved(both_1, (-1, 1), 0)

    block = (toks // 2, rows // 2)
    kept_1, *sent = call(
        functools.partial(near_kernel, heads, tile, scale, parts),
        (span_ids, q, g, terms, key_1, value_1, key_sum, value_sum, both_1),
        [SMEM] + [VMEM] * 7 + [ANY],
        [shape((2,) + block, bf16)] + grads + grads[1:],
        accs + [pltpu.VMEM((2,) + block, bf16)],
        2 * heads,
        18,
        "near",
    )
    swapped = [moved(part, (-1, 1), 0) for part in sent[:parts]]
    sent = call(
        join_kernel,
        (*swapped[1:], *sent[parts:]),
        [VMEM] * (2 * parts - 2),
        grads[1:],
        [],
        0.01,
        4,
        "join",
    )
    whole = [moved(part, (0, 0), away) for away, part in enumerate(sent, 1)]
    both_2, kept_2, *sent = call(
        functools.partial(far_kernel, heads, tile, scale),
        (span_ids, q, g, terms, over, beside, sent[0], *swapped),
        [SMEM] + [VMEM] * 5 + [ANY] + [VMEM] * parts,
        [shape((2 * toks, dim), bf16), shape((2,) + block, bf16)] + grads,
        accs + [pltpu.VMEM((2,) + block, bf16)],
        2 * heads,
        18,
        "far",
    )
    landed = whole + [moved(part, (2, 2), away) for away, part in enumerate(sent)]
    kept, _, _, total = call(
        functools.partial(last_kernel, heads, tile, scale, parts),
        (span_ids, q, g, terms, both, kept, key_sum, value_sum, sent[0]),
        [SMEM] + [VMEM] * 7 + [ANY],
        sums + [shape((share, dim), f32)],
        [probs],
        1.625 * heads,
        20,
        "last",
        {5: 0, 6: 1, 7: 2},
    )
    (query_grad,) = call(
        functools.partial(query_kernel, heads, tile, scale),
        (span_ids, both, kept, key_1, both_2, kept_1, kept_2),
        [SMEM] + [VMEM] * 6,
        [shape((rows, dim), bf16)],
        [pltpu.VMEM((dim, rows), f32), pltpu.VMEM((STEPS, dim, toks), bf16)],
        0.02 * heads,
        28,
        "queries",
    )
    key_grad, value_grad = call(
        total_kernel,
        (total, swapped[0], *landed),
        [VMEM] * (2 + len(landed)),
        [shape((share // 2, dim), bf16)] * 2,
        [],
        0.01,
        8,
        "total",
    )
    return query_grad.reshape(toks, heads, dim), key_grad, value_grad


def solution(mesh):
    in_specs = (
        P("ctx", "head", None),
        P("ctx", None),
        P("ctx", None),
        P("ctx", "head", None),
        P("ctx", "head", None),
        P("head", "ctx"),
        P(),
    )
    out_specs = (P("ctx", "head", None), P(("ctx", "head"), None), P(("ctx", "head"), None))
    return jax.shard_map(local, mesh=mesh, in_specs=in_specs, out_specs=out_specs, check_vma=False)
```

```python
import functools
import math

import jax
import jax.numpy as jnp
from jax import lax
from jax.experimental import pallas as pl
from jax.experimental.pallas import tpu as pltpu
from jax.sharding import PartitionSpec as P

STEPS = 3
NT = (((1,), (1,)), ((), ()))
NN = (((1,), (0,)), ((), ()))
TN = (((0,), (0,)), ((), ()))


def dot(a, b, dims):
    return lax.dot_general(a, b, dims, preferred_element_type=jnp.float32)


def three_terms(x):
    high = x.astype(jnp.bfloat16)
    rest = x - high.astype(jnp.float32)
    mid = rest.astype(jnp.bfloat16)
    low = (rest - mid.astype(jnp.float32)).astype(jnp.bfloat16)
    return high, mid, low


def row_terms(heads, tile, span, refs, out):
    grad_ref, outputs_ref, norm_ref = refs
    rows = grad_ref.shape[0] // 2
    toks = tile // heads
    spread = (
        lax.broadcasted_iota(jnp.int32, (toks, tile), 1) // heads
        == lax.broadcasted_iota(jnp.int32, (toks, tile), 0)
    ).astype(jnp.bfloat16)
    mine = (
        lax.broadcasted_iota(jnp.int32, (heads, tile), 1) % heads
        == lax.broadcasted_iota(jnp.int32, (heads, tile), 0)
    )
    ones = jnp.ones((8, grad_ref.shape[1]), jnp.bfloat16)
    for index in range(rows // tile):
        tok = pl.multiple_of(span * (rows // heads) + index * toks, toks)
        row = pl.multiple_of(span * rows + index * tile, tile)
        norm = norm_ref[:, pl.ds(tok, toks)] * math.log2(math.e)
        wide = sum(dot(part, spread, NN) for part in three_terms(norm))
        out[0:1, pl.ds(row, tile)] = jnp.sum(jnp.where(mine, wide, 0.0), axis=0, keepdims=True)
        prod = grad_ref[pl.ds(row, tile), :].astype(jnp.float32) * outputs_ref[
            pl.ds(row, tile), :
        ].astype(jnp.float32)
        high = prod.astype(jnp.bfloat16)
        low = (prod - high.astype(jnp.float32)).astype(jnp.bfloat16)
        out[1:2, pl.ds(row, tile)] = (dot(ones, high, NT) + dot(ones, low, NT))[0:1]


def opened(group, row, key, length):
    query_ref, grad_ref, key_ref, value_ref, _, tile = group
    k = key_ref[pl.ds(key, length), :]
    v = value_ref[pl.ds(key, length), :]
    scores = dot(k, query_ref[pl.ds(row, tile), :], NT)
    return scores, dot(v, grad_ref[pl.ds(row, tile), :], NT)


def closed(group, scale, row, triangle, scores, dprob):
    terms_ref, tile = group[4:]
    norm = terms_ref[0:1, pl.ds(row, tile)]
    delta = terms_ref[1:2, pl.ds(row, tile)]
    prob = jnp.exp2(scores * (scale * math.log2(math.e)) - norm)
    if triangle is not None:
        edge = prob.shape[0] - triangle.shape[0]
        last = jnp.where(triangle, prob[edge:], 0.0)
        prob = last if edge == 0 else jnp.concatenate([prob[:edge], last], axis=0)
    return prob.astype(jnp.bfloat16), (prob * (dprob - delta)).astype(jnp.bfloat16)


def triangle_grads(group, accs, scale, row, key, half, triangle, kept_ref):
    query_ref, grad_ref, tile = group[0], group[1], group[-1]
    key_acc, value_acc = accs
    per = triangle.shape[0]
    tiles = [(pl.multiple_of(row + p * tile, tile), (p + 1) * per) for p in range(half // per)]
    ahead = opened(group, tiles[0][0], key, tiles[0][1])
    for index, (row, length) in enumerate(tiles):
        now = ahead
        if index + 1 < len(tiles):
            ahead = opened(group, tiles[index + 1][0], key, tiles[index + 1][1])
        prob, dscore = closed(group, scale, row, triangle, *now)
        kept_ref[pl.ds(key, length), pl.ds(row, tile)] = dscore
        value_acc[pl.ds(key, length), :] += dot(prob, grad_ref[pl.ds(row, tile), :], NN)
        key_acc[pl.ds(key, length), :] += dot(dscore, query_ref[pl.ds(row, tile), :], NN)


def block_grads(group, accs, scale, rows, blocks):
    query_ref, grad_ref, tile = group[0], group[1], 256
    group = group[:-1] + (tile,)
    key_acc, value_acc = accs
    count, depth = rows // tile, 256
    tiles = [
        (block, p, low)
        for block in blocks
        for p in range(count)
        for low in range(0, block[2], depth)
    ]

    def start(block, p, low):
        row, key = block[:2]
        row, key = pl.multiple_of(row + p * tile, tile), pl.multiple_of(key + low, depth)
        return opened(group, row, key, depth)

    ahead = start(*tiles[0])
    for index, (block, p, low) in enumerate(tiles):
        now = ahead
        if index + 1 < len(tiles):
            ahead = start(*tiles[index + 1])
        row, key, length, kept, probs = block
        prob, dscore = closed(group, scale, pl.multiple_of(row + p * tile, tile), None, *now)
        probs[low : low + depth, p * tile : (p + 1) * tile] = prob
        kept[low : low + depth, p * tile : (p + 1) * tile] = dscore
        if p == count - 1 and low == length - depth:
            value_acc[pl.ds(key, length), :] += dot(probs[...], grad_ref[pl.ds(row, rows), :], NN)
            key_acc[pl.ds(key, length), :] += dot(kept[...], query_ref[pl.ds(row, rows), :], NN)


def span_pair(span_ids, holder):
    return span_ids[2 * holder], span_ids[2 * holder + 1]


def far_halves(span_ids, step):
    me, holders = lax.axis_index("ctx"), lax.axis_size("ctx")
    mine = span_pair(span_ids, me)
    theirs = span_pair(span_ids, lax.rem(me + holders - step, holders))
    high_only = jnp.minimum(*mine) < jnp.minimum(*theirs)
    our_high = jnp.where(mine[0] > mine[1], 0, 1)
    their_low = jnp.where(theirs[0] > theirs[1], 1, 0)
    return lambda item: (
        jnp.where(high_only, our_high, item),
        jnp.where(high_only, item, their_low),
    )


def put_shares(outs, key_acc, value_acc, scale, first=0, parts=None, more=None):
    parts = parts or len(outs) + first
    share = key_acc.shape[0] // parts
    x = lax.axis_index("head")
    for away, out in enumerate(outs, first):
        start = pl.multiple_of(lax.rem(x + away, parts) * share, share)
        for low, part in (
            (0, key_acc[pl.ds(start, share), :] * scale),
            (share, value_acc[pl.ds(start, share), :]),
        ):
            if more is not None:
                part = part + more(away, low, share)
            out[low : low + share, :] = part.astype(out.dtype)


def own_work(group, accs, scale, span_ids, kept_ref, probs_ref, heads):
    tile = group[-1]
    toks, rows = kept_ref.shape
    half, span_rows, per = toks // 2, rows // 2, tile // heads
    first, second = span_pair(span_ids, lax.axis_index("ctx"))
    low = jnp.where(first > second, 1, 0)
    triangle = lax.broadcasted_iota(jnp.int32, (per, tile), 0) <= (
        lax.broadcasted_iota(jnp.int32, (per, tile), 1) // heads
    )

    def corner(which):
        key = pl.multiple_of(which * half, half)
        row = pl.multiple_of(which * span_rows, span_rows)
        triangle_grads(group, accs, scale, row, key, half, triangle, kept_ref)

    def square():
        key = pl.multiple_of(low * half, half)
        row = pl.multiple_of((1 - low) * span_rows, span_rows)
        kept = kept_ref.at[pl.ds(key, half), pl.ds(row, span_rows)]
        block_grads(group, accs, scale, span_rows, [(row, key, half, kept, probs_ref)])

    return low, corner, square


def first_kernel(heads, tile, scale, parts, *refs):
    inputs, refs = refs[:7], refs[7:]
    terms_ref, both_ref, kept_ref, key_acc, value_acc = refs[:5]
    held, (probs_ref, span_ids, sems) = refs[5:-3], refs[-3:]
    grad_ref, outputs_ref, query_ref, norm_ref = held
    toks = both_ref.shape[0] // 2
    key_ref, value_ref = both_ref.at[pl.ds(0, toks)], both_ref.at[pl.ds(toks, toks)]
    rows = toks * heads // 2
    whole = [
        pltpu.make_async_copy(a, b, sems.at[i, 2])
        for i, (a, b) in enumerate(zip(inputs[3:], (norm_ref, key_ref, value_ref, span_ids)))
    ]

    def halves(slot, index):
        part = pl.ds(pl.multiple_of(index * rows, rows), rows)
        return [
            pltpu.make_async_copy(inputs[i].at[part], held[i].at[part], sems.at[i, slot])
            for i in range(3)
        ]

    x = lax.axis_index("head")
    order = (1 - x, x) if parts == 2 else (0, 1)
    for copy in whole + halves(0, order[0]) + halves(1, order[1]):
        copy.start()
    key_acc[...] = jnp.zeros_like(key_acc)
    value_acc[...] = jnp.zeros_like(value_acc)
    for copy in whole:
        copy.wait()

    def arrive(slot):
        for copy in halves(slot, order[slot]):
            copy.wait()
        row_terms(heads, tile, order[slot], (grad_ref, outputs_ref, norm_ref), terms_ref)

    group = (query_ref, grad_ref, key_ref, value_ref, terms_ref, tile)
    accs = (key_acc, value_acc)
    low, corner, square = own_work(group, accs, scale, span_ids, kept_ref, probs_ref, heads)
    arrive(0)
    corner(order[0])
    arrive(1)
    if parts == 2:
        pl.when(low == order[0])(square)
        pl.when(low == order[1])(lambda: corner(order[1]))
    else:
        corner(order[1])
        square()


def last_kernel(heads, tile, scale, parts, span_ids, *refs):
    query_ref, grad_ref, terms_ref, both_ref = refs[:4]
    kept_ref, key_acc, value_acc, total_ref, probs_ref = refs[8:]
    if parts == 2:
        toks = both_ref.shape[0] // 2
        key_ref, value_ref = both_ref.at[pl.ds(0, toks)], both_ref.at[pl.ds(toks, toks)]
        group = (query_ref, grad_ref, key_ref, value_ref, terms_ref, tile)
        accs = (key_acc, value_acc)
        x = lax.axis_index("head")
        low, corner, square = own_work(group, accs, scale, span_ids, kept_ref, probs_ref, heads)
        pl.when(low == x)(square)
        pl.when(low != x)(lambda: corner(x))
    put_shares([total_ref], key_acc, value_acc, scale, 0, parts)


def near_kernel(heads, tile, scale, parts, span_ids, *refs):
    query_ref, grad_ref, terms_ref, key_ref, value_ref, own_keys, own_values, _, kept_ref = refs[:9]
    outs, own_outs, (key_acc, value_acc, probs_ref) = refs[9 : 9 + parts], refs[9 + parts : -3], refs[-3:]
    put_shares(own_outs, own_keys, own_values, scale, 1)
    group = (query_ref, grad_ref, key_ref, value_ref, terms_ref, tile)
    far_work(group, (key_acc, value_acc), scale, span_ids, kept_ref, probs_ref, heads, 1)
    put_shares(outs, key_acc, value_acc, scale)


def pack_kernel(key_ref, value_ref, out_ref):
    toks = key_ref.shape[0]
    out_ref[0:toks, :] = key_ref[...]
    out_ref[toks : 2 * toks, :] = value_ref[...]


def far_kernel(heads, tile, scale, span_ids, *refs):
    query_ref, grad_ref, terms_ref, over_ref, beside_ref, _ = refs[:6]
    parts = (len(refs) - 11) // 2
    swapped, both_ref, kept_ref = refs[6 : 6 + parts], refs[6 + parts], refs[7 + parts]
    outs, (key_acc, value_acc, probs_ref) = refs[8 + parts : -3], refs[-3:]
    toks = both_ref.shape[0] // 2
    is_odd = lax.rem(lax.axis_index("ctx"), 2) == 1

    @pl.when(is_odd)
    def _():
        both_ref[...] = beside_ref[...]

    @pl.when(jnp.logical_not(is_odd))
    def _():
        both_ref[...] = over_ref[...]

    key_ref, value_ref = both_ref.at[pl.ds(0, toks)], both_ref.at[pl.ds(toks, toks)]
    group = (query_ref, grad_ref, key_ref, value_ref, terms_ref, tile)
    far_work(group, (key_acc, value_acc), scale, span_ids, kept_ref, probs_ref, heads, 2)
    odd = is_odd.astype(jnp.float32)

    def more(away, low, share):
        return swapped[away][low : low + share, :].astype(jnp.float32) * odd

    put_shares(outs, key_acc, value_acc, scale, more=more)


def far_work(group, accs, scale, span_ids, kept_ref, probs_ref, heads, step):
    key_acc, value_acc = accs
    key_acc[...] = jnp.zeros_like(key_acc)
    value_acc[...] = jnp.zeros_like(value_acc)
    half = group[2].shape[0] // 2
    rows = half * heads
    halves = far_halves(span_ids, step)
    blocks = []
    for item in range(2):
        row_half, key_half = halves(item)
        row = pl.multiple_of(row_half * rows, rows)
        key = pl.multiple_of(key_half * half, half)
        blocks.append((row, key, half, kept_ref.at[item], probs_ref.at[item]))
    block_grads(group, accs, scale, rows, blocks)


def join_kernel(*refs):
    count = len(refs) // 3
    even = 1.0 - lax.rem(lax.axis_index("ctx"), 2).astype(jnp.float32)
    for swapped, this, out in zip(refs, refs[count:], refs[2 * count :]):
        more = swapped[...].astype(jnp.float32) * even
        out[...] = (this[...].astype(jnp.float32) + more).astype(out.dtype)


def total_kernel(total_ref, swapped_ref, *refs):
    ins, (key_out, value_out) = refs[:-2], refs[-2:]
    share = key_out.shape[0]
    even = 1.0 - lax.rem(lax.axis_index("ctx"), 2).astype(jnp.float32)
    for low, out in ((0, key_out), (share, value_out)):
        part = total_ref[low : low + share, :]
        part = part + swapped_ref[low : low + share, :].astype(jnp.float32) * even
        for ref in ins:
            part = part + ref[low : low + share, :].astype(jnp.float32)
        out[...] = part.astype(out.dtype)


def query_kernel(heads, tile, scale, span_ids, both_ref, own_ref, *refs):
    (key_1, both_2), kept_refs, (out_ref, acc, turned) = refs[:2], refs[2:-3], refs[-3:]
    toks = both_ref.shape[0] // 2
    half = toks // 2
    rows = half * heads
    per = tile // heads
    for index, key_ref in enumerate((both_ref, key_1, both_2)):
        for low in range(0, toks, half):
            turned[index, :, low : low + half] = key_ref[low : low + half, :].T

    @pl.loop(0, 2)
    def _(index):
        key = pl.multiple_of(index * half, half)
        for p in range(half // per):
            row = pl.multiple_of(index * rows + p * tile, tile)
            length = (p + 1) * per
            acc[:, pl.ds(row, tile)] = dot(
                turned[0, :, pl.ds(key, length)], own_ref[pl.ds(key, length), pl.ds(row, tile)], NN
            )

    first, second = span_pair(span_ids, lax.axis_index("ctx"))
    low = jnp.where(first > second, 1, 0)
    key = pl.multiple_of(low * half, half)
    for p in range(rows // tile):
        row = pl.multiple_of((1 - low) * rows + p * tile, tile)
        acc[:, pl.ds(row, tile)] += dot(
            turned[0, :, pl.ds(key, half)], own_ref[pl.ds(key, half), pl.ds(row, tile)], NN
        )
    for step, kept_ref in enumerate(kept_refs, 1):
        halves = far_halves(span_ids, step)

        @pl.loop(0, 2)
        def _(item):
            row_half, key_half = halves(item)
            key = pl.multiple_of(key_half * half, half)
            for p in range(rows // tile):
                row = pl.multiple_of(row_half * rows + p * tile, tile)
                acc[:, pl.ds(row, tile)] += dot(
                    turned[step, :, pl.ds(key, half)],
                    kept_ref[item, :, p * tile : (p + 1) * tile],
                    NN,
                )

    for row in range(0, 2 * rows, tile):
        out_ref[row : row + tile, :] = (acc[:, row : row + tile] * scale).astype(out_ref.dtype).T


VMEM = pl.BlockSpec(memory_space=pltpu.VMEM)
SMEM = pl.BlockSpec(memory_space=pltpu.SMEM)
HBM = pl.BlockSpec(memory_space=pltpu.HBM)
ANY = pl.BlockSpec(memory_space=pl.ANY)
MIB = 1024 * 1024


def call(kernel, ins, where, outs, scratch, blocks, limit, name, aliases=None):
    flops = blocks * 40 * 512 * 512 * 128
    return pl.pallas_call(
        kernel,
        out_shape=outs,
        in_specs=where,
        out_specs=[VMEM] * len(outs),
        scratch_shapes=scratch,
        input_output_aliases=aliases or {},
        compiler_params=pltpu.CompilerParams(vmem_limit_bytes=limit * MIB),
        name=name,
        cost_estimate=pl.CostEstimate(flops=int(flops), bytes_accessed=int(blocks * (1 << 20)), transcendentals=0),
    )(*ins)


def moved(block, back, away):
    holders, parts = lax.axis_size("ctx"), lax.axis_size("head")
    route = [
        (h * parts + x, ((h - back[h % 2]) % holders) * parts + (x + away) % parts)
        for h in range(holders)
        for x in range(parts)
    ]
    return lax.ppermute(block, ("ctx", "head"), route)


def local(queries, keys, values, outputs, out_grad, log_norm, span_ids):
    toks, heads, dim = queries.shape
    rows = toks * heads
    scale = dim ** (-0.5)
    parts = lax.axis_size("head")
    tile = 512
    q = queries.reshape(rows, dim)
    g = out_grad.reshape(rows, dim)
    o = outputs.reshape(rows, dim)
    share = 2 * toks // parts
    f32, bf16 = jnp.float32, jnp.bfloat16
    shape = jax.ShapeDtypeStruct
    grads = [shape((share, dim), bf16)] * parts
    accs = [pltpu.VMEM((toks, dim), f32)] * 2
    probs = pltpu.VMEM((toks // 2, rows // 2), bf16)

    key_1, value_1 = moved(keys, (-1, -1), 0), moved(values, (-1, -1), 0)
    inputs = tuple(
        pltpu.with_memory_space_constraint(a, pltpu.HBM)
        for a in (g, o, q, log_norm, keys, values, span_ids)
    )
    sums = [shape((toks, rows), bf16), shape((toks, dim), f32), shape((toks, dim), f32)]
    terms, both, kept, key_sum, value_sum = call(
        functools.partial(first_kernel, heads, tile, scale, parts),
        inputs,
        [HBM] * len(inputs),
        [shape((8, rows), f32), shape((2 * toks, dim), bf16)] + sums,
        [pltpu.VMEM(a.shape, a.dtype) for a in inputs[:4]]
        + [probs, pltpu.SMEM(span_ids.shape, span_ids.dtype), pltpu.SemaphoreType.DMA((4, 3))],
        1.625 * heads,
        20,
        "first",
    )
    (both_1,) = call(
        pack_kernel, (key_1, value_1), [VMEM] * 2, [shape((2 * toks, dim), bf16)], [], 0.01, 4, "pack"
    )
    over, beside = moved(both, (-2, 0), 0), moved(both_1, (-1, 1), 0)

    block = (toks // 2, rows // 2)
    kept_1, *sent = call(
        functools.partial(near_kernel, heads, tile, scale, parts),
        (span_ids, q, g, terms, key_1, value_1, key_sum, value_sum, both_1),
        [SMEM] + [VMEM] * 7 + [ANY],
        [shape((2,) + block, bf16)] + grads + grads[1:],
        accs + [pltpu.VMEM((2,) + block, bf16)],
        2 * heads,
        18,
        "near",
    )
    swapped = [moved(part, (-1, 1), 0) for part in sent[:parts]]
    sent = call(
        join_kernel,
        (*swapped[1:], *sent[parts:]),
        [VMEM] * (2 * parts - 2),
        grads[1:],
        [],
        0.01,
        4,
        "join",
    )
    whole = [moved(part, (0, 0), away) for away, part in enumerate(sent, 1)]
    both_2, kept_2, *sent = call(
        functools.partial(far_kernel, heads, tile, scale),
        (span_ids, q, g, terms, over, beside, sent[0], *swapped),
        [SMEM] + [VMEM] * 5 + [ANY] + [VMEM] * parts,
        [shape((2 * toks, dim), bf16), shape((2,) + block, bf16)] + grads,
        accs + [pltpu.VMEM((2,) + block, bf16)],
        2 * heads,
        18,
        "far",
    )
    landed = whole + [moved(part, (2, 2), away) for away, part in enumerate(sent)]
    kept, _, _, total = call(
        functools.partial(last_kernel, heads, tile, scale, parts),
        (span_ids, q, g, terms, both, kept, key_sum, value_sum, sent[0]),
        [SMEM] + [VMEM] * 7 + [ANY],
        sums + [shape((share, dim), f32)],
        [probs],
        1.625 * heads,
        20,
        "last",
        {5: 0, 6: 1, 7: 2},
    )
    (query_grad,) = call(
        functools.partial(query_kernel, heads, tile, scale),
        (span_ids, both, kept, key_1, both_2, kept_1, kept_2),
        [SMEM] + [VMEM] * 6,
        [shape((rows, dim), bf16)],
        [pltpu.VMEM((dim, rows), f32), pltpu.VMEM((STEPS, dim, toks), bf16)],
        0.02 * heads,
        28,
        "queries",
    )
    key_grad, value_grad = call(
        total_kernel,
        (total, swapped[0], *landed),
        [VMEM] * (2 + len(landed)),
        [shape((share // 2, dim), bf16)] * 2,
        [],
        0.01,
        8,
        "total",
    )
    return query_grad.reshape(toks, heads, dim), key_grad, value_grad


def solution(mesh):
    in_specs = (
        P("ctx", "head", None),
        P("ctx", None),
        P("ctx", None),
        P("ctx", "head", None),
        P("ctx", "head", None),
        P("head", "ctx"),
        P(),
    )
    out_specs = (P("ctx", "head", None), P(("ctx", "head"), None), P(("ctx", "head"), None))
    return jax.shard_map(local, mesh=mesh, in_specs=in_specs, out_specs=out_specs, check_vma=False)
```

```python
import functools
import math

import jax
import jax.numpy as jnp
from jax import lax
from jax.experimental import pallas as pl
from jax.experimental.pallas import tpu as pltpu
from jax.sharding import PartitionSpec as P

STEPS = 3
NT = (((1,), (1,)), ((), ()))
NN = (((1,), (0,)), ((), ()))
TN = (((0,), (0,)), ((), ()))


def dot(a, b, dims):
    return lax.dot_general(a, b, dims, preferred_element_type=jnp.float32)


def three_terms(x):
    high = x.astype(jnp.bfloat16)
    rest = x - high.astype(jnp.float32)
    mid = rest.astype(jnp.bfloat16)
    low = (rest - mid.astype(jnp.float32)).astype(jnp.bfloat16)
    return high, mid, low


def row_terms(heads, tile, span, refs, out):
    grad_ref, outputs_ref, norm_ref = refs
    rows = grad_ref.shape[0] // 2
    toks = tile // heads
    spread = (
        lax.broadcasted_iota(jnp.int32, (toks, tile), 1) // heads
        == lax.broadcasted_iota(jnp.int32, (toks, tile), 0)
    ).astype(jnp.bfloat16)
    mine = (
        lax.broadcasted_iota(jnp.int32, (heads, tile), 1) % heads
        == lax.broadcasted_iota(jnp.int32, (heads, tile), 0)
    )
    ones = jnp.ones((8, grad_ref.shape[1]), jnp.bfloat16)
    for index in range(rows // tile):
        tok = pl.multiple_of(span * (rows // heads) + index * toks, toks)
        row = pl.multiple_of(span * rows + index * tile, tile)
        norm = norm_ref[:, pl.ds(tok, toks)] * math.log2(math.e)
        wide = sum(dot(part, spread, NN) for part in three_terms(norm))
        out[0:1, pl.ds(row, tile)] = jnp.sum(jnp.where(mine, wide, 0.0), axis=0, keepdims=True)
        prod = grad_ref[pl.ds(row, tile), :].astype(jnp.float32) * outputs_ref[
            pl.ds(row, tile), :
        ].astype(jnp.float32)
        high = prod.astype(jnp.bfloat16)
        low = (prod - high.astype(jnp.float32)).astype(jnp.bfloat16)
        out[1:2, pl.ds(row, tile)] = (dot(ones, high, NT) + dot(ones, low, NT))[0:1]


def opened(group, row, key, length):
    query_ref, grad_ref, key_ref, value_ref, _, tile = group
    k = key_ref[pl.ds(key, length), :]
    v = value_ref[pl.ds(key, length), :]
    scores = dot(k, query_ref[pl.ds(row, tile), :], NT)
    return scores, dot(v, grad_ref[pl.ds(row, tile), :], NT)


def closed(group, scale, row, triangle, scores, dprob):
    terms_ref, tile = group[4:]
    norm = terms_ref[0:1, pl.ds(row, tile)]
    delta = terms_ref[1:2, pl.ds(row, tile)]
    prob = jnp.exp2(scores * (scale * math.log2(math.e)) - norm)
    if triangle is not None:
        edge = prob.shape[0] - triangle.shape[0]
        last = jnp.where(triangle, prob[edge:], 0.0)
        prob = last if edge == 0 else jnp.concatenate([prob[:edge], last], axis=0)
    return prob.astype(jnp.bfloat16), (prob * (dprob - delta)).astype(jnp.bfloat16)


def triangle_grads(group, accs, scale, row, key, half, triangle, kept_ref):
    query_ref, grad_ref, tile = group[0], group[1], group[-1]
    key_acc, value_acc = accs
    per = triangle.shape[0]
    tiles = [(pl.multiple_of(row + p * tile, tile), (p + 1) * per) for p in range(half // per)]
    ahead = opened(group, tiles[0][0], key, tiles[0][1])
    for index, (row, length) in enumerate(tiles):
        now = ahead
        if index + 1 < len(tiles):
            ahead = opened(group, tiles[index + 1][0], key, tiles[index + 1][1])
        prob, dscore = closed(group, scale, row, triangle, *now)
        kept_ref[pl.ds(key, length), pl.ds(row, tile)] = dscore
        value_acc[pl.ds(key, length), :] += dot(prob, grad_ref[pl.ds(row, tile), :], NN)
        key_acc[pl.ds(key, length), :] += dot(dscore, query_ref[pl.ds(row, tile), :], NN)


def block_grads(group, accs, scale, rows, blocks):
    query_ref, grad_ref, tile = group[0], group[1], 256
    group = group[:-1] + (tile,)
    key_acc, value_acc = accs
    count, depth = rows // tile, 256
    tiles = [
        (block, p, low)
        for block in blocks
        for p in range(count)
        for low in range(0, block[2], depth)
    ]

    def start(block, p, low):
        row, key = block[:2]
        row, key = pl.multiple_of(row + p * tile, tile), pl.multiple_of(key + low, depth)
        return opened(group, row, key, depth)

    ahead = start(*tiles[0])
    for index, (block, p, low) in enumerate(tiles):
        now = ahead
        if index + 1 < len(tiles):
            ahead = start(*tiles[index + 1])
        row, key, length, kept, probs = block
        prob, dscore = closed(group, scale, pl.multiple_of(row + p * tile, tile), None, *now)
        probs[low : low + depth, p * tile : (p + 1) * tile] = prob
        kept[low : low + depth, p * tile : (p + 1) * tile] = dscore
        if p == count - 1 and low == length - depth:
            value_acc[pl.ds(key, length), :] += dot(probs[...], grad_ref[pl.ds(row, rows), :], NN)
            key_acc[pl.ds(key, length), :] += dot(kept[...], query_ref[pl.ds(row, rows), :], NN)


def span_pair(span_ids, holder):
    return span_ids[2 * holder], span_ids[2 * holder + 1]


def far_halves(span_ids, step):
    me, holders = lax.axis_index("ctx"), lax.axis_size("ctx")
    mine = span_pair(span_ids, me)
    theirs = span_pair(span_ids, lax.rem(me + holders - step, holders))
    high_only = jnp.minimum(*mine) < jnp.minimum(*theirs)
    our_high = jnp.where(mine[0] > mine[1], 0, 1)
    their_low = jnp.where(theirs[0] > theirs[1], 1, 0)
    return lambda item: (
        jnp.where(high_only, our_high, item),
        jnp.where(high_only, item, their_low),
    )


def put_shares(outs, key_acc, value_acc, scale, first=0, parts=None, more=None):
    parts = parts or len(outs) + first
    share = key_acc.shape[0] // parts
    x = lax.axis_index("head")
    for away, out in enumerate(outs, first):
        start = pl.multiple_of(lax.rem(x + away, parts) * share, share)
        for low, part in (
            (0, key_acc[pl.ds(start, share), :] * scale),
            (share, value_acc[pl.ds(start, share), :]),
        ):
            if more is not None:
                part = part + more(away, low, share)
            out[low : low + share, :] = part.astype(out.dtype)


def own_work(group, accs, scale, span_ids, kept_ref, probs_ref, heads):
    tile = group[-1]
    toks, rows = kept_ref.shape
    half, span_rows, per = toks // 2, rows // 2, tile // heads
    first, second = span_pair(span_ids, lax.axis_index("ctx"))
    low = jnp.where(first > second, 1, 0)
    triangle = lax.broadcasted_iota(jnp.int32, (per, tile), 0) <= (
        lax.broadcasted_iota(jnp.int32, (per, tile), 1) // heads
    )

    def corner(which):
        key = pl.multiple_of(which * half, half)
        row = pl.multiple_of(which * span_rows, span_rows)
        triangle_grads(group, accs, scale, row, key, half, triangle, kept_ref)

    def square():
        key = pl.multiple_of(low * half, half)
        row = pl.multiple_of((1 - low) * span_rows, span_rows)
        kept = kept_ref.at[pl.ds(key, half), pl.ds(row, span_rows)]
        block_grads(group, accs, scale, span_rows, [(row, key, half, kept, probs_ref)])

    return low, corner, square


def first_kernel(heads, tile, scale, parts, *refs):
    inputs, refs = refs[:7], refs[7:]
    terms_ref, both_ref, kept_ref, key_acc, value_acc = refs[:5]
    held, (probs_ref, span_ids, sems) = refs[5:-3], refs[-3:]
    grad_ref, outputs_ref, query_ref, norm_ref = held
    toks = both_ref.shape[0] // 2
    key_ref, value_ref = both_ref.at[pl.ds(0, toks)], both_ref.at[pl.ds(toks, toks)]
    rows = toks * heads // 2
    whole = [
        pltpu.make_async_copy(a, b, sems.at[i, 2])
        for i, (a, b) in enumerate(zip(inputs[3:], (norm_ref, key_ref, value_ref, span_ids)))
    ]

    def halves(slot, index):
        part = pl.ds(pl.multiple_of(index * rows, rows), rows)
        return [
            pltpu.make_async_copy(inputs[i].at[part], held[i].at[part], sems.at[i, slot])
            for i in range(3)
        ]

    x = lax.axis_index("head")
    order = (1 - x, x) if parts == 2 else (0, 1)
    for copy in whole + halves(0, order[0]) + halves(1, order[1]):
        copy.start()
    key_acc[...] = jnp.zeros_like(key_acc)
    value_acc[...] = jnp.zeros_like(value_acc)
    for copy in whole:
        copy.wait()

    def arrive(slot):
        for copy in halves(slot, order[slot]):
            copy.wait()
        row_terms(heads, tile, order[slot], (grad_ref, outputs_ref, norm_ref), terms_ref)

    group = (query_ref, grad_ref, key_ref, value_ref, terms_ref, tile)
    accs = (key_acc, value_acc)
    low, corner, square = own_work(group, accs, scale, span_ids, kept_ref, probs_ref, heads)
    arrive(0)
    corner(order[0])
    arrive(1)
    if parts == 2:
        pl.when(low == order[0])(square)
        pl.when(low == order[1])(lambda: corner(order[1]))
    else:
        corner(order[1])
        square()


def last_kernel(heads, tile, scale, parts, span_ids, *refs):
    query_ref, grad_ref, terms_ref, both_ref = refs[:4]
    kept_ref, key_acc, value_acc, total_ref, probs_ref = refs[8:]
    if parts == 2:
        toks = both_ref.shape[0] // 2
        key_ref, value_ref = both_ref.at[pl.ds(0, toks)], both_ref.at[pl.ds(toks, toks)]
        group = (query_ref, grad_ref, key_ref, value_ref, terms_ref, tile)
        accs = (key_acc, value_acc)
        x = lax.axis_index("head")
        low, corner, square = own_work(group, accs, scale, span_ids, kept_ref, probs_ref, heads)
        pl.when(low == x)(square)
        pl.when(low != x)(lambda: corner(x))
    put_shares([total_ref], key_acc, value_acc, scale, 0, parts)


def near_kernel(heads, tile, scale, parts, span_ids, *refs):
    query_ref, grad_ref, terms_ref, key_ref, value_ref, own_keys, own_values, _, kept_ref = refs[:9]
    outs, own_outs, (key_acc, value_acc, probs_ref) = refs[9 : 9 + parts], refs[9 + parts : -3], refs[-3:]
    put_shares(own_outs, own_keys, own_values, scale, 1)
    group = (query_ref, grad_ref, key_ref, value_ref, terms_ref, tile)
    far_work(group, (key_acc, value_acc), scale, span_ids, kept_ref, probs_ref, heads, 1)
    put_shares(outs, key_acc, value_acc, scale)


def pack_kernel(key_ref, value_ref, out_ref):
    toks = key_ref.shape[0]
    out_ref[0:toks, :] = key_ref[...]
    out_ref[toks : 2 * toks, :] = value_ref[...]


def far_kernel(heads, tile, scale, span_ids, *refs):
    query_ref, grad_ref, terms_ref, over_ref, beside_ref, _ = refs[:6]
    parts = (len(refs) - 11) // 2
    swapped, both_ref, kept_ref = refs[6 : 6 + parts], refs[6 + parts], refs[7 + parts]
    outs, (key_acc, value_acc, probs_ref) = refs[8 + parts : -3], refs[-3:]
    toks = both_ref.shape[0] // 2
    is_odd = lax.rem(lax.axis_index("ctx"), 2) == 1

    @pl.when(is_odd)
    def _():
        both_ref[...] = beside_ref[...]

    @pl.when(jnp.logical_not(is_odd))
    def _():
        both_ref[...] = over_ref[...]

    key_ref, value_ref = both_ref.at[pl.ds(0, toks)], both_ref.at[pl.ds(toks, toks)]
    group = (query_ref, grad_ref, key_ref, value_ref, terms_ref, tile)
    far_work(group, (key_acc, value_acc), scale, span_ids, kept_ref, probs_ref, heads, 2)

    def more(away, low, share):
        return jnp.where(is_odd, swapped[away][low : low + share, :].astype(jnp.float32), 0.0)

    put_shares(outs, key_acc, value_acc, scale, more=more)


def far_work(group, accs, scale, span_ids, kept_ref, probs_ref, heads, step):
    key_acc, value_acc = accs
    key_acc[...] = jnp.zeros_like(key_acc)
    value_acc[...] = jnp.zeros_like(value_acc)
    half = group[2].shape[0] // 2
    rows = half * heads
    halves = far_halves(span_ids, step)
    blocks = []
    for item in range(2):
        row_half, key_half = halves(item)
        row = pl.multiple_of(row_half * rows, rows)
        key = pl.multiple_of(key_half * half, half)
        blocks.append((row, key, half, kept_ref.at[item], probs_ref.at[item]))
    block_grads(group, accs, scale, rows, blocks)


def join_kernel(*refs):
    count = len(refs) // 3
    even = lax.rem(lax.axis_index("ctx"), 2) == 0
    for swapped, this, out in zip(refs, refs[count:], refs[2 * count :]):
        more = jnp.where(even, swapped[...].astype(jnp.float32), 0.0)
        out[...] = (this[...].astype(jnp.float32) + more).astype(out.dtype)


def total_kernel(total_ref, swapped_ref, *refs):
    ins, (key_out, value_out) = refs[:-2], refs[-2:]
    share = key_out.shape[0]
    even = lax.rem(lax.axis_index("ctx"), 2) == 0
    for low, out in ((0, key_out), (share, value_out)):
        part = total_ref[low : low + share, :]
        part = part + jnp.where(even, swapped_ref[low : low + share, :].astype(jnp.float32), 0.0)
        for ref in ins:
            part = part + ref[low : low + share, :].astype(jnp.float32)
        out[...] = part.astype(out.dtype)


def query_kernel(heads, tile, scale, span_ids, both_ref, own_ref, *refs):
    (key_1, both_2), kept_refs, (out_ref, acc, turned) = refs[:2], refs[2:-3], refs[-3:]
    toks = both_ref.shape[0] // 2
    half = toks // 2
    rows = half * heads
    per = tile // heads
    for index, key_ref in enumerate((both_ref, key_1, both_2)):
        for low in range(0, toks, half):
            turned[index, :, low : low + half] = key_ref[low : low + half, :].T

    @pl.loop(0, 2)
    def _(index):
        key = pl.multiple_of(index * half, half)
        for p in range(half // per):
            row = pl.multiple_of(index * rows + p * tile, tile)
            length = (p + 1) * per
            acc[:, pl.ds(row, tile)] = dot(
                turned[0, :, pl.ds(key, length)], own_ref[pl.ds(key, length), pl.ds(row, tile)], NN
            )

    first, second = span_pair(span_ids, lax.axis_index("ctx"))
    low = jnp.where(first > second, 1, 0)
    key = pl.multiple_of(low * half, half)
    for p in range(rows // tile):
        row = pl.multiple_of((1 - low) * rows + p * tile, tile)
        acc[:, pl.ds(row, tile)] += dot(
            turned[0, :, pl.ds(key, half)], own_ref[pl.ds(key, half), pl.ds(row, tile)], NN
        )
    for step, kept_ref in enumerate(kept_refs, 1):
        halves = far_halves(span_ids, step)

        @pl.loop(0, 2)
        def _(item):
            row_half, key_half = halves(item)
            key = pl.multiple_of(key_half * half, half)
            for p in range(rows // tile):
                row = pl.multiple_of(row_half * rows + p * tile, tile)
                acc[:, pl.ds(row, tile)] += dot(
                    turned[step, :, pl.ds(key, half)],
                    kept_ref[item, :, p * tile : (p + 1) * tile],
                    NN,
                )

    for row in range(0, 2 * rows, tile):
        out_ref[row : row + tile, :] = (acc[:, row : row + tile] * scale).astype(out_ref.dtype).T


VMEM = pl.BlockSpec(memory_space=pltpu.VMEM)
SMEM = pl.BlockSpec(memory_space=pltpu.SMEM)
HBM = pl.BlockSpec(memory_space=pltpu.HBM)
ANY = pl.BlockSpec(memory_space=pl.ANY)
MIB = 1024 * 1024


def call(kernel, ins, where, outs, scratch, blocks, limit, name, aliases=None):
    flops = blocks * 40 * 512 * 512 * 128
    return pl.pallas_call(
        kernel,
        out_shape=outs,
        in_specs=where,
        out_specs=[VMEM] * len(outs),
        scratch_shapes=scratch,
        input_output_aliases=aliases or {},
        compiler_params=pltpu.CompilerParams(vmem_limit_bytes=limit * MIB),
        name=name,
        cost_estimate=pl.CostEstimate(flops=int(flops), bytes_accessed=int(blocks * (1 << 20)), transcendentals=0),
    )(*ins)


def moved(block, back, away):
    holders, parts = lax.axis_size("ctx"), lax.axis_size("head")
    route = [
        (h * parts + x, ((h - back[h % 2]) % holders) * parts + (x + away) % parts)
        for h in range(holders)
        for x in range(parts)
    ]
    return lax.ppermute(block, ("ctx", "head"), route)


def local(queries, keys, values, outputs, out_grad, log_norm, span_ids):
    toks, heads, dim = queries.shape
    rows = toks * heads
    scale = dim ** (-0.5)
    parts = lax.axis_size("head")
    tile = 512
    q = queries.reshape(rows, dim)
    g = out_grad.reshape(rows, dim)
    o = outputs.reshape(rows, dim)
    share = 2 * toks // parts
    f32, bf16 = jnp.float32, jnp.bfloat16
    shape = jax.ShapeDtypeStruct
    grads = [shape((share, dim), bf16)] * parts
    accs = [pltpu.VMEM((toks, dim), f32)] * 2
    probs = pltpu.VMEM((toks // 2, rows // 2), bf16)

    key_1, value_1 = moved(keys, (-1, -1), 0), moved(values, (-1, -1), 0)
    inputs = tuple(
        pltpu.with_memory_space_constraint(a, pltpu.HBM)
        for a in (g, o, q, log_norm, keys, values, span_ids)
    )
    sums = [shape((toks, rows), bf16), shape((toks, dim), f32), shape((toks, dim), f32)]
    terms, both, kept, key_sum, value_sum = call(
        functools.partial(first_kernel, heads, tile, scale, parts),
        inputs,
        [HBM] * len(inputs),
        [shape((8, rows), f32), shape((2 * toks, dim), bf16)] + sums,
        [pltpu.VMEM(a.shape, a.dtype) for a in inputs[:4]]
        + [probs, pltpu.SMEM(span_ids.shape, span_ids.dtype), pltpu.SemaphoreType.DMA((4, 3))],
        1.625 * heads,
        20,
        "first",
    )
    (both_1,) = call(
        pack_kernel, (key_1, value_1), [VMEM] * 2, [shape((2 * toks, dim), bf16)], [], 0.01, 4, "pack"
    )
    over, beside = moved(both, (-2, 0), 0), moved(both_1, (-1, 1), 0)

    block = (toks // 2, rows // 2)
    kept_1, *sent = call(
        functools.partial(near_kernel, heads, tile, scale, parts),
        (span_ids, q, g, terms, key_1, value_1, key_sum, value_sum, both_1),
        [SMEM] + [VMEM] * 7 + [ANY],
        [shape((2,) + block, bf16)] + grads + grads[1:],
        accs + [pltpu.VMEM((2,) + block, bf16)],
        2 * heads,
        18,
        "near",
    )
    swapped = [moved(part, (-1, 1), 0) for part in sent[:parts]]
    sent = call(
        join_kernel,
        (*swapped[1:], *sent[parts:]),
        [VMEM] * (2 * parts - 2),
        grads[1:],
        [],
        0.01,
        4,
        "join",
    )
    whole = [moved(part, (0, 0), away) for away, part in enumerate(sent, 1)]
    both_2, kept_2, *sent = call(
        functools.partial(far_kernel, heads, tile, scale),
        (span_ids, q, g, terms, over, beside, sent[0], *swapped),
        [SMEM] + [VMEM] * 5 + [ANY] + [VMEM] * parts,
        [shape((2 * toks, dim), bf16), shape((2,) + block, bf16)] + grads,
        accs + [pltpu.VMEM((2,) + block, bf16)],
        2 * heads,
        18,
        "far",
    )
    landed = whole + [moved(part, (2, 2), away) for away, part in enumerate(sent)]
    kept, _, _, total = call(
        functools.partial(last_kernel, heads, tile, scale, parts),
        (span_ids, q, g, terms, both, kept, key_sum, value_sum, sent[0]),
        [SMEM] + [VMEM] * 7 + [ANY],
        sums + [shape((share, dim), f32)],
        [probs],
        1.625 * heads,
        20,
        "last",
        {5: 0, 6: 1, 7: 2},
    )
    (query_grad,) = call(
        functools.partial(query_kernel, heads, tile, scale),
        (span_ids, both, kept, key_1, both_2, kept_1, kept_2),
        [SMEM] + [VMEM] * 6,
        [shape((rows, dim), bf16)],
        [pltpu.VMEM((dim, rows), f32), pltpu.VMEM((STEPS, dim, toks), bf16)],
        0.02 * heads,
        28,
        "queries",
    )
    key_grad, value_grad = call(
        total_kernel,
        (total, swapped[0], *landed),
        [VMEM] * (2 + len(landed)),
        [shape((share // 2, dim), bf16)] * 2,
        [],
        0.01,
        8,
        "total",
    )
    return query_grad.reshape(toks, heads, dim), key_grad, value_grad


def solution(mesh):
    in_specs = (
        P("ctx", "head", None),
        P("ctx", None),
        P("ctx", None),
        P("ctx", "head", None),
        P("ctx", "head", None),
        P("head", "ctx"),
        P(),
    )
    out_specs = (P("ctx", "head", None), P(("ctx", "head"), None), P(("ctx", "head"), None))
    return jax.shard_map(local, mesh=mesh, in_specs=in_specs, out_specs=out_specs, check_vma=False)
```

```python
import functools
import math

import jax
import jax.numpy as jnp
from jax import lax
from jax.experimental import pallas as pl
from jax.experimental.pallas import tpu as pltpu
from jax.sharding import PartitionSpec as P

STEPS = 3
NT = (((1,), (1,)), ((), ()))
NN = (((1,), (0,)), ((), ()))
TN = (((0,), (0,)), ((), ()))


def dot(a, b, dims):
    return lax.dot_general(a, b, dims, preferred_element_type=jnp.float32)


def three_terms(x):
    high = x.astype(jnp.bfloat16)
    rest = x - high.astype(jnp.float32)
    mid = rest.astype(jnp.bfloat16)
    low = (rest - mid.astype(jnp.float32)).astype(jnp.bfloat16)
    return high, mid, low


def row_terms(heads, tile, span, refs, out):
    grad_ref, outputs_ref, norm_ref = refs
    rows = grad_ref.shape[0] // 2
    toks = tile // heads
    spread = (
        lax.broadcasted_iota(jnp.int32, (toks, tile), 1) // heads
        == lax.broadcasted_iota(jnp.int32, (toks, tile), 0)
    ).astype(jnp.bfloat16)
    mine = (
        lax.broadcasted_iota(jnp.int32, (heads, tile), 1) % heads
        == lax.broadcasted_iota(jnp.int32, (heads, tile), 0)
    )
    ones = jnp.ones((8, grad_ref.shape[1]), jnp.bfloat16)
    for index in range(rows // tile):
        tok = pl.multiple_of(span * (rows // heads) + index * toks, toks)
        row = pl.multiple_of(span * rows + index * tile, tile)
        norm = norm_ref[:, pl.ds(tok, toks)] * math.log2(math.e)
        wide = sum(dot(part, spread, NN) for part in three_terms(norm))
        out[0:1, pl.ds(row, tile)] = jnp.sum(jnp.where(mine, wide, 0.0), axis=0, keepdims=True)
        prod = grad_ref[pl.ds(row, tile), :].astype(jnp.float32) * outputs_ref[
            pl.ds(row, tile), :
        ].astype(jnp.float32)
        high = prod.astype(jnp.bfloat16)
        low = (prod - high.astype(jnp.float32)).astype(jnp.bfloat16)
        out[1:2, pl.ds(row, tile)] = (dot(ones, high, NT) + dot(ones, low, NT))[0:1]


def opened(group, row, key, length):
    query_ref, grad_ref, key_ref, value_ref, _, tile = group
    k = key_ref[pl.ds(key, length), :]
    v = value_ref[pl.ds(key, length), :]
    scores = dot(k, query_ref[pl.ds(row, tile), :], NT)
    return scores, dot(v, grad_ref[pl.ds(row, tile), :], NT)


def closed(group, scale, row, triangle, scores, dprob):
    terms_ref, tile = group[4:]
    norm = terms_ref[0:1, pl.ds(row, tile)]
    delta = terms_ref[1:2, pl.ds(row, tile)]
    prob = jnp.exp2(scores * (scale * math.log2(math.e)) - norm)
    if triangle is not None:
        edge = prob.shape[0] - triangle.shape[0]
        last = jnp.where(triangle, prob[edge:], 0.0)
        prob = last if edge == 0 else jnp.concatenate([prob[:edge], last], axis=0)
    return prob.astype(jnp.bfloat16), (prob * (dprob - delta)).astype(jnp.bfloat16)


def triangle_grads(group, accs, scale, row, key, half, triangle, kept_ref):
    query_ref, grad_ref, tile = group[0], group[1], group[-1]
    key_acc, value_acc = accs
    per = triangle.shape[0]
    tiles = [(pl.multiple_of(row + p * tile, tile), (p + 1) * per) for p in range(half // per)]
    ahead = opened(group, tiles[0][0], key, tiles[0][1])
    for index, (row, length) in enumerate(tiles):
        now = ahead
        if index + 1 < len(tiles):
            ahead = opened(group, tiles[index + 1][0], key, tiles[index + 1][1])
        prob, dscore = closed(group, scale, row, triangle, *now)
        kept_ref[pl.ds(key, length), pl.ds(row, tile)] = dscore
        value_acc[pl.ds(key, length), :] += dot(prob, grad_ref[pl.ds(row, tile), :], NN)
        key_acc[pl.ds(key, length), :] += dot(dscore, query_ref[pl.ds(row, tile), :], NN)


def block_grads(group, accs, scale, rows, blocks):
    query_ref, grad_ref, tile = group[0], group[1], 256
    group = group[:-1] + (tile,)
    key_acc, value_acc = accs
    count, depth = rows // tile, 256
    tiles = [
        (block, p, low)
        for block in blocks
        for p in range(count)
        for low in range(0, block[2], depth)
    ]

    def start(block, p, low):
        row, key = block[:2]
        row, key = pl.multiple_of(row + p * tile, tile), pl.multiple_of(key + low, depth)
        return opened(group, row, key, depth)

    ahead = start(*tiles[0])
    for index, (block, p, low) in enumerate(tiles):
        now = ahead
        if index + 1 < len(tiles):
            ahead = start(*tiles[index + 1])
        row, key, length, kept, probs = block
        prob, dscore = closed(group, scale, pl.multiple_of(row + p * tile, tile), None, *now)
        probs[low : low + depth, p * tile : (p + 1) * tile] = prob
        kept[low : low + depth, p * tile : (p + 1) * tile] = dscore
        if p == count - 1 and low == length - depth:
            value_acc[pl.ds(key, length), :] += dot(probs[...], grad_ref[pl.ds(row, rows), :], NN)
            key_acc[pl.ds(key, length), :] += dot(kept[...], query_ref[pl.ds(row, rows), :], NN)


def span_pair(span_ids, holder):
    return span_ids[2 * holder], span_ids[2 * holder + 1]


def far_halves(span_ids, step):
    me, holders = lax.axis_index("ctx"), lax.axis_size("ctx")
    mine = span_pair(span_ids, me)
    theirs = span_pair(span_ids, lax.rem(me + holders - step, holders))
    high_only = jnp.minimum(*mine) < jnp.minimum(*theirs)
    our_high = jnp.where(mine[0] > mine[1], 0, 1)
    their_low = jnp.where(theirs[0] > theirs[1], 1, 0)
    return lambda item: (
        jnp.where(high_only, our_high, item),
        jnp.where(high_only, item, their_low),
    )


def put_shares(outs, key_acc, value_acc, scale, first=0, parts=None, more=None):
    parts = parts or len(outs) + first
    share = key_acc.shape[0] // parts
    x = lax.axis_index("head")
    for away, out in enumerate(outs, first):
        start = pl.multiple_of(lax.rem(x + away, parts) * share, share)
        for low, part in (
            (0, key_acc[pl.ds(start, share), :] * scale),
            (share, value_acc[pl.ds(start, share), :]),
        ):
            if more is not None:
                part = part + more(away, low, share)
            out[low : low + share, :] = part.astype(out.dtype)


def own_work(group, accs, scale, span_ids, kept_ref, probs_ref, heads):
    tile = group[-1]
    toks, rows = kept_ref.shape
    half, span_rows, per = toks // 2, rows // 2, tile // heads
    first, second = span_pair(span_ids, lax.axis_index("ctx"))
    low = jnp.where(first > second, 1, 0)
    triangle = lax.broadcasted_iota(jnp.int32, (per, tile), 0) <= (
        lax.broadcasted_iota(jnp.int32, (per, tile), 1) // heads
    )

    def corner(which):
        key = pl.multiple_of(which * half, half)
        row = pl.multiple_of(which * span_rows, span_rows)
        triangle_grads(group, accs, scale, row, key, half, triangle, kept_ref)

    def square():
        key = pl.multiple_of(low * half, half)
        row = pl.multiple_of((1 - low) * span_rows, span_rows)
        kept = kept_ref.at[pl.ds(key, half), pl.ds(row, span_rows)]
        block_grads(group, accs, scale, span_rows, [(row, key, half, kept, probs_ref)])

    return low, corner, square


def first_kernel(heads, tile, scale, parts, *refs):
    inputs, refs = refs[:7], refs[7:]
    terms_ref, both_ref, kept_ref, key_acc, value_acc = refs[:5]
    held, (probs_ref, span_ids, sems) = refs[5:-3], refs[-3:]
    grad_ref, outputs_ref, query_ref, norm_ref = held
    toks = both_ref.shape[0] // 2
    key_ref, value_ref = both_ref.at[pl.ds(0, toks)], both_ref.at[pl.ds(toks, toks)]
    rows = toks * heads // 2
    whole = [
        pltpu.make_async_copy(a, b, sems.at[i, 2])
        for i, (a, b) in enumerate(zip(inputs[3:], (norm_ref, key_ref, value_ref, span_ids)))
    ]

    def halves(slot, index):
        part = pl.ds(pl.multiple_of(index * rows, rows), rows)
        return [
            pltpu.make_async_copy(inputs[i].at[part], held[i].at[part], sems.at[i, slot])
            for i in range(3)
        ]

    x = lax.axis_index("head")
    order = (1 - x, x) if parts == 2 else (0, 1)
    for copy in whole[:1] + halves(0, order[0]) + whole[1:] + halves(1, order[1]):
        copy.start()
    key_acc[...] = jnp.zeros_like(key_acc)
    value_acc[...] = jnp.zeros_like(value_acc)
    whole[0].wait()

    def arrive(slot):
        for copy in halves(slot, order[slot]):
            copy.wait()
        row_terms(heads, tile, order[slot], (grad_ref, outputs_ref, norm_ref), terms_ref)

    group = (query_ref, grad_ref, key_ref, value_ref, terms_ref, tile)
    accs = (key_acc, value_acc)
    arrive(0)
    for copy in whole[1:]:
        copy.wait()
    low, corner, square = own_work(group, accs, scale, span_ids, kept_ref, probs_ref, heads)
    corner(order[0])
    arrive(1)
    if parts == 2:
        pl.when(low == order[0])(square)
        pl.when(low == order[1])(lambda: corner(order[1]))
    else:
        corner(order[1])
        square()


def last_kernel(heads, tile, scale, parts, span_ids, *refs):
    query_ref, grad_ref, terms_ref, both_ref = refs[:4]
    kept_ref, key_acc, value_acc, total_ref, probs_ref = refs[8:]
    if parts == 2:
        toks = both_ref.shape[0] // 2
        key_ref, value_ref = both_ref.at[pl.ds(0, toks)], both_ref.at[pl.ds(toks, toks)]
        group = (query_ref, grad_ref, key_ref, value_ref, terms_ref, tile)
        accs = (key_acc, value_acc)
        x = lax.axis_index("head")
        low, corner, square = own_work(group, accs, scale, span_ids, kept_ref, probs_ref, heads)
        pl.when(low == x)(square)
        pl.when(low != x)(lambda: corner(x))
    put_shares([total_ref], key_acc, value_acc, scale, 0, parts)


def near_kernel(heads, tile, scale, parts, span_ids, *refs):
    query_ref, grad_ref, terms_ref, key_ref, value_ref, own_keys, own_values, _, kept_ref = refs[:9]
    outs, own_outs, (key_acc, value_acc, probs_ref) = refs[9 : 9 + parts], refs[9 + parts : -3], refs[-3:]
    put_shares(own_outs, own_keys, own_values, scale, 1)
    group = (query_ref, grad_ref, key_ref, value_ref, terms_ref, tile)
    far_work(group, (key_acc, value_acc), scale, span_ids, kept_ref, probs_ref, heads, 1)
    put_shares(outs, key_acc, value_acc, scale)


def pack_kernel(key_ref, value_ref, out_ref):
    toks = key_ref.shape[0]
    out_ref[0:toks, :] = key_ref[...]
    out_ref[toks : 2 * toks, :] = value_ref[...]


def far_kernel(heads, tile, scale, span_ids, *refs):
    query_ref, grad_ref, terms_ref, over_ref, beside_ref, _ = refs[:6]
    parts = (len(refs) - 11) // 2
    swapped, both_ref, kept_ref = refs[6 : 6 + parts], refs[6 + parts], refs[7 + parts]
    outs, (key_acc, value_acc, probs_ref) = refs[8 + parts : -3], refs[-3:]
    toks = both_ref.shape[0] // 2
    is_odd = lax.rem(lax.axis_index("ctx"), 2) == 1

    @pl.when(is_odd)
    def _():
        both_ref[...] = beside_ref[...]

    @pl.when(jnp.logical_not(is_odd))
    def _():
        both_ref[...] = over_ref[...]

    key_ref, value_ref = both_ref.at[pl.ds(0, toks)], both_ref.at[pl.ds(toks, toks)]
    group = (query_ref, grad_ref, key_ref, value_ref, terms_ref, tile)
    far_work(group, (key_acc, value_acc), scale, span_ids, kept_ref, probs_ref, heads, 2)

    def more(away, low, share):
        return jnp.where(is_odd, swapped[away][low : low + share, :].astype(jnp.float32), 0.0)

    put_shares(outs, key_acc, value_acc, scale, more=more)


def far_work(group, accs, scale, span_ids, kept_ref, probs_ref, heads, step):
    key_acc, value_acc = accs
    key_acc[...] = jnp.zeros_like(key_acc)
    value_acc[...] = jnp.zeros_like(value_acc)
    half = group[2].shape[0] // 2
    rows = half * heads
    halves = far_halves(span_ids, step)
    blocks = []
    for item in range(2):
        row_half, key_half = halves(item)
        row = pl.multiple_of(row_half * rows, rows)
        key = pl.multiple_of(key_half * half, half)
        blocks.append((row, key, half, kept_ref.at[item], probs_ref.at[item]))
    block_grads(group, accs, scale, rows, blocks)


def join_kernel(*refs):
    count = len(refs) // 3
    even = lax.rem(lax.axis_index("ctx"), 2) == 0
    for swapped, this, out in zip(refs, refs[count:], refs[2 * count :]):
        more = jnp.where(even, swapped[...].astype(jnp.float32), 0.0)
        out[...] = (this[...].astype(jnp.float32) + more).astype(out.dtype)


def total_kernel(total_ref, swapped_ref, *refs):
    ins, (key_out, value_out) = refs[:-2], refs[-2:]
    share = key_out.shape[0]
    even = lax.rem(lax.axis_index("ctx"), 2) == 0
    for low, out in ((0, key_out), (share, value_out)):
        part = total_ref[low : low + share, :]
        part = part + jnp.where(even, swapped_ref[low : low + share, :].astype(jnp.float32), 0.0)
        for ref in ins:
            part = part + ref[low : low + share, :].astype(jnp.float32)
        out[...] = part.astype(out.dtype)


def query_kernel(heads, tile, scale, span_ids, both_ref, own_ref, *refs):
    (key_1, both_2), kept_refs, (out_ref, acc, turned) = refs[:2], refs[2:-3], refs[-3:]
    toks = both_ref.shape[0] // 2
    half = toks // 2
    rows = half * heads
    per = tile // heads
    for index, key_ref in enumerate((both_ref, key_1, both_2)):
        for low in range(0, toks, half):
            turned[index, :, low : low + half] = key_ref[low : low + half, :].T

    @pl.loop(0, 2)
    def _(index):
        key = pl.multiple_of(index * half, half)
        for p in range(half // per):
            row = pl.multiple_of(index * rows + p * tile, tile)
            length = (p + 1) * per
            acc[:, pl.ds(row, tile)] = dot(
                turned[0, :, pl.ds(key, length)], own_ref[pl.ds(key, length), pl.ds(row, tile)], NN
            )

    first, second = span_pair(span_ids, lax.axis_index("ctx"))
    low = jnp.where(first > second, 1, 0)
    key = pl.multiple_of(low * half, half)
    for p in range(rows // tile):
        row = pl.multiple_of((1 - low) * rows + p * tile, tile)
        acc[:, pl.ds(row, tile)] += dot(
            turned[0, :, pl.ds(key, half)], own_ref[pl.ds(key, half), pl.ds(row, tile)], NN
        )
    for step, kept_ref in enumerate(kept_refs, 1):
        halves = far_halves(span_ids, step)

        @pl.loop(0, 2)
        def _(item):
            row_half, key_half = halves(item)
            key = pl.multiple_of(key_half * half, half)
            for p in range(rows // tile):
                row = pl.multiple_of(row_half * rows + p * tile, tile)
                acc[:, pl.ds(row, tile)] += dot(
                    turned[step, :, pl.ds(key, half)],
                    kept_ref[item, :, p * tile : (p + 1) * tile],
                    NN,
                )

    for row in range(0, 2 * rows, tile):
        out_ref[row : row + tile, :] = (acc[:, row : row + tile] * scale).astype(out_ref.dtype).T


VMEM = pl.BlockSpec(memory_space=pltpu.VMEM)
SMEM = pl.BlockSpec(memory_space=pltpu.SMEM)
HBM = pl.BlockSpec(memory_space=pltpu.HBM)
ANY = pl.BlockSpec(memory_space=pl.ANY)
MIB = 1024 * 1024


def call(kernel, ins, where, outs, scratch, blocks, limit, name, aliases=None):
    flops = blocks * 40 * 512 * 512 * 128
    return pl.pallas_call(
        kernel,
        out_shape=outs,
        in_specs=where,
        out_specs=[VMEM] * len(outs),
        scratch_shapes=scratch,
        input_output_aliases=aliases or {},
        compiler_params=pltpu.CompilerParams(vmem_limit_bytes=limit * MIB),
        name=name,
        cost_estimate=pl.CostEstimate(flops=int(flops), bytes_accessed=int(blocks * (1 << 20)), transcendentals=0),
    )(*ins)


def moved(block, back, away):
    holders, parts = lax.axis_size("ctx"), lax.axis_size("head")
    route = [
        (h * parts + x, ((h - back[h % 2]) % holders) * parts + (x + away) % parts)
        for h in range(holders)
        for x in range(parts)
    ]
    return lax.ppermute(block, ("ctx", "head"), route)


def local(queries, keys, values, outputs, out_grad, log_norm, span_ids):
    toks, heads, dim = queries.shape
    rows = toks * heads
    scale = dim ** (-0.5)
    parts = lax.axis_size("head")
    tile = 512
    q = queries.reshape(rows, dim)
    g = out_grad.reshape(rows, dim)
    o = outputs.reshape(rows, dim)
    share = 2 * toks // parts
    f32, bf16 = jnp.float32, jnp.bfloat16
    shape = jax.ShapeDtypeStruct
    grads = [shape((share, dim), bf16)] * parts
    accs = [pltpu.VMEM((toks, dim), f32)] * 2
    probs = pltpu.VMEM((toks // 2, rows // 2), bf16)

    key_1, value_1 = moved(keys, (-1, -1), 0), moved(values, (-1, -1), 0)
    inputs = tuple(
        pltpu.with_memory_space_constraint(a, pltpu.HBM)
        for a in (g, o, q, log_norm, keys, values, span_ids)
    )
    sums = [shape((toks, rows), bf16), shape((toks, dim), f32), shape((toks, dim), f32)]
    terms, both, kept, key_sum, value_sum = call(
        functools.partial(first_kernel, heads, tile, scale, parts),
        inputs,
        [HBM] * len(inputs),
        [shape((8, rows), f32), shape((2 * toks, dim), bf16)] + sums,
        [pltpu.VMEM(a.shape, a.dtype) for a in inputs[:4]]
        + [probs, pltpu.SMEM(span_ids.shape, span_ids.dtype), pltpu.SemaphoreType.DMA((4, 3))],
        1.625 * heads,
        20,
        "first",
    )
    (both_1,) = call(
        pack_kernel, (key_1, value_1), [VMEM] * 2, [shape((2 * toks, dim), bf16)], [], 0.01, 4, "pack"
    )
    over, beside = moved(both, (-2, 0), 0), moved(both_1, (-1, 1), 0)

    block = (toks // 2, rows // 2)
    kept_1, *sent = call(
        functools.partial(near_kernel, heads, tile, scale, parts),
        (span_ids, q, g, terms, key_1, value_1, key_sum, value_sum, both_1),
        [SMEM] + [VMEM] * 7 + [ANY],
        [shape((2,) + block, bf16)] + grads + grads[1:],
        accs + [pltpu.VMEM((2,) + block, bf16)],
        2 * heads,
        18,
        "near",
    )
    swapped = [moved(part, (-1, 1), 0) for part in sent[:parts]]
    sent = call(
        join_kernel,
        (*swapped[1:], *sent[parts:]),
        [VMEM] * (2 * parts - 2),
        grads[1:],
        [],
        0.01,
        4,
        "join",
    )
    whole = [moved(part, (0, 0), away) for away, part in enumerate(sent, 1)]
    both_2, kept_2, *sent = call(
        functools.partial(far_kernel, heads, tile, scale),
        (span_ids, q, g, terms, over, beside, sent[0], *swapped),
        [SMEM] + [VMEM] * 5 + [ANY] + [VMEM] * parts,
        [shape((2 * toks, dim), bf16), shape((2,) + block, bf16)] + grads,
        accs + [pltpu.VMEM((2,) + block, bf16)],
        2 * heads,
        18,
        "far",
    )
    landed = whole + [moved(part, (2, 2), away) for away, part in enumerate(sent)]
    kept, _, _, total = call(
        functools.partial(last_kernel, heads, tile, scale, parts),
        (span_ids, q, g, terms, both, kept, key_sum, value_sum, sent[0]),
        [SMEM] + [VMEM] * 7 + [ANY],
        sums + [shape((share, dim), f32)],
        [probs],
        1.625 * heads,
        20,
        "last",
        {5: 0, 6: 1, 7: 2},
    )
    (query_grad,) = call(
        functools.partial(query_kernel, heads, tile, scale),
        (span_ids, both, kept, key_1, both_2, kept_1, kept_2),
        [SMEM] + [VMEM] * 6,
        [shape((rows, dim), bf16)],
        [pltpu.VMEM((dim, rows), f32), pltpu.VMEM((STEPS, dim, toks), bf16)],
        0.02 * heads,
        28,
        "queries",
    )
    key_grad, value_grad = call(
        total_kernel,
        (total, swapped[0], *landed),
        [VMEM] * (2 + len(landed)),
        [shape((share // 2, dim), bf16)] * 2,
        [],
        0.01,
        8,
        "total",
    )
    return query_grad.reshape(toks, heads, dim), key_grad, value_grad


def solution(mesh):
    in_specs = (
        P("ctx", "head", None),
        P("ctx", None),
        P("ctx", None),
        P("ctx", "head", None),
        P("ctx", "head", None),
        P("head", "ctx"),
        P(),
    )
    out_specs = (P("ctx", "head", None), P(("ctx", "head"), None), P(("ctx", "head"), None))
    return jax.shard_map(local, mesh=mesh, in_specs=in_specs, out_specs=out_specs, check_vma=False)
```
